32 devices in a mesh: dp: 16 (over z, y, x), mp: 2 (over core).
Axes of the slice: x: 2, y: 2, z: 4, core: 2. Of those that a mesh axis runs over, the one named last changes fastest.
Arguments:
- tokens: bfloat16 [6144, 1024], P('dp'), may hold values from -6 to 6
- cotangent: bfloat16 [6144, 1024], P('dp'), may hold values from -6 to 6
- qkv_weight: bfloat16 [3, 1024, 1024], P(None, None, 'mp'), may hold values from -0.1875 to 0.1875
- out_weight: bfloat16 [1024, 1024], P('mp'), may hold values from -4 to 4
- up_weight: bfloat16 [1024, 4096], P(None, 'mp'), may hold values from -0.1875 to 0.1875
- down_weight: bfloat16 [4096, 1024], P('mp'), may hold values from -0.09375 to 0.09375
- norm_gain: float32 [2, 8, 1024], replicated, may hold values from 0.5 to 1.5
- norm_shift: float32 [2, 8, 1024], replicated, may hold values from -1.25 to 1.25
- lengths: int32 [16], P('dp'), may hold values from 192 to 384, as said below
- prompt_src: int32 [16], P('dp'), may hold values from 0 to 15, as said below
- prompt_len: int32 [16], P('dp'), may hold values from 48 to 96, as said below
- codebook_section: int32 [16], P('dp'), may hold values from 1 to 7
- adam_step: int32 [1], replicated, may hold values from 1 to 4
- master: float32 [2, 6307840], P('mp', 'dp')
- first_moment: float32 [2, 6307840], P('mp', 'dp')
- second_moment: float32 [2, 6307840], P('mp', 'dp'), as said below
- ema_weight: float32 [2, 6307840], P('mp', 'dp')
Outputs:
- block_out: bfloat16 [6144, 1024], P('dp')
- input_grad: bfloat16 [6144, 1024], P('dp')
- grad_norm: float32 [1], replicated
- new_first: float32 [2, 6307840], P('mp', 'dp')
- new_second: float32 [2, 6307840], P('mp', 'dp')
- new_master: float32 [2, 6307840], P('mp', 'dp')
- master_copy: bfloat16 [2, 6307840], P('mp', 'dp')
- new_ema: float32 [2, 6307840], P('mp', 'dp')
The draws below stay inside these ranges and needn't reach their ends.
Inputs may be any that keep to these rules, and one draw needn't show every extreme that they name: `lengths`: valid frames at the start of each utterance's 384 slots; some utterance fills them all. `prompt_src`: another utterance of the same speaker group; speaker groups are aligned runs of four dp indices or halves of such runs, and the first run is one group. `prompt_len`: frames taken from the start of the source utterance; some utterance takes 96. `second_moment`: positive.
All inputs are finite; a program needn't handle non-finite values.
Results may differ from the reference program's by a relative error of at most 0.015.
Values may be sent and summed in bfloat16 or wider, within the bound.
No kernel may reach another device: no remote copies, remote signals or barrier semaphores. Data moves between devices by JAX's collectives and lax.ppermute only.
A program may use at most 192 MiB of HBM per device.

```python
import math
import jax
import jax.numpy as jnp
from jax import lax

D = 1024
HDIM = 64
FF = 4096
SECTIONS = 8
TOK_DEV = 384
QBLOCK = 384
PMAX = 96
OUT_FAN = 2
TOKENS = 6144
N_DP = 16
N_MP = 2


def segment_sizes():
    half_model = D // N_MP
    half_hidden = FF // N_MP
    table_size = 2 * SECTIONS * half_model // N_DP
    return [3 * D * half_model // N_DP, half_model * D // N_DP, D * half_hidden // N_DP, half_hidden * D // N_DP, table_size, table_size]


def spread_by_kind(kind_values):
    pieces = [jnp.full((entry_count,), kind_value, jnp.float32) for entry_count, kind_value in zip(segment_sizes(), kind_values)]
    single_row = jnp.concatenate(pieces)
    return jnp.tile(single_row, (N_MP, N_DP))


def gradient_sizes():
    out_scale = 1.4 * (TOK_DEV // 2) ** (-0.5)
    table_scale = 1.5 * (SECTIONS - 1) ** (-0.5)
    kinds = [1.4, out_scale, 0.3, 0.6, table_scale, table_scale]
    overall = 3 * D * D * 1.96 + D * D * out_scale * out_scale + D * FF * 0.45 + 4 * SECTIONS * D * table_scale * table_scale
    return [entry / math.sqrt(overall) for entry in kinds]


def weight_law(key):
    spreads = spread_by_kind([D ** (-0.5), OUT_FAN ** (-0.5), D ** (-0.5), FF ** (-0.5), 0.1, 0.2])
    centres = spread_by_kind([0.0, 0.0, 0.0, 0.0, 1.0, 0.0])
    return centres + spreads * jnp.clip(jax.random.normal(key, spreads.shape, jnp.float32), -4.0, 4.0)


def draw_master(key, part):
    return weight_law(jax.random.fold_in(key, 3))


def draw_ema_weight(key, part):
    return weight_law(jax.random.fold_in(key, 5))


def draw_first_moment(key, part):
    scales = spread_by_kind(gradient_sizes())
    return scales * jax.random.normal(jax.random.fold_in(key, 11), scales.shape, jnp.float32)


def draw_second_moment(key, part):
    scales = spread_by_kind([entry * entry for entry in gradient_sizes()])
    factor = jnp.exp(jax.random.uniform(jax.random.fold_in(key, 13), scales.shape, jnp.float32, 0.0, math.log(4.0)))
    return scales * factor


def draw_lengths(key, part):
    inner = jax.random.fold_in(key, 21)
    drawn = jax.random.randint(inner, (N_DP,), TOK_DEV // 2, TOK_DEV + 1)
    chosen = jax.random.randint(jax.random.fold_in(inner, 1), (), 0, N_DP)
    return jnp.where(jnp.arange(N_DP) == chosen, TOK_DEV, drawn).astype(jnp.int32)


def group_plan(key):
    inner = jax.random.fold_in(key, 31)
    block_whole = jax.random.randint(jax.random.fold_in(inner, 1), (N_DP // 4,), 0, 2)
    block_whole = block_whole.at[0].set(1)
    device_ids = jnp.arange(N_DP)
    within = device_ids % 4
    start_of = device_ids - within
    rotate = jax.random.randint(jax.random.fold_in(inner, 2), (N_DP,), 1, 4)
    rotate = rotate.at[0].set(3)
    whole_src = start_of + (within + rotate) % 4
    pair_src = device_ids + 1 - 2 * (within % 2)
    source = jnp.where(jnp.repeat(block_whole, 4) == 1, whole_src, pair_src)
    frames = jax.random.randint(jax.random.fold_in(inner, 3), (N_DP,), PMAX // 2, PMAX + 1)
    chosen = jax.random.randint(jax.random.fold_in(inner, 4), (), 0, N_DP)
    frames = jnp.where(device_ids == chosen, PMAX, frames)
    return (source.astype(jnp.int32), frames.astype(jnp.int32))


def draw_prompt_src(key, part):
    return group_plan(key)[0]


def draw_prompt_len(key, part):
    return group_plan(key)[1]


def set_ends(array, stream_key, low, largest):
    extent = array.shape
    index_at = [jax.random.randint(jax.random.fold_in(stream_key, axis), (), 0, extent[axis]) for axis in range(len(extent))]
    array = array.at[tuple(index_at)].set(low)
    longest = extent.index(max(extent))
    index_at[longest] = (index_at[longest] + 1) % extent[longest]
    return array.at[tuple(index_at)].set(largest)


def shard_levels(rng, shape, split, least, high):
    def one(axis_at, parts):
        draws = jax.random.uniform(jax.random.fold_in(jax.random.fold_in(rng, 6), axis_at), (parts,), jnp.float32, least / len(split), high / len(split))
        return jnp.repeat(jnp.exp(draws), shape[axis_at] // parts).reshape((-1,) + (1,) * (len(shape) - axis_at - 1))

    loudness = one(*split[0])
    for cut in split[1:]:
        loudness = loudness * one(*cut)
    return loudness


def scatter_about(key, shape, width, bound, cuts=(), held_as=jnp.bfloat16):
    entries = jax.random.normal(key, shape, jnp.float32) * width
    if len(cuts) > 0:
        entries = shard_levels(key, shape, cuts, -0.22, 0.18) * entries
    return jnp.clip(entries, min=-bound, max=bound).astype(held_as)


def setup_inputs(seed: int = 0) -> dict:
    arg_keys = jax.random.split(jax.random.key(seed), 18)
    return {
        "tokens": scatter_about(arg_keys[0], (TOKENS, D), 1.0, 6.0, ((0, 16),)),
        "cotangent": scatter_about(arg_keys[1], (TOKENS, D), 1.0, 6.0, ((0, 16),)),
        "qkv_weight": scatter_about(arg_keys[2], (3, D, D), D ** -0.5, 0.1875, ((2, 2),)),
        "out_weight": scatter_about(arg_keys[3], (D, D), OUT_FAN ** -0.5, 4.0, ((0, 2),)),
        "up_weight": scatter_about(arg_keys[4], (D, FF), D ** -0.5, 0.1875, ((1, 2),)),
        "down_weight": scatter_about(arg_keys[5], (FF, D), FF ** -0.5, 0.09375, ((0, 2),)),
        "norm_gain": jnp.clip(1.0 + 0.1 * jax.random.normal(arg_keys[6], (2, SECTIONS, D), jnp.float32), 0.5, 1.5),
        "norm_shift": scatter_about(arg_keys[7], (2, SECTIONS, D), 0.2, 1.25, (), jnp.float32),
        "lengths": draw_lengths(jax.random.fold_in(arg_keys[17], 71), 0),
        "prompt_src": draw_prompt_src(jax.random.fold_in(arg_keys[17], 71), 0),
        "prompt_len": draw_prompt_len(jax.random.fold_in(arg_keys[17], 71), 0),
        "codebook_section": set_ends(jax.random.randint(arg_keys[11], (N_DP,), 1, SECTIONS), jax.random.fold_in(arg_keys[11], 1), 1, SECTIONS - 1).astype(jnp.int32),
        "adam_step": jax.random.randint(arg_keys[12], (1,), 1, 5).astype(jnp.int32),
        "master": draw_master(jax.random.fold_in(arg_keys[17], 71), 0),
        "first_moment": draw_first_moment(jax.random.fold_in(arg_keys[17], 71), 0),
        "second_moment": draw_second_moment(jax.random.fold_in(arg_keys[17], 71), 0),
        "ema_weight": draw_ema_weight(jax.random.fold_in(arg_keys[17], 71), 0),
    }


CLIP_NORM = 1.0
BETA_ONE = 0.5
BETA_TWO = 0.5
WEIGHT_DECAY = 0.1
EMA_DECAY = 0.75

@jax.custom_vjp
def low(v):
    return lax.optimization_barrier(v.astype(jnp.bfloat16)).astype(jnp.float32)

@jax.custom_vjp
def low_back(v):
    return v

def low_keep(v):
    return (low(v), None)

def low_pass(kept, grad):
    return (grad,)

def back_keep(v):
    return (v, None)

def back_low(kept, grad):
    return (low(grad),)
low.defvjp(low_keep, low_pass)
low_back.defvjp(back_keep, back_low)

def normalize(values, gain_row, shift_row):
    centred = values - lax.optimization_barrier(jnp.mean(values, axis=-1, keepdims=True))
    variance = lax.optimization_barrier(jnp.mean(centred * centred, axis=-1, keepdims=True))
    return gain_row * (centred * lax.rsqrt(variance + 1e-05)) + shift_row

def attention(queries, key_all, value_all, key_ok):
    head_count = queries.shape[1] // HDIM
    query_blocks = queries.reshape(TOK_DEV // QBLOCK, QBLOCK, head_count, HDIM)
    key_heads = key_all.reshape(-1, head_count, HDIM)
    value_heads = value_all.reshape(-1, head_count, HDIM)

    def one_block(query_block):
        scores = jnp.einsum('qhe,khe->hqk', query_block, key_heads, precision=lax.Precision.HIGHEST) * HDIM ** (-0.5)
        scores = low_back(scores)
        scores = jnp.where(key_ok[None, None, :], scores, -1e+30)
        row_max = lax.optimization_barrier(jnp.max(scores, axis=2, keepdims=True))
        exponent = jnp.exp(scores - row_max)
        probability = low(exponent / lax.optimization_barrier(jnp.sum(exponent, axis=2, keepdims=True)))
        return jnp.einsum('hqk,khe->qhe', probability, value_heads, precision=lax.Precision.HIGHEST)
    mixed = lax.map(jax.checkpoint(one_block), query_blocks)
    return mixed.reshape(TOK_DEV, head_count * HDIM)

def to_flat(arrays):
    half_model = D // N_MP
    half_hidden = FF // N_MP
    shards = []
    for mp_part in range(N_MP):
        model_span = slice(mp_part * half_model, (mp_part + 1) * half_model)
        hidden_span = slice(mp_part * half_hidden, (mp_part + 1) * half_hidden)
        pieces = [arrays[0][:, :, model_span], arrays[1][model_span], arrays[2][:, hidden_span], arrays[3][hidden_span], arrays[4][:, :, model_span], arrays[5][:, :, model_span]]
        shards.append(jnp.concatenate([piece_item.reshape(N_DP, -1) for piece_item in pieces], axis=1).reshape(-1))
    return jnp.stack(shards)

def reference(tokens, cotangent, qkv_weight, out_weight, up_weight, down_weight, norm_gain, norm_shift, lengths, prompt_src, prompt_len, codebook_section, adam_step, master, first_moment, second_moment, ema_weight):
    highest = lax.Precision.HIGHEST
    frame_ids = jnp.arange(TOK_DEV).astype(jnp.int32)
    inputs = tokens.astype(jnp.float32).reshape(N_DP, TOK_DEV, D)
    row_ok = (frame_ids[None, :] < lengths[:, None]).astype(jnp.float32)[:, :, None]
    grad_out = cotangent.astype(jnp.float32).reshape(N_DP, TOK_DEV, D) * row_ok
    selector = (codebook_section[:, None] == jnp.arange(SECTIONS).astype(jnp.int32)[None, :]).astype(jnp.float32)
    positions = jnp.arange(TOK_DEV + PMAX).astype(jnp.int32)

    def forward(frames_all, qkv_full, out_full, up_full, down_full, gain_full, shift_full):
        table = jnp.stack([gain_full[0], shift_full[0], gain_full[1], shift_full[1]])
        section_rows = jnp.einsum('ns,ksd->nkd', selector, table, precision=highest)
        prompt_in = low(normalize(frames_all[:, :PMAX], section_rows[:, 0:1], section_rows[:, 1:2]))
        prompt_all = low_back(low(jnp.einsum('npd,cde->ncpe', prompt_in, qkv_full[1:], precision=highest)))
        chosen = low_back(jnp.take(prompt_all, prompt_src, axis=0))

        def utterance(scan_carry, scan_item):
            frames_in, section_row, prompt_pair, length, prompt_count = scan_item
            normed = low(normalize(frames_in, section_row[0], section_row[1]))
            projected = low_back(low(jnp.einsum('td,cde->cte', normed, qkv_full, precision=highest)))
            key_all = jnp.concatenate([projected[1], prompt_pair[0]], axis=0)
            value_all = jnp.concatenate([projected[2], prompt_pair[1]], axis=0)
            key_ok = jnp.where(positions < TOK_DEV, positions < length, positions - TOK_DEV < prompt_count)
            attended = low_back(low(attention(projected[0], key_all, value_all, key_ok)))
            hidden = frames_in + low_back(jnp.dot(attended, out_full, precision=highest))
            normed_two = low(normalize(hidden, section_row[2], section_row[3]))
            pre_act = low_back(jnp.dot(normed_two, up_full, precision=highest))
            activated = low(jax.nn.gelu(pre_act, approximate=False))
            return (scan_carry, hidden + low_back(jnp.dot(activated, down_full, precision=highest)))
        final_carry, outputs = lax.scan(jax.checkpoint(utterance), jnp.zeros((), jnp.float32), (frames_all, section_rows, chosen, lengths, prompt_len))
        return outputs
    block_all, pull_back = jax.vjp(forward, inputs, qkv_weight.astype(jnp.float32), out_weight.astype(jnp.float32), up_weight.astype(jnp.float32), down_weight.astype(jnp.float32), norm_gain, norm_shift)
    grads = pull_back(grad_out)
    weight_grads = list(grads[1:])
    square_sum = jnp.zeros((), jnp.float32)
    for weight_item in weight_grads:
        square_sum = square_sum + jnp.sum(weight_item * weight_item)
    grad_norm = jnp.sqrt(square_sum)
    rates = [D ** (-0.5), OUT_FAN ** (-0.5), D ** (-0.5), FF ** (-0.5), 0.2, 0.2]
    rate_flat = to_flat([jnp.full(weight_item.shape, rate_item, jnp.float32) for weight_item, rate_item in zip(weight_grads, rates)])
    gradient = to_flat(weight_grads)
    clip_scale = jnp.minimum(1.0, CLIP_NORM / (grad_norm + 1e-06))
    clipped = clip_scale * gradient
    new_first = BETA_ONE * first_moment + (1.0 - BETA_ONE) * clipped
    new_second = BETA_TWO * second_moment + (1.0 - BETA_TWO) * clipped * clipped
    step_count = adam_step[0].astype(jnp.float32)
    first_fix = 1.0 - jnp.power(BETA_ONE, step_count)
    second_fix = 1.0 - jnp.power(BETA_TWO, step_count)
    update = new_first / first_fix / (jnp.sqrt(new_second / second_fix) + 1e-08)
    new_master = master - rate_flat * (update + WEIGHT_DECAY * master)
    new_ema = EMA_DECAY * ema_weight + (1.0 - EMA_DECAY) * new_master
    block_out = block_all.reshape(TOKENS, D).astype(jnp.bfloat16)
    input_grad = grads[0].reshape(TOKENS, D).astype(jnp.bfloat16)
    return (block_out, input_grad, grad_norm.reshape(1), new_first, new_second, new_master, new_master.astype(jnp.bfloat16), new_ema)
```

```python
import functools

import jax
import jax.numpy as jnp
from jax import lax
from jax.experimental import pallas as pl
from jax.experimental.pallas import tpu as pltpu
from jax.sharding import PartitionSpec as P

D = 1024
HDIM = 64
FF = 4096
SECTIONS = 8
TOK = 384
PMAX = 96
KEYS = TOK + PMAX
OUT_FAN = 2
HW = D // 2
HF = FF // 2
HEADS = HW // HDIM
CLIP_NORM = 1.0
BETA_ONE = 0.5
BETA_TWO = 0.5
WEIGHT_DECAY = 0.1
EMA_DECAY = 0.75

BF = jnp.bfloat16
F32 = jnp.float32
MP, PX, PY, PLANE, OUTER, LENGTH, SOURCE, PROMPT, SECTION = range(9)


def shaped(shape, dtype):
    return jax.ShapeDtypeStruct(shape, dtype)


def dot_nn(a, b):
    return lax.dot_general(a, b, (((1,), (0,)), ((), ())), preferred_element_type=F32)


def dot_nt(a, b):
    return lax.dot_general(a, b, (((1,), (1,)), ((), ())), preferred_element_type=F32)


def dot_tn(a, b):
    return lax.dot_general(a, b, (((0,), (0,)), ((), ())), preferred_element_type=F32)


def block(shape, index):
    return pl.BlockSpec(shape, index)


def whole(shape):
    rank = len(shape)
    return pl.BlockSpec(shape, lambda *_: (0,) * rank)


def call(kernel, meta, inputs, in_specs, outs, out_specs, grid=(1,), scratch=(), flops=0, name=None, vmem=30):
    moved = sum(a.size * a.dtype.itemsize for a in list(inputs) + list(outs))
    return pl.pallas_call(
        kernel,
        grid_spec=pltpu.PrefetchScalarGridSpec(
            num_scalar_prefetch=1, grid=grid, in_specs=in_specs, out_specs=out_specs, scratch_shapes=scratch
        ),
        out_shape=outs,
        compiler_params=pltpu.CompilerParams(vmem_limit_bytes=vmem << 20),
        cost_estimate=pl.CostEstimate(flops=int(flops), bytes_accessed=int(moved), transcendentals=0),
        name=name,
    )(meta, *inputs)


def simple(kernel, meta, inputs, outs, **kw):
    return call(kernel, meta, inputs, [whole(a.shape) for a in inputs], outs, [whole(o.shape) for o in outs], **kw)


def unit_rows(values):
    centred = values - jnp.mean(values, axis=-1, keepdims=True)
    scale = lax.rsqrt(jnp.mean(centred * centred, axis=-1, keepdims=True) + 1e-05)
    return centred * scale, scale


def norm_back(grad, gain_row, unit, scale):
    e = gain_row * grad
    return scale * (e - jnp.mean(e, axis=-1, keepdims=True) - unit * jnp.mean(e * unit, axis=-1, keepdims=True))


def row_of(ref, which, meta):
    return ref[which, pl.ds(meta[SECTION], 1), :]


def valid_rows(meta):
    return lax.broadcasted_iota(jnp.int32, (TOK, 1), 0) < meta[LENGTH]


def keys_ok(meta):
    at = lax.broadcasted_iota(jnp.int32, (KEYS, 1), 0)
    return at < jnp.where(at < TOK, meta[LENGTH], TOK + meta[PROMPT])


def prompt_norm_kernel(meta, tokens, gain, shift, out):
    unit, _ = unit_rows(tokens[...].astype(F32))
    out[...] = (row_of(gain, 0, meta) * unit + row_of(shift, 0, meta)).astype(BF)


def mask_kernel(meta, cotangent, low, half):
    kept = jnp.where(valid_rows(meta), cotangent[...], jnp.zeros((), BF))
    low[...] = kept

    @pl.when(meta[MP] == 0)
    def _():
        half[...] = kept[:, :HW]

    @pl.when(meta[MP] == 1)
    def _():
        half[...] = kept[:, HW:]


def qkv_kernel(meta, tokens, gain, shift, weight, normed, projected):
    @pl.when(pl.program_id(0) == 0)
    def _():
        unit, _ = unit_rows(tokens[...].astype(F32))
        normed[...] = (row_of(gain, 0, meta) * unit + row_of(shift, 0, meta)).astype(BF)

    projected[0] = dot_nn(normed[...], weight[0]).astype(BF)


def grad_act_kernel(meta, low, down, out):
    out[...] = dot_nt(low[...], down[...])


def attend_kernel(meta, projected, here, there, qkv, out_weight, normed_prompt, prompt_pair, attended_t, log_total, partial, keys, values, values_t):
    half = PMAX // 2
    normed_prompt[pl.ds(pl.multiple_of(meta[MP] * half, half), half), :] = here[...]
    normed_prompt[pl.ds(pl.multiple_of((1 - meta[MP]) * half, half), half), :] = there[...]
    rows = normed_prompt[...]
    pair_k = dot_nn(rows, qkv[1]).astype(BF)
    pair_v = dot_nn(rows, qkv[2]).astype(BF)
    prompt_pair[0] = pair_k
    prompt_pair[1] = pair_v
    keys[:TOK] = projected[1]
    keys[TOK:] = pair_k
    values[:TOK] = projected[2]
    values[TOK:] = pair_v
    values_t[...] = values[...].T
    counted = keys_ok(meta)
    lane = lax.broadcasted_iota(jnp.int32, (1, 2 * HDIM), 1)
    for head in range(HEADS):
        at = (head // 2) * 2 * HDIM
        mine = jnp.where((lane // HDIM) == head % 2, HDIM ** (-0.5), 0.0).astype(BF)
        query = projected[0, :, at : at + 2 * HDIM] * mine
        scores = jnp.where(counted, dot_nt(keys[:, at : at + 2 * HDIM], query), -1e30)
        top = jnp.max(scores, axis=0, keepdims=True)
        grown = jnp.exp(scores - top)
        total = jnp.sum(grown, axis=0, keepdims=True)
        probability = (grown * (1.0 / total)).astype(BF)
        rows_at = slice(head * HDIM, (head + 1) * HDIM)
        attended_t[rows_at, :] = dot_nn(values_t[rows_at, :], probability).astype(BF)
        log_total[head : head + 1, :] = top + jnp.log(total)
    partial[...] = dot_tn(attended_t[...], out_weight[...]).astype(BF)


TILE = 256


def ffn_kernel(split, meta, tokens, here, there, gain, shift, up, grad_act, hidden, normed, act, pre_low, partial, total):
    step = pl.program_id(0)

    @pl.when(step == 0)
    def _():
        state = tokens[...].astype(F32) + (here[...].astype(F32) + there[...].astype(F32))
        hidden[...] = state
        unit, _ = unit_rows(state)
        normed[...] = (row_of(gain, 1, meta) * unit + row_of(shift, 1, meta)).astype(BF)
        total[...] = jnp.zeros_like(total)

    pre = dot_nn(normed[...], up[...])
    cdf = 0.5 * (1.0 + lax.erf(pre * (0.5**0.5)))
    slope = cdf + pre * (jnp.exp(-0.5 * pre * pre) * (0.5 / jnp.pi) ** 0.5)
    activated = (pre * cdf).astype(BF)
    grad = (grad_act[...] * slope).astype(BF)
    pre_low[...] = grad
    if split:
        for sub in range(TILE // split):
            number = step * (TILE // split) + sub
            piece = jnp.bitwise_xor(lax.rem(number, 4), meta[PLANE])
            at = pl.multiple_of((number // 4) * split, split)
            act[piece, :, pl.ds(at, split)] = activated[:, sub * split : (sub + 1) * split]
    else:
        act[0, :, pl.ds(pl.multiple_of(step * TILE, TILE), TILE)] = activated
    total[...] += dot_nt(grad, up[...])

    @pl.when(step == pl.num_programs(0) - 1)
    def _():
        partial[...] = total[...].astype(BF)


def down_kernel(split, meta, act, down, partial, total):
    step = pl.program_id(0)

    @pl.when(step == 0)
    def _():
        total[...] = jnp.zeros_like(total)

    if split:
        for sub in range(TILE // split):
            number = step * (TILE // split) + sub
            piece = jnp.bitwise_xor(lax.rem(number, 4), meta[PLANE])
            at = pl.multiple_of((number // 4) * split, split)
            total[...] += dot_nn(act[piece, :, pl.ds(at, split)], down[sub * split : (sub + 1) * split, :])
    else:
        total[...] += dot_nn(act[0, :, pl.ds(pl.multiple_of(step * TILE, TILE), TILE)], down[...])

    @pl.when(step == pl.num_programs(0) - 1)
    def _():
        partial[...] = total[...].astype(BF)


def block_out_kernel(meta, hidden, here, there, out):
    out[...] = (hidden[...] + (here[...].astype(F32) + there[...].astype(F32))).astype(BF)


def attend_back_kernel(
    meta, here, there, hidden, gain, low, out_weight, projected, prompt_pair, log_total,
    local, sent, grad_hidden, hidden_low, tables, keys, values, keys_t, grads, query_t,
):
    back = here[...].astype(F32) + there[...].astype(F32)
    unit, scale = unit_rows(hidden[...])
    full = low[...].astype(F32) + norm_back(back, row_of(gain, 1, meta), unit, scale)
    grad_hidden[...] = full
    tables[0:1, :] = jnp.sum(back * unit, axis=0, keepdims=True)
    tables[1:2, :] = jnp.sum(back, axis=0, keepdims=True)
    rounded = full.astype(BF)
    hidden_low[...] = rounded
    grads[...] = dot_nt(rounded, out_weight[...]).astype(BF)
    keys[:TOK] = projected[1]
    keys[TOK:] = prompt_pair[0]
    values[:TOK] = projected[2]
    values[TOK:] = prompt_pair[1]
    keys_t[...] = keys[...].T
    counted = keys_ok(meta)
    lane = lax.broadcasted_iota(jnp.int32, (1, 2 * HDIM), 1)
    left = lane < HDIM
    for pair in range(HEADS // 2):
        at = pair * 2 * HDIM
        span = slice(at, at + 2 * HDIM)
        key_pair, value_pair = keys[:, span], values[:, span]
        query_pair = projected[0, :, span] * jnp.asarray(HDIM ** (-0.5), BF)
        grad_pair = grads[:, span]
        found = []
        for head in (2 * pair, 2 * pair + 1):
            mine = ((lane // HDIM) == head % 2).astype(BF)
            scores = jnp.where(counted, dot_nt(key_pair, query_pair * mine), -1e30)
            probability = jnp.exp(scores - log_total[head : head + 1, :])
            grad_prob = dot_nt(value_pair, grad_pair * mine)
            centre = jnp.sum(probability * grad_prob, axis=0, keepdims=True)
            grad_scores = (probability * (grad_prob - centre)).astype(BF)
            rows_at = slice(head * HDIM, (head + 1) * HDIM)
            query_t[rows_at, :] = dot_nn(keys_t[rows_at, :], grad_scores) * HDIM ** (-0.5)
            found.append((dot_nn(grad_scores, query_pair), dot_nn(probability.astype(BF), grad_pair)))
        local[1, :, span] = jnp.where(left, found[0][0], found[1][0]).astype(BF)
        local[2, :, span] = jnp.where(left, found[0][1], found[1][1]).astype(BF)
    local[0, :TOK, :] = query_t[...].T.astype(BF)
    local[0, TOK:, :] = jnp.zeros((PMAX, HW), BF)
    relative = jnp.bitwise_xor(lax.rem(meta[SOURCE], 4), meta[PLANE])
    for k in range(1, 4):
        keep = relative == k
        for c in range(2):
            sent[k - 1, c] = jnp.where(keep, local[1 + c, TOK:, :], jnp.zeros((), BF))


def grad_normed_kernel(meta, local, first, second, third, qkv, out, returned_low, total):
    c = pl.program_id(0)

    @pl.when(c == 0)
    def _():
        total[...] = jnp.zeros_like(total)

    total[...] += dot_nt(local[0, :TOK, :], qkv[0])

    @pl.when(c > 0)
    def _():
        at = c - 1
        returned = first[at].astype(F32) + second[at].astype(F32) + third[at].astype(F32)
        returned_low[...] = returned.astype(BF)
        total[:PMAX, :] += dot_nt(returned_low[...], qkv[0])

    @pl.when(c == 2)
    def _():
        out[...] = total[...].astype(BF)


def input_grad_kernel(meta, here, there, tokens, gain, grad_hidden, out, tables):
    back = here[...].astype(F32) + there[...].astype(F32)
    unit, scale = unit_rows(tokens[...].astype(F32))
    out[...] = (grad_hidden[...] + norm_back(back, row_of(gain, 0, meta), unit, scale)).astype(BF)
    tables[0:1, :] = jnp.sum(back * unit, axis=0, keepdims=True)
    tables[1:2, :] = jnp.sum(back, axis=0, keepdims=True)


def part_out(out, at, whole_ref, axis, side):
    if axis == "x":
        out[..., at] = whole_ref[:, :, side]
    else:
        out[..., at] = whole_ref[:, side]


def up_product_kernel(axis, meta, normed, pre_low, away, kept, held):
    held[...] = dot_tn(normed[...], pre_low[...]).astype(BF).reshape(held.shape)
    side = meta[PX] if axis == "x" else meta[PY]
    if axis == "x":
        away[...] = held[:, :, 1 - side]
        kept[...] = held[:, :, side]
    else:
        away[...] = held[:, 1 - side]
        kept[...] = held[:, side]


def down_product_kernel(meta, mine, act_a, act_b, act_c, low, low_a, low_b, low_c, swap_a, swap_b, swap_c, own, away, lows, held):
    @pl.when(pl.program_id(0) == 0)
    def _():
        here = pl.multiple_of(meta[MP] * HW, HW)
        there = pl.multiple_of((1 - meta[MP]) * HW, HW)
        for k, (half, other) in enumerate(((low_a, swap_a), (low_b, swap_b), (low_c, swap_c))):
            lows[k, :, pl.ds(here, HW)] = half[...]
            lows[k, :, pl.ds(there, HW)] = other[...]

    at = pl.ds(pl.multiple_of(pl.program_id(0) * TILE, TILE), TILE)
    found = dot_tn(mine[...], low[:, at])
    for k, act in enumerate((act_a, act_b, act_c)):
        found += dot_tn(act[...], lows[k, :, at])
    held[...] = found.reshape(held.shape)
    own[...] = held[meta[OUTER]]
    for m in range(1, held.shape[0]):
        away[m - 1] = held[jnp.bitwise_xor(meta[OUTER], m)].astype(BF)


def qkv_product_kernel(axis, meta, normed, normed_prompt, local, away, kept, normed_t, held):
    c = pl.program_id(0)

    @pl.when(c == 0)
    def _():
        normed_t[:, :TOK] = normed[...].T
        normed_t[:, TOK:] = normed_prompt[...].T

    held[pl.ds(pl.multiple_of(c * D, D), D), :] = dot_nn(normed_t[...], local[0]).astype(BF)

    @pl.when(c == 2)
    def _():
        outer, _, rows, columns = away.shape
        parts = held[...].reshape(outer, 2, 2, rows, columns)
        if axis == "x":
            low_side, high_side = parts[:, :, 0], parts[:, :, 1]
            side = meta[PX]
        else:
            low_side, high_side = parts[:, 0], parts[:, 1]
            side = meta[PY]
        away[...] = jnp.where(side == 0, high_side, low_side)
        kept[...] = jnp.where(side == 0, low_side, high_side)


def out_product_kernel(meta, attended_t, hidden_low, tables, away_x, kept_x, away_y, kept_y, held_x, held_y):
    found = dot_nn(attended_t[...], hidden_low[...]).astype(BF)
    rows = held_x.shape[3]
    held_x[..., :HW] = found[:, :HW].reshape(held_x.shape[:3] + (rows, HW))
    held_x[..., HW:] = tables[...].reshape(held_x.shape[:3] + (rows, 128))
    held_y[...] = found[:, HW:].reshape(held_y.shape)
    away_x[...] = held_x[:, :, 1 - meta[PX]]
    kept_x[...] = held_x[:, :, meta[PX]]
    away_y[...] = held_y[:, 1 - meta[PY]]
    kept_y[...] = held_y[:, meta[PY]]


def second_kernel(meta, kept_x, got_x, kept_y, got_y, away_x, own_x, away_y, own_y, held_x, held_y):
    held_x[...] = kept_x[...].astype(F32) + got_x[...].astype(F32)
    held_y[...] = kept_y[...].astype(F32) + got_y[...].astype(F32)
    away_x[...] = held_x[:, 1 - meta[PY]].astype(BF)
    own_x[...] = held_x[:, meta[PY]].astype(BF)
    away_y[...] = held_y[:, 1 - meta[PX]].astype(BF)
    own_y[...] = held_y[:, meta[PX]].astype(BF)


def third_kernel(radix, meta, kept_x, got_x, kept_y, got_y, own, away, held):
    left = kept_x.shape[-1]
    held[..., :left] = kept_x[...].astype(F32) + got_x[...].astype(F32)
    held[..., left:] = kept_y[...].astype(F32) + got_y[...].astype(F32)
    rest = held.shape[0] // radix
    digit = meta[OUTER] // rest
    for m in range(radix):
        at = pl.ds(jnp.bitwise_xor(digit, m) * rest, rest)
        if m == 0:
            own[...] = held[at]
        else:
            away[m - 1] = held[at].astype(BF)


def to_rows(out, at, value):
    rows, columns = value.shape
    across = columns // 128
    for j in range(across):
        piece = value[:, 128 * j : 128 * (j + 1)]
        if across == 1:
            out[at : at + rows, :] = piece
        else:
            out[pl.ds(at + j, rows, stride=across), :] = piece


def finish_kernel(received, meta, *refs):
    *ins, out, squares = refs
    sums = []
    for k in range(4):
        own, got = ins[2 * k], ins[2 * k + 1]
        value = own[0]
        for m in range(received):
            value = value + got[m, 0].astype(F32)
        sums.append(value)
    at = 0
    tables = sums[1][:, HW : HW + 128]
    third = jnp.concatenate([sums[1][:, :HW], sums[1][:, HW + 128 :]], axis=1)
    for value in (sums[0], third, sums[2], sums[3]):
        to_rows(out, at, value)
        at += value.size // 128
    entries = out.shape[0] - at
    out[at:, :] = tables[:entries, :]
    total = jnp.sum(tables * tables, axis=0, keepdims=True)
    for value in (sums[0], third, sums[2], sums[3]):
        line = jnp.sum(value * value, axis=0, keepdims=True)
        for j in range(value.shape[1] // 128):
            total = total + line[:, 128 * j : 128 * (j + 1)]
    squares[...] = jnp.broadcast_to(jnp.sum(total, axis=1, keepdims=True), squares.shape)


def adam_kernel(bounds, rates, meta, square_sum, fixes, gradient, master, first, second, ema, new_first, new_second, new_master, copy, new_ema):
    norm = jnp.sqrt(square_sum[0:1, 0:1])
    clip = jnp.minimum(1.0, CLIP_NORM / (norm + 1e-06))
    rows = gradient.shape[0]
    at = pl.program_id(0) * rows + lax.broadcasted_iota(jnp.int32, (rows, 1), 0)
    rate = jnp.full((rows, 1), rates[0], F32)
    for bound, value in zip(bounds, rates[1:]):
        rate = jnp.where(at >= bound, value, rate)
    clipped = clip * gradient[...]
    moment = BETA_ONE * first[...] + (1.0 - BETA_ONE) * clipped
    square = BETA_TWO * second[...] + (1.0 - BETA_TWO) * clipped * clipped
    new_first[...] = moment
    new_second[...] = square
    one, two = fixes[0:1, 0:1], fixes[0:1, 1:2]
    update = (moment * one) / (jnp.sqrt(square * two) + 1e-08)
    weights = master[...] - rate * (update + WEIGHT_DECAY * master[...])
    new_master[...] = weights
    copy[...] = weights.astype(BF)
    new_ema[...] = EMA_DECAY * ema[...] + (1.0 - EMA_DECAY) * weights


def partner(value, axis, flip):
    count = lax.axis_size(axis)
    return lax.ppermute(value, axis, [(i, i ^ flip) for i in range(count)])


def radices(outer):
    found = []
    while outer > 1:
        step = 4 if outer % 4 == 0 else 2
        found.append(step)
        outer //= step
    return found


def outer_steps(own, away, outer, outer_index):
    steps = radices(outer)
    rest = outer // steps[0]
    got = [partner(away[m - 1], "dp", 4 * m * rest) for m in range(1, steps[0])]
    for radix in steps[1:]:
        total = own
        for item in got:
            total = total + item.astype(F32)
        width = rest
        rest //= radix
        digit = lax.rem(outer_index, width) // rest
        cut = total.reshape((radix, rest) + total.shape[1:])
        own = lax.dynamic_index_in_dim(cut, digit, 0, keepdims=False)
        got = [
            partner(lax.dynamic_index_in_dim(cut, digit ^ m, 0, keepdims=False).astype(BF), "dp", 4 * m * rest)
            for m in range(1, radix)
        ]
    return own, got


def body(
    tokens, cotangent, qkv_weight, out_weight, up_weight, down_weight, norm_gain, norm_shift,
    lengths, prompt_src, prompt_len, codebook_section, adam_step, master, first_moment, second_moment, ema_weight,
):
    dp_index = lax.axis_index("dp")
    mp_index = lax.axis_index("mp")
    count = lax.axis_size("dp")
    outer = count // 4
    plane, outer_index = lax.rem(dp_index, 4), dp_index // 4
    meta = jnp.stack(
        [mp_index, plane % 2, plane // 2, plane, outer_index, lengths[0], prompt_src[0], prompt_len[0], codebook_section[0]]
    ).astype(jnp.int32)
    first_radix = radices(outer)[0]
    rest = outer // first_radix

    half_rows = PMAX // 2
    (prompt_rows,) = call(
        prompt_norm_kernel, meta, (tokens, norm_gain, norm_shift),
        [block((half_rows, D), lambda i, m: (m[MP], 0)), whole(norm_gain.shape), whole(norm_shift.shape)],
        [shaped((half_rows, D), BF)], [whole((half_rows, D))], name="prompt_norm",
    )
    rows_from = [partner(prompt_rows, "dp", k) for k in (1, 2, 3)]
    low, low_half = simple(
        mask_kernel, meta, (cotangent,), [shaped((TOK, D), BF), shaped((TOK, HW), BF)], name="mask"
    )
    hidden_rows = HF // count
    split = hidden_rows if hidden_rows % 128 == 0 else 0
    low_from = [partner(low_half, "dp", k) for k in (1, 2, 3)]
    low_swap = [partner(item, "mp", 1) for item in low_from]

    normed, projected = call(
        qkv_kernel, meta, (tokens, norm_gain, norm_shift, qkv_weight),
        [whole(tokens.shape), whole(norm_gain.shape), whole(norm_shift.shape), block((1, D, HW), lambda c, m: (c, 0, 0))],
        [shaped((TOK, D), BF), shaped((3, TOK, HW), BF)],
        [whole((TOK, D)), block((1, TOK, HW), lambda c, m: (c, 0, 0))],
        grid=(3,), flops=2 * TOK * D * 3 * HW, name="qkv",
    )
    (grad_act,) = call(
        grad_act_kernel, meta, (low, down_weight),
        [whole((TOK, D)), block((2 * TILE, D), lambda t, m: (t, 0))],
        [shaped((TOK, HF), F32)], [block((TOK, 2 * TILE), lambda t, m: (0, t))],
        grid=(HF // (2 * TILE),), flops=2 * TOK * D * HF, name="grad_act",
    )
    relative = jnp.bitwise_xor(lax.rem(prompt_src[0], 4), plane)
    here = jnp.where(relative == 1, rows_from[0], jnp.where(relative == 2, rows_from[1], rows_from[2]))
    there = partner(here, "mp", 1)
    normed_prompt, prompt_pair, attended_t, log_total, mixed = simple(
        attend_kernel, meta, (projected, here, there, qkv_weight, out_weight),
        [shaped((PMAX, D), BF), shaped((2, PMAX, HW), BF), shaped((HW, TOK), BF), shaped((HEADS, TOK), F32), shaped((TOK, D), BF)],
        scratch=[pltpu.VMEM((KEYS, HW), BF), pltpu.VMEM((KEYS, HW), BF), pltpu.VMEM((HW, KEYS), BF)],
        flops=2 * TOK * HW * (4 * KEYS + D), name="attend",
    )
    mixed_there = partner(mixed, "mp", 1)
    pieces = 4 if split else 1
    hidden, normed_second, act, pre_low, second_part = call(
        functools.partial(ffn_kernel, split), meta, (tokens, mixed, mixed_there, norm_gain, norm_shift, up_weight, grad_act),
        [whole((TOK, D))] * 3 + [whole(norm_gain.shape)] * 2
        + [block((D, TILE), lambda t, m: (0, t)), block((TOK, TILE), lambda t, m: (0, t))],
        [shaped((TOK, D), F32), shaped((TOK, D), BF), shaped((pieces, TOK, HF // pieces), BF), shaped((TOK, HF), BF), shaped((TOK, D), BF)],
        [whole((TOK, D)), whole((TOK, D)), whole((pieces, TOK, HF // pieces)), block((TOK, TILE), lambda t, m: (0, t)), whole((TOK, D))],
        grid=(HF // TILE,), scratch=[pltpu.VMEM((TOK, D), F32)], flops=4 * TOK * D * HF, name="ffn",
    )
    second_there = partner(second_part, "mp", 1)

    if split:
        act_pieces = [act[k] for k in range(4)]
    else:
        cut = act[0].reshape(TOK, outer, 4, hidden_rows)
        act_pieces = [
            lax.dynamic_index_in_dim(cut, plane ^ k, 2, keepdims=False).reshape(TOK, HF // 4) for k in range(4)
        ]
    act_from = [partner(act_pieces[k], "dp", k) for k in (1, 2, 3)]

    up_rows = D // count
    up_half = [shaped((outer, 2, up_rows, D), BF)] * 2

    def up_product(axis, at):
        return call(
            functools.partial(up_product_kernel, axis), meta, (normed_second, pre_low),
            [whole((TOK, D)), block((TOK, TILE), lambda t, m: (0, at + t))],
            up_half, [block((outer, 2, up_rows, TILE), lambda t, m: (0, 0, 0, t))] * 2,
            grid=(D // TILE,), scratch=[pltpu.VMEM((outer, 2, 2, up_rows, TILE), BF)],
            flops=2 * TOK * D * D, name="up_product_" + axis,
        )

    up_away_x, up_kept_x = up_product("x", 0)
    up_got_x = partner(up_away_x, "dp", 1)
    up_away_y, up_kept_y = up_product("y", D // TILE)
    up_got_y = partner(up_away_y, "dp", 2)

    local, sent, grad_hidden, hidden_low, tables_second = simple(
        attend_back_kernel, meta,
        (second_part, second_there, hidden, norm_gain, low, out_weight, projected, prompt_pair, log_total),
        [shaped((3, KEYS, HW), BF), shaped((3, 2, PMAX, HW), BF), shaped((TOK, D), F32), shaped((TOK, D), BF), shaped((2, D), F32)],
        scratch=[pltpu.VMEM((KEYS, HW), BF), pltpu.VMEM((KEYS, HW), BF), pltpu.VMEM((HW, KEYS), BF), pltpu.VMEM((TOK, HW), BF), pltpu.VMEM((HW, TOK), F32)],
        flops=2 * TOK * HW * (10 * KEYS + D), name="attend_back",
    )
    returned = [partner(sent[k - 1], "dp", k) for k in (1, 2, 3)]

    (ffn_part,) = call(
        functools.partial(down_kernel, split), meta, (act, down_weight),
        [whole(act.shape), block((TILE, D), lambda t, m: (t, 0))],
        [shaped((TOK, D), BF)], [whole((TOK, D))],
        grid=(HF // TILE,), scratch=[pltpu.VMEM((TOK, D), F32)], flops=2 * TOK * D * HF, name="down",
    )
    ffn_there = partner(ffn_part, "mp", 1)
    (block_out,) = simple(block_out_kernel, meta, (hidden, ffn_part, ffn_there), [shaped((TOK, D), BF)], name="block_out")

    if first_radix == outer:
        down_own, down_away = call(
            down_product_kernel, meta,
            tuple([act_pieces[0]] + act_from + [low] + low_from + low_swap),
            [whole((TOK, HF // 4))] * 4 + [whole((TOK, D))] + [whole((TOK, HW))] * 6,
            [shaped((hidden_rows, D), F32), shaped((outer - 1, hidden_rows, D), BF)],
            [block((hidden_rows, TILE), lambda t, m: (0, t)), block((outer - 1, hidden_rows, TILE), lambda t, m: (0, 0, t))],
            grid=(D // TILE,), scratch=[pltpu.VMEM((3, TOK, D), BF), pltpu.VMEM((outer, hidden_rows, TILE), F32)],
            flops=2 * TOK * D * HF, name="down_product",
        )
        down_own = down_own[None]
        down_away = down_away[:, None]
    else:
        lows = [low] + [
            jnp.where(mp_index == 0, jnp.concatenate([a, b], 1), jnp.concatenate([b, a], 1)) for a, b in zip(low_from, low_swap)
        ]
        found = sum(dot_tn(a, b) for a, b in zip(act_pieces[:1] + act_from, lows))
        cut = found.reshape(first_radix, rest, hidden_rows, D)
        digit = outer_index // rest
        down_own = lax.dynamic_index_in_dim(cut, digit, 0, keepdims=False)
        down_away = jnp.stack(
            [lax.dynamic_index_in_dim(cut, digit ^ m, 0, keepdims=False) for m in range(1, first_radix)]
        ).astype(BF)
    down_sum = outer_steps(down_own, down_away, outer, outer_index)

    def second_stage(kept_x, got_x, kept_y, got_y, name):
        _, _, rows, wide = kept_x.shape
        tall = kept_y.shape[-1]
        outs = [shaped((outer, rows, wide), BF)] * 2 + [shaped((outer, rows, tall), BF)] * 2
        away_x, own_x, away_y, own_y = simple(
            second_kernel, meta, (kept_x, got_x, kept_y, got_y), outs,
            scratch=[pltpu.VMEM(kept_x.shape, F32), pltpu.VMEM(kept_y.shape, F32)], name=name + "_second",
        )
        return own_x, partner(away_x, "dp", 2), own_y, partner(away_y, "dp", 1)

    def third_stage(own_x, got_x, own_y, got_y, name):
        rows = own_x.shape[1]
        columns = own_x.shape[2] + own_y.shape[2]
        own, away = simple(
            functools.partial(third_kernel, first_radix), meta, (own_x, got_x, own_y, got_y),
            [shaped((rest, rows, columns), F32), shaped((first_radix - 1, rest, rows, columns), BF)],
            scratch=[pltpu.VMEM((outer, rows, columns), F32)], name=name + "_third",
        )
        return outer_steps(own, away, outer, outer_index)

    up_sum = third_stage(*second_stage(up_kept_x, up_got_x, up_kept_y, up_got_y, "up"), "up")

    qkv_rows = 3 * D // count
    qkv_half = [shaped((outer, 2, qkv_rows, HW // 2), BF)] * 2

    def qkv_product(axis, at):
        return call(
            functools.partial(qkv_product_kernel, axis), meta, (normed, normed_prompt, local),
            [whole((TOK, D)), whole((PMAX, D)), block((1, KEYS, HW // 2), lambda c, m: (c, 0, at))],
            qkv_half, [whole(item.shape) for item in qkv_half],
            grid=(3,), scratch=[pltpu.VMEM((D, KEYS), BF), pltpu.VMEM((3 * D, HW // 2), BF)],
            flops=2 * KEYS * D * 3 * HW // 2, name="qkv_product_" + axis,
        )

    qkv_away_x, qkv_kept_x = qkv_product("x", 0)
    qkv_got_x = partner(qkv_away_x, "dp", 1)
    qkv_away_y, qkv_kept_y = qkv_product("y", 1)
    qkv_got_y = partner(qkv_away_y, "dp", 2)

    (normed_part,) = call(
        grad_normed_kernel, meta, (local, *returned, qkv_weight),
        [block((1, KEYS, HW), lambda c, m: (c, 0, 0))] + [whole((2, PMAX, HW))] * 3 + [block((1, D, HW), lambda c, m: (c, 0, 0))],
        [shaped((TOK, D), BF)], [whole((TOK, D))],
        grid=(3,), scratch=[pltpu.VMEM((PMAX, HW), BF), pltpu.VMEM((TOK, D), F32)],
        flops=2 * KEYS * D * 3 * HW, name="grad_normed",
    )
    normed_there = partner(normed_part, "mp", 1)
    input_grad, tables_first = simple(
        input_grad_kernel, meta, (normed_part, normed_there, tokens, norm_gain, grad_hidden),
        [shaped((TOK, D), BF), shaped((2, D), F32)], name="input_grad",
    )
    qkv_sum = third_stage(*second_stage(qkv_kept_x, qkv_got_x, qkv_kept_y, qkv_got_y, "qkv"), "qkv")

    out_rows = HW // count
    selector = (jnp.arange(SECTIONS) == codebook_section[0]).astype(F32)
    tables = jnp.stack([tables_first, tables_second])
    tables = lax.dynamic_slice_in_dim(tables, mp_index * HW, HW, 2)
    spread = selector[None, None, :, None] * jnp.transpose(tables, (1, 0, 2))[:, :, None, :]
    entries = 2 * SECTIONS * HW // count
    spread = jnp.transpose(spread.reshape(2, count, entries), (1, 0, 2)).reshape(count, 2 * entries // 128, 128).astype(BF)
    spread = jnp.pad(spread, ((0, 0), (0, out_rows - 2 * entries // 128), (0, 0)))
    wide, tall = HW + 128, HW
    away_x, kept_x, away_y, kept_y = simple(
        out_product_kernel, meta, (attended_t, hidden_low, spread),
        [shaped((outer, 2, out_rows, wide), BF)] * 2 + [shaped((outer, 2, out_rows, tall), BF)] * 2,
        scratch=[pltpu.VMEM((outer, 2, 2, out_rows, wide), BF), pltpu.VMEM((outer, 2, 2, out_rows, tall), BF)],
        flops=2 * TOK * HW * D, name="out_product",
    )
    out_sum = third_stage(
        *second_stage(kept_x, partner(away_x, "dp", 1), kept_y, partner(away_y, "dp", 2), "out"), "out"
    )

    flat = master.shape[1]
    received = len(down_sum[1])
    ins = []
    for own, got in (qkv_sum, out_sum, up_sum, down_sum):
        ins += [own, jnp.stack(got)]
    gradient, squares = simple(
        functools.partial(finish_kernel, received), meta, ins,
        [shaped((flat // 128, 128), F32), shaped((8, 128), F32)], name="finish",
    )
    squares = squares + partner(squares, "mp", 1)
    step = 1
    while step < count:
        squares = squares + partner(squares, "dp", step)
        step *= 2
    grad_norm = jnp.sqrt(squares[0, :1])
    step_count = adam_step[0].astype(F32)
    fixes = jnp.stack([1.0 / (1.0 - jnp.power(BETA_ONE, step_count)), 1.0 / (1.0 - jnp.power(BETA_TWO, step_count))]).reshape(1, 2)
    lines = flat // 128
    sizes = [qkv_rows * HW, out_rows * D, up_rows * HF, hidden_rows * D, entries, entries]
    bounds, at = [], 0
    for size in sizes[:-1]:
        at += size // 128 if size % 128 == 0 else 0
        bounds.append(at)
    rates = [D ** (-0.5), OUT_FAN ** (-0.5), D ** (-0.5), FF ** (-0.5), 0.2, 0.2]
    grid = next((g for g in (7, 5, 1) if lines % (8 * g) == 0), 1)
    chunk = block((lines // grid, 128), lambda t, m: (t, 0))
    flats = [item.reshape(lines, 128) for item in (master, first_moment, second_moment, ema_weight)]
    new_first, new_second, new_master, copy, new_ema = call(
        functools.partial(adam_kernel, bounds, rates), meta, (squares, fixes, gradient, *flats),
        [whole((8, 128)), whole((1, 2))] + [chunk] * 5,
        [shaped((lines, 128), F32)] * 3 + [shaped((lines, 128), BF), shaped((lines, 128), F32)],
        [chunk] * 5, grid=(grid,), name="adam",
    )
    return (
        block_out,
        input_grad,
        grad_norm,
        new_first.reshape(1, flat),
        new_second.reshape(1, flat),
        new_master.reshape(1, flat),
        copy.reshape(1, flat),
        new_ema.reshape(1, flat),
    )


def solution(mesh):
    placed = (
        P("dp", None), P("dp", None), P(None, None, "mp"), P("mp", None), P(None, "mp"), P("mp", None), P(), P(),
        P("dp"), P("dp"), P("dp"), P("dp"), P(),
        P("mp", "dp"), P("mp", "dp"), P("mp", "dp"), P("mp", "dp"),
    )
    flat = P("mp", "dp")
    return jax.shard_map(
        body, mesh=mesh, in_specs=placed,
        out_specs=(P("dp", None), P("dp", None), P(), flat, flat, flat, flat, flat),
        check_vma=False,
    )
```

```python
import functools

import jax
import jax.numpy as jnp
from jax import lax
from jax.experimental import pallas as pl
from jax.experimental.pallas import tpu as pltpu
from jax.sharding import PartitionSpec as P

D = 1024
HDIM = 64
FF = 4096
SECTIONS = 8
TOK = 384
PMAX = 96
KEYS = TOK + PMAX
OUT_FAN = 2
HW = D // 2
HF = FF // 2
HEADS = HW // HDIM
CLIP_NORM = 1.0
BETA_ONE = 0.5
BETA_TWO = 0.5
WEIGHT_DECAY = 0.1
EMA_DECAY = 0.75

BF = jnp.bfloat16
F32 = jnp.float32
MP, PX, PY, PLANE, OUTER, LENGTH, SOURCE, PROMPT, SECTION = range(9)


def shaped(shape, dtype):
    return jax.ShapeDtypeStruct(shape, dtype)


def dot_nn(a, b):
    return lax.dot_general(a, b, (((1,), (0,)), ((), ())), preferred_element_type=F32)


def dot_nt(a, b):
    return lax.dot_general(a, b, (((1,), (1,)), ((), ())), preferred_element_type=F32)


def dot_tn(a, b):
    return lax.dot_general(a, b, (((0,), (0,)), ((), ())), preferred_element_type=F32)


def block(shape, index):
    return pl.BlockSpec(shape, index)


def whole(shape):
    rank = len(shape)
    return pl.BlockSpec(shape, lambda *_: (0,) * rank)


class Order:
    def __init__(self, meta):
        self.meta = meta
        self.last = None

    def next(self):
        if self.last is None:
            return self.meta
        return lax.optimization_barrier((self.meta, self.last))[0]


HBM = pl.BlockSpec(memory_space=pltpu.HBM)


def fetch(source, target, sem):
    copy = pltpu.make_async_copy(source, target, sem)
    copy.start()
    return copy


def call(kernel, order, inputs, in_specs, outs, out_specs, grid=(1,), scratch=(), flops=0, name=None, vmem=20):
    found = pl.pallas_call(
        kernel,
        grid_spec=pltpu.PrefetchScalarGridSpec(
            num_scalar_prefetch=1, grid=grid, in_specs=in_specs, out_specs=out_specs, scratch_shapes=scratch
        ),
        out_shape=outs,
        compiler_params=pltpu.CompilerParams(vmem_limit_bytes=vmem << 20),
        cost_estimate=pl.CostEstimate(flops=1, bytes_accessed=1, transcendentals=0),
        name=name,
    )(order.next(), *inputs)
    order.last = min(found, key=lambda item: item.size)
    return found


def simple(kernel, order, inputs, outs, far=(), **kw):
    return call(kernel, order, inputs, [HBM if k in far else whole(a.shape) for k, a in enumerate(inputs)], outs, [whole(o.shape) for o in outs], **kw)


def unit_rows(values):
    centred = values - jnp.mean(values, axis=-1, keepdims=True)
    scale = lax.rsqrt(jnp.mean(centred * centred, axis=-1, keepdims=True) + 1e-05)
    return centred * scale, scale


def norm_back(grad, gain_row, unit, scale):
    e = gain_row * grad
    return scale * (e - jnp.mean(e, axis=-1, keepdims=True) - unit * jnp.mean(e * unit, axis=-1, keepdims=True))


def row_of(rows, which):
    return rows[which : which + 1, :]


def valid_rows(meta):
    return lax.broadcasted_iota(jnp.int32, (TOK, 1), 0) < meta[LENGTH]


def keys_ok(meta):
    at = lax.broadcasted_iota(jnp.int32, (KEYS, 1), 0)
    return at < jnp.where(at < TOK, meta[LENGTH], TOK + meta[PROMPT])


def summed(refs):
    here, there = refs
    return here[...].astype(F32) + there[...].astype(F32)


def start_kernel(
    place, lengths, source, prompt, section, tokens, cotangent, gain, shift,
    out, low, half, meta, rows, some, whole_low, tables, sems,
):
    size = out.shape[0]
    copies = [fetch(tokens.at[pl.ds(pl.multiple_of(place[MP] * size, size), size), :], some, sems.at[0])]
    for k, (table, norm) in enumerate(((gain, 0), (shift, 0), (gain, 1), (shift, 1))):
        copies.append(fetch(table.at[norm], tables.at[k], sems.at[1 + k]))
    late = fetch(cotangent, whole_low, sems.at[5])
    for k in range(LENGTH):
        meta[k] = place[k]
    meta[LENGTH] = lengths[0]
    meta[SOURCE] = source[0]
    meta[PROMPT] = prompt[0]
    meta[SECTION] = section[0]
    for copy in copies:
        copy.wait()
    for k in range(4):
        rows[k : k + 1, :] = tables[k, pl.ds(section[0], 1), :]
    rows[4:, :] = jnp.zeros((4, D), F32)
    unit, _ = unit_rows(some[...].astype(F32))
    out[...] = (row_of(rows, 0) * unit + row_of(rows, 1)).astype(BF)
    late.wait()
    valid = lax.broadcasted_iota(jnp.int32, (TOK, 1), 0) < lengths[0]
    kept = jnp.where(valid, whole_low[...], jnp.zeros((), BF))
    low[...] = kept

    @pl.when(place[MP] == 0)
    def _():
        half[...] = kept[:, :HW]

    @pl.when(place[MP] == 1)
    def _():
        half[...] = kept[:, HW:]


def qkv_kernel(meta, tokens, rows, qkv, normed, projected, frames, weights, sems):
    first = fetch(tokens, frames, sems.at[3])
    copies = [fetch(qkv.at[c], weights.at[c], sems.at[c]) for c in range(3)]
    first.wait()
    unit, _ = unit_rows(frames[...].astype(F32))
    normed[...] = (row_of(rows, 0) * unit + row_of(rows, 1)).astype(BF)
    for c in range(3):
        copies[c].wait()
        projected[c] = dot_nn(normed[...], weights[c]).astype(BF)


def grad_act_kernel(meta, low, down, out, weights, sems):
    size = HF // 4
    copies = [fetch(down.at[pl.ds(t * size, size), :], weights.at[pl.ds(t * size, size), :], sems.at[t]) for t in range(4)]
    for t in range(4):
        copies[t].wait()
        out[:, t * size : (t + 1) * size] = dot_nt(low[...], weights[t * size : (t + 1) * size, :])


def attend_kernel(
    meta, projected, here, there, qkv, out_weight, low_half, low_x,
    normed_prompt, prompt_pair, attended_t, log_total, part, joined, keys, values, values_t, weights, out_w, sems,
):
    copies = [fetch(qkv.at[c], weights.at[c - 1], sems.at[c - 1]) for c in (1, 2)]
    last = fetch(out_weight, out_w, sems.at[2])
    joined[0] = low_half[...]
    joined[1] = low_x[...]
    keys[:TOK] = projected[1]
    values[:TOK] = projected[2]
    half = PMAX // 2
    normed_prompt[pl.ds(pl.multiple_of(meta[MP] * half, half), half), :] = here[...]
    normed_prompt[pl.ds(pl.multiple_of((1 - meta[MP]) * half, half), half), :] = there[...]
    rows = normed_prompt[...]
    copies[0].wait()
    pair_k = dot_nn(rows, weights[0]).astype(BF)
    copies[1].wait()
    pair_v = dot_nn(rows, weights[1]).astype(BF)
    prompt_pair[0] = pair_k
    prompt_pair[1] = pair_v
    keys[TOK:] = pair_k
    values[TOK:] = pair_v
    values_t[...] = values[...].T
    counted = keys_ok(meta)
    lane = lax.broadcasted_iota(jnp.int32, (1, 2 * HDIM), 1)
    for head in range(HEADS):
        at = (head // 2) * 2 * HDIM
        mine = jnp.where((lane // HDIM) == head % 2, HDIM ** (-0.5), 0.0).astype(BF)
        query = projected[0, :, at : at + 2 * HDIM] * mine
        scores = jnp.where(counted, dot_nt(keys[:, at : at + 2 * HDIM], query), -1e30)
        top = jnp.max(scores, axis=0, keepdims=True)
        grown = jnp.exp(scores - top)
        total = jnp.sum(grown, axis=0, keepdims=True)
        probability = (grown * (1.0 / total)).astype(BF)
        rows_at = slice(head * HDIM, (head + 1) * HDIM)
        attended_t[rows_at, :] = dot_nn(values_t[rows_at, :], probability).astype(BF)
        log_total[head : head + 1, :] = top + jnp.log(total)
    last.wait()
    part[...] = dot_tn(attended_t[...], out_w[...]).astype(BF)


TILE = 256


ERFC = (0.235325614, 0.0913858287, 0.649566092, -0.635408842, 0.886669787, -0.227538481)


def gelu_parts(values):
    decay = jnp.exp(-0.5 * values * values)
    t = 1.0 / (1.0 + (0.39 * 0.5**0.5) * jnp.abs(values))
    tail = 0.5 * ERFC[-1]
    for factor in ERFC[-2::-1]:
        tail = tail * t + 0.5 * factor
    tail = tail * t * decay
    cdf = jnp.where(values < 0.0, tail, 1.0 - tail)
    return cdf, cdf + values * (decay * (0.5 / jnp.pi) ** 0.5)


def ffn_kernel(split, meta, tokens, here, there, rows, up, grad_act, hidden, normed, *refs):
    *act, pre_low, part, pre, held, frames, weights, sems = refs
    steps = HF // TILE
    first = fetch(tokens, frames, sems.at[steps])
    copies = [fetch(up.at[:, pl.ds(t * TILE, TILE)], weights.at[:, pl.ds(t * TILE, TILE)], sems.at[t]) for t in range(steps)]
    first.wait()
    state = frames[...].astype(F32) + summed((here, there))
    hidden[...] = state
    unit, _ = unit_rows(state)
    normed[...] = (row_of(rows, 2) * unit + row_of(rows, 3)).astype(BF)
    for t in range(steps):
        copies[t].wait()
        at = slice(t * TILE, (t + 1) * TILE)
        pre[:, at] = dot_nn(normed[...], weights[:, at])
    across = split or 128

    def block_of_rows(r, _):
        some = pl.ds(pl.multiple_of(r * 64, 64), 64)
        for t in range(HF // across):
            at = slice(t * across, (t + 1) * across)
            values = pre[some, at]
            cdf, slope = gelu_parts(values)
            activated = (values * cdf).astype(BF)
            if split:
                held[t % 4, some, (t // 4) * split : (t // 4 + 1) * split] = activated
            else:
                act[0][some, at] = activated
            pre_low[some, at] = (grad_act[some, at] * slope).astype(BF)
        return 0

    lax.fori_loop(0, TOK // 64, block_of_rows, 0)
    part[...] = dot_nt(pre_low[...], weights[...]).astype(BF)
    if split:
        for k, out in enumerate(act):
            out[...] = held[jnp.bitwise_xor(meta[PLANE], k)]


def join_kernel(meta, act_x, act_y, out):
    out[...] = act_x[1]


def down_kernel(split, meta, *refs):
    *act, down, part, total = refs
    step = pl.program_id(0)

    @pl.when(step == 0)
    def _():
        total[...] = jnp.zeros_like(total)

    if split:
        rows = down[...].reshape(HF // 4, D)
        piece = jnp.bitwise_xor(step, meta[PLANE])
        for k, value in enumerate(act):

            @pl.when(piece == k)
            def _(value=value):
                total[...] += dot_nn(value[...], rows)

    else:
        total[...] += dot_nn(act[0][:, pl.ds(pl.multiple_of(step * (HF // 4), HF // 4), HF // 4)], down[...])

    @pl.when(step == pl.num_programs(0) - 1)
    def _():
        part[...] = total[...].astype(BF)


def block_out_kernel(meta, hidden, here, there, out):
    out[...] = (hidden[...] + summed((here, there))).astype(BF)


def attend_back_kernel(
    meta, here, there, hidden, rows, low, out_weight, projected, prompt_pair, log_total,
    local, sent, along, grad_hidden, hidden_low, tables, keys, values, keys_t, grads, query_t, out_w, sems,
):
    last = fetch(out_weight, out_w, sems.at[0])
    back = summed((here, there))
    unit, scale = unit_rows(hidden[...])
    full = low[...].astype(F32) + norm_back(back, row_of(rows, 2), unit, scale)
    grad_hidden[...] = full
    tables[0:1, :] = jnp.sum(back * unit, axis=0, keepdims=True)
    tables[1:2, :] = jnp.sum(back, axis=0, keepdims=True)
    rounded = full.astype(BF)
    hidden_low[...] = rounded
    last.wait()
    grads[...] = dot_nt(rounded, out_w[...]).astype(BF)
    keys[:TOK] = projected[1]
    keys[TOK:] = prompt_pair[0]
    values[:TOK] = projected[2]
    values[TOK:] = prompt_pair[1]
    keys_t[...] = keys[...].T
    counted = keys_ok(meta)
    lane = lax.broadcasted_iota(jnp.int32, (1, 2 * HDIM), 1)
    left = lane < HDIM
    for pair in range(HEADS // 2):
        at = pair * 2 * HDIM
        span = slice(at, at + 2 * HDIM)
        key_pair, value_pair = keys[:, span], values[:, span]
        query_pair = projected[0, :, span] * jnp.asarray(HDIM ** (-0.5), BF)
        grad_pair = grads[:, span]
        found = []
        for head in (2 * pair, 2 * pair + 1):
            mine = ((lane // HDIM) == head % 2).astype(BF)
            scores = jnp.where(counted, dot_nt(key_pair, query_pair * mine), -1e30)
            probability = jnp.exp(scores - log_total[head : head + 1, :])
            grad_prob = dot_nt(value_pair, grad_pair * mine)
            centre = jnp.sum(probability * grad_prob, axis=0, keepdims=True)
            grad_scores = (probability * (grad_prob - centre)).astype(BF)
            rows_at = slice(head * HDIM, (head + 1) * HDIM)
            query_t[rows_at, :] = dot_nn(keys_t[rows_at, :], grad_scores) * HDIM ** (-0.5)
            found.append((dot_nn(grad_scores, query_pair), dot_nn(probability.astype(BF), grad_pair)))
        local[1, :, span] = jnp.where(left, found[0][0], found[1][0]).astype(BF)
        local[2, :, span] = jnp.where(left, found[0][1], found[1][1]).astype(BF)
    local[0, :TOK, :] = query_t[...].T.astype(BF)
    local[0, TOK:, :] = jnp.zeros((PMAX, HW), BF)
    relative = jnp.bitwise_xor(lax.rem(meta[SOURCE], 4), meta[PLANE])
    for c in range(2):
        prompt = local[1 + c, TOK:, :]
        for j in range(2):
            sent[j, c] = jnp.where(relative == 1 + 2 * j, prompt, jnp.zeros((), BF))
        along[c] = jnp.where(relative == 2, prompt, jnp.zeros((), BF))


def pass_on_kernel(meta, along, got, out):
    out[...] = (along[...].astype(F32) + got[1].astype(F32)).astype(BF)


def grad_normed_kernel(meta, local, first, second, qkv, part, returned_low, total):
    c = pl.program_id(0)

    @pl.when(c == 0)
    def _():
        total[...] = jnp.zeros_like(total)

    total[...] += dot_nt(local[0, :TOK, :], qkv[0])

    @pl.when(c > 0)
    def _():
        at = c - 1
        returned = first[0, at].astype(F32) + second[at].astype(F32)
        returned_low[...] = returned.astype(BF)
        total[:PMAX, :] += dot_nt(returned_low[...], qkv[0])

    @pl.when(c == 2)
    def _():
        part[...] = total[...].astype(BF)


def input_grad_kernel(meta, here, there, tokens, rows, grad_hidden, out, tables):
    back = summed((here, there))
    unit, scale = unit_rows(tokens[...].astype(F32))
    out[...] = (grad_hidden[...] + norm_back(back, row_of(rows, 0), unit, scale)).astype(BF)
    tables[0:1, :] = jnp.sum(back * unit, axis=0, keepdims=True)
    tables[1:2, :] = jnp.sum(back, axis=0, keepdims=True)


def part_out(out, at, whole_ref, axis, side):
    if axis == "x":
        out[..., at] = whole_ref[:, :, side]
    else:
        out[..., at] = whole_ref[:, side]


def pick(held, axis, side):
    return held[:, :, side] if axis == "x" else held[:, side]


def up_product_kernel(axis, at, meta, normed, pre_low, away, kept, held):
    held[...] = dot_tn(normed[...], pre_low[:, at : at + D]).astype(BF).reshape(held.shape)
    side = meta[PX] if axis == "x" else meta[PY]
    away[...] = pick(held, axis, 1 - side)
    kept[...] = pick(held, axis, side)


def down_product_kernel(meta, mine, act_x, act_y, act_far, low, low_x, low_y, swap_x, swap_y, own, away, held):
    here = pl.ds(pl.multiple_of(meta[MP] * HW, HW), HW)
    there = pl.ds(pl.multiple_of((1 - meta[MP]) * HW, HW), HW)
    for at, x, y in ((here, low_x, low_y), (there, swap_x, swap_y)):
        found = dot_tn(mine[...], low[:, at])
        found += dot_tn(act_x[0], x[...])
        found += dot_tn(act_y[...], y[0])
        found += dot_tn(act_far[...], y[1])
        held[:, :, :, at] = found.reshape(held.shape[:3] + (HW,))
    side = lax.rem(meta[OUTER], 2)
    own[...] = held[:, side]
    away[...] = held[:, 1 - side].astype(BF)


def qkv_product_kernel(axis, at, meta, normed, normed_prompt, local, away, kept, normed_t, held):
    normed_t[:, :TOK] = normed[...].T
    normed_t[:, TOK:] = normed_prompt[...].T
    outer, _, rows, columns = kept.shape
    for c in range(3):
        held[c * D : (c + 1) * D, :] = dot_nn(normed_t[...], local[c, :, at : at + columns]).astype(BF)
    parts = held.reshape(outer, 2, 2, rows, columns)
    side = meta[PX] if axis == "x" else meta[PY]
    away[:, :, :rows] = pick(parts, axis, 1 - side)
    kept[...] = pick(parts, axis, side)


def out_product_kernel(meta, attended_t, hidden_low, tables, away_x, kept_x, away_y, kept_y, held_x, held_y):
    found = dot_nn(attended_t[...], hidden_low[...]).astype(BF)
    rows = held_x.shape[3]
    held_x[..., :HW] = found[:, :HW].reshape(held_x.shape[:3] + (rows, HW))
    held_x[..., HW:] = tables[...].reshape(held_x.shape[:3] + (rows, 128))
    held_y[...] = found[:, HW:].reshape(held_y.shape)
    away_x[...] = held_x[:, :, 1 - meta[PX]]
    kept_x[...] = held_x[:, :, meta[PX]]
    away_y[...] = held_y[:, 1 - meta[PY]]
    kept_y[...] = held_y[:, meta[PY]]


def second_kernel(meta, kept_x, got_x, kept_y, got_y, away_x, own_x, away_y, own_y, held_x, held_y):
    rows = kept_x.shape[2]
    held_x[...] = kept_x[...].astype(F32) + got_x[:, :, :rows].astype(F32)
    held_y[...] = kept_y[...].astype(F32) + got_y[:, :, :rows].astype(F32)
    away_x[...] = held_x[:, 1 - meta[PY]].astype(BF)
    own_x[...] = held_x[:, meta[PY]].astype(BF)
    away_y[...] = held_y[:, 1 - meta[PX]].astype(BF)
    own_y[...] = held_y[:, meta[PX]].astype(BF)


def third_kernel(meta, kept_x, got_x, kept_y, got_y, own, away, held):
    left = kept_x.shape[-1]
    shape = held.shape[:2] + kept_x.shape[1:]
    held[..., :left] = (kept_x[...].astype(F32) + got_x[...].astype(F32)).reshape(shape)
    shape = held.shape[:2] + kept_y.shape[1:]
    held[..., left:] = (kept_y[...].astype(F32) + got_y[...].astype(F32)).reshape(shape)
    side = lax.rem(meta[OUTER], 2)
    own[...] = held[:, side]
    away[...] = held[:, 1 - side].astype(BF)


def direct_kernel(meta, kept_x, got_x, kept_y, got_y, own, *refs):
    *away, held = refs
    left = kept_x.shape[-1]
    held[..., :left] = kept_x[...].astype(F32) + got_x[...].astype(F32)
    held[..., left:] = kept_y[...].astype(F32) + got_y[...].astype(F32)
    own[0] = held[meta[OUTER]]
    for m, out in enumerate(away):
        out[0] = held[jnp.bitwise_xor(meta[OUTER], m + 1)].astype(BF)


def halve_kernel(bit, meta, kept, got, own, away, held):
    held[...] = (kept[...] + got[...].astype(F32)).reshape(held.shape)
    side = lax.rem(lax.shift_right_logical(meta[OUTER], bit), 2)
    own[...] = held[:, side]
    away[...] = held[:, 1 - side].astype(BF)


def to_rows(out, at, value):
    rows, columns = value.shape
    across = columns // 128
    for j in range(across):
        piece = value[:, 128 * j : 128 * (j + 1)]
        if across == 1:
            out[at : at + rows, :] = piece
        else:
            out[pl.ds(at + j, rows, stride=across), :] = piece


def total_of(terms):
    value = terms[0][0]
    for got in terms[1:]:
        value = value + got[0].astype(F32)
    return value


def square_sum(values):
    total = jnp.zeros((1, 128), F32)
    for value in values:
        line = jnp.sum(value * value, axis=0, keepdims=True)
        for j in range(value.shape[1] // 128):
            total = total + line[:, 128 * j : 128 * (j + 1)]
    return jnp.sum(total, axis=1, keepdims=True)


def finish_kernel(counts, meta, *refs):
    *ins, out, squares = refs
    value = total_of(ins)
    to_rows(out, 0, value)
    squares[...] = jnp.broadcast_to(square_sum([value]), squares.shape)


def finish_last_kernel(first, meta, *refs):
    *ins, up_squares, down_squares, qkv_out, out_out, table_out, squares = refs
    value = total_of(ins[:first])
    to_rows(qkv_out, 0, value)
    both = total_of(ins[first:])
    tables = both[:, HW : HW + 128]
    third = jnp.concatenate([both[:, :HW], both[:, HW + 128 :]], axis=1)
    to_rows(out_out, 0, third)
    table_out[...] = tables[: table_out.shape[0], :]
    squares[...] = square_sum([value, third, tables]) + up_squares[...] + down_squares[...]


def adam_kernel(rates, meta, squares, fixes, *refs):
    pieces, (master, first, second, ema, new_first, new_second, new_master, copy, new_ema) = refs[: len(rates)], refs[len(rates) :]
    clip = jnp.minimum(1.0, CLIP_NORM / (jnp.sqrt(squares[0:1, 0:1]) + 1e-06))
    one, two = fixes[0:1, 0:1], fixes[0:1, 1:2]
    start = 0
    for piece, rate in zip(pieces, rates):
        rows = piece.shape[0]
        step = next(n for n in (256, 128, 64, 32, 16, 8, 4, 2, 1) if rows % n == 0)

        def one_chunk(k, _, piece=piece, rate=rate, start=start, step=step):
            at = pl.ds(start + k * step, step)
            clipped = clip * piece[pl.ds(k * step, step), :]
            moment = BETA_ONE * first[at, :] + (1.0 - BETA_ONE) * clipped
            square = BETA_TWO * second[at, :] + (1.0 - BETA_TWO) * clipped * clipped
            new_first[at, :] = moment
            new_second[at, :] = square
            update = (moment * one) / (jnp.sqrt(square * two) + 1e-08)
            old = master[at, :]
            weights = old - rate * (update + WEIGHT_DECAY * old)
            new_master[at, :] = weights
            new_ema[at, :] = EMA_DECAY * ema[at, :] + (1.0 - EMA_DECAY) * weights
            return 0

        lax.fori_loop(0, rows // step, one_chunk, 0)
        start += rows
    copy[...] = new_master[...].astype(BF).reshape(copy.shape)


def partner(value, axis, flip):
    count = lax.axis_size(axis)
    return lax.ppermute(value, axis, [(i, i ^ flip) for i in range(count)])


def body(
    tokens, cotangent, qkv_weight, out_weight, up_weight, down_weight, norm_gain, norm_shift,
    lengths, prompt_src, prompt_len, codebook_section, adam_step, master, first_moment, second_moment, ema_weight,
):
    dp_index = lax.axis_index("dp")
    mp_index = lax.axis_index("mp")
    count = lax.axis_size("dp")
    outer = count // 4
    plane, outer_index = lax.rem(dp_index, 4), dp_index // 4
    place = jnp.stack([mp_index, plane % 2, plane // 2, plane, outer_index]).astype(jnp.int32)

    half_rows = PMAX // 2
    prompt_rows, low, low_half, meta, rows = pl.pallas_call(
        start_kernel,
        grid_spec=pltpu.PrefetchScalarGridSpec(
            num_scalar_prefetch=5, grid=(1,), in_specs=[HBM] * 4,
            out_specs=[whole((half_rows, D)), whole((TOK, D)), whole((TOK, HW)), pl.BlockSpec(memory_space=pltpu.SMEM), whole((8, D))],
            scratch_shapes=[pltpu.VMEM((half_rows, D), BF), pltpu.VMEM((TOK, D), BF), pltpu.VMEM((4, SECTIONS, D), F32), pltpu.SemaphoreType.DMA((6,))],
        ),
        out_shape=[shaped((half_rows, D), BF), shaped((TOK, D), BF), shaped((TOK, HW), BF), shaped((9,), jnp.int32), shaped((8, D), F32)],
        compiler_params=pltpu.CompilerParams(vmem_limit_bytes=60 << 20),
        cost_estimate=pl.CostEstimate(flops=1, bytes_accessed=1, transcendentals=0),
        name="start",
    )(place, lengths, prompt_src, prompt_len, codebook_section, tokens, cotangent, norm_gain, norm_shift)
    order = Order(meta)
    rows_from = [partner(prompt_rows, "dp", k) for k in (1, 2, 3)]
    low_x = partner(low_half, "dp", 1)
    normed, projected = simple(
        qkv_kernel, order, (tokens, rows, qkv_weight), [shaped((TOK, D), BF), shaped((3, TOK, HW), BF)], far=(0, 2),
        scratch=[pltpu.VMEM((TOK, D), BF), pltpu.VMEM((3, D, HW), BF), pltpu.SemaphoreType.DMA((4,))], name="qkv",
    )
    rows_from = lax.optimization_barrier((*rows_from, projected))[:3]
    relative = jnp.bitwise_xor(lax.rem(meta[SOURCE], 4), meta[PLANE])
    here = jnp.where(relative == 1, rows_from[0], jnp.where(relative == 2, rows_from[1], rows_from[2]))
    there = partner(here, "mp", 1)
    hidden_rows = HF // count
    split = hidden_rows if hidden_rows % 128 == 0 else 0
    low_x = partner(low_half, "dp", 1)
    rows_from = lax.optimization_barrier((*rows_from, low_half))[:3]
    here = jnp.where(relative == 1, rows_from[0], jnp.where(relative == 2, rows_from[1], rows_from[2]))
    there = partner(here, "mp", 1)
    (grad_act,) = simple(
        grad_act_kernel, order, (low, down_weight), [shaped((TOK, HF), F32)], far=(1,),
        scratch=[pltpu.VMEM((HF, D), BF), pltpu.SemaphoreType.DMA((4,))], name="grad_act",
    )
    halves = [shaped((TOK, D), BF)]
    half_specs = [whole((TOK, D))]

    def both(parts):
        return (*parts, *[partner(item, "mp", 1) for item in parts])

    normed_prompt, prompt_pair, attended_t, log_total, mixed, joined = simple(
        attend_kernel, order, (projected, here, there, qkv_weight, out_weight, low_half, low_x),
        [shaped((PMAX, D), BF), shaped((2, PMAX, HW), BF), shaped((HW, TOK), BF), shaped((HEADS, TOK), F32), *halves, shaped((2, TOK, HW), BF)],
        scratch=[pltpu.VMEM((KEYS, HW), BF), pltpu.VMEM((KEYS, HW), BF), pltpu.VMEM((HW, KEYS), BF),
            pltpu.VMEM((2, D, HW), BF), pltpu.VMEM((HW, D), BF), pltpu.SemaphoreType.DMA((3,))],
        far=(3, 4), name="attend",
    )
    mixed = both((mixed,))
    low_y = partner(joined, "dp", 2)
    low_x_swap = partner(lax.optimization_barrier((low_x, mixed[0]))[0], "mp", 1)
    pieces = 4 if split else 1
    act_shape = (TOK, HF // pieces)
    hidden, normed_second, *act, pre_low, second_part = simple(
        functools.partial(ffn_kernel, split), order, (tokens, *mixed, rows, up_weight, grad_act),
        [shaped((TOK, D), F32), shaped((TOK, D), BF)] + [shaped(act_shape, BF)] * pieces + [shaped((TOK, HF), BF), *halves],
        scratch=[pltpu.VMEM((TOK, HF), F32), pltpu.VMEM((pieces, TOK, HF // pieces), BF), pltpu.VMEM((TOK, D), BF), pltpu.VMEM((D, HF), BF), pltpu.SemaphoreType.DMA((HF // TILE + 1,))],
        far=(0, 4), name="ffn",
    )
    second = both((second_part,))

    if split:
        act_pieces = act
    else:
        cut = act[0].reshape(TOK, outer, 4, hidden_rows)
        act_pieces = [
            lax.dynamic_index_in_dim(cut, plane ^ k, 2, keepdims=False).reshape(TOK, HF // 4) for k in range(4)
        ]
    act_x = partner(jnp.stack([act_pieces[1], act_pieces[3]]), "dp", 1)
    act_y = partner(act_pieces[2], "dp", 2)

    up_rows = D // count
    up_half = [shaped((outer, 2, up_rows, D), BF)] * 2

    def up_product(axis, at):
        return simple(
            functools.partial(up_product_kernel, axis, at), order, (normed_second, pre_low), up_half,
            scratch=[pltpu.VMEM((outer, 2, 2, up_rows, D), BF)], name="up_product_" + axis,
        )

    up_away_x, up_kept_x = up_product("x", 0)
    up_got_x = partner(up_away_x, "dp", 1)
    low_y_swap = partner(lax.optimization_barrier((low_y, up_away_x))[0], "mp", 1)
    up_away_y, up_kept_y = up_product("y", D)
    up_got_y = partner(up_away_y, "dp", 2)

    local, sent, along, grad_hidden, hidden_low, tables_second = simple(
        attend_back_kernel, order,
        (*second, hidden, rows, low, out_weight, projected, prompt_pair, log_total),
        [shaped((3, KEYS, HW), BF), shaped((2, 2, PMAX, HW), BF), shaped((2, PMAX, HW), BF), shaped((TOK, D), F32), shaped((TOK, D), BF), shaped((2, D), F32)],
        scratch=[pltpu.VMEM((KEYS, HW), BF), pltpu.VMEM((KEYS, HW), BF), pltpu.VMEM((HW, KEYS), BF), pltpu.VMEM((TOK, HW), BF), pltpu.VMEM((HW, TOK), F32),
            pltpu.VMEM((HW, D), BF), pltpu.SemaphoreType.DMA((1,))],
        far=(5,), name="attend_back",
    )
    first_back = partner(sent, "dp", 1)
    (act_onward,) = simple(join_kernel, order, (act_x, act_y), [shaped(act_y.shape, BF)], name="join")
    act_far = partner(act_onward, "dp", 2)

    if split:
        down_in, down_spec = down_weight.reshape(outer, 4, hidden_rows, D), block((outer, None, hidden_rows, D), lambda t, m: (0, t, 0, 0))
    else:
        down_in, down_spec = down_weight, block((HF // 4, D), lambda t, m: (t, 0))
    ffn_part = call(
        functools.partial(down_kernel, split), order, (*act, down_in), [whole(act_shape)] * pieces + [down_spec],
        halves, half_specs, grid=(4,), scratch=[pltpu.VMEM((TOK, D), F32)], name="down",
    )
    ffn_both = both(ffn_part)

    half_outer = max(outer // 2, 1)
    lows = (act_pieces[0], act_x, act_y, act_far, low, low_x, low_y, low_x_swap, low_y_swap)
    piece_shape = (half_outer, hidden_rows, D)
    down_own, down_away = simple(
        down_product_kernel, order, lows, [shaped(piece_shape, F32), shaped(piece_shape, BF)],
        scratch=[pltpu.VMEM((half_outer, 2, hidden_rows, D), F32)], name="down_product",
    )

    def outer_step(own, away, bit, name):
        got = partner(away, "dp", 4 << bit)
        if own.shape[0] == 1:
            return lambda: [own, got]

        def later():
            left = own.shape[0] // 2
            shape = (left,) + own.shape[1:]
            next_own, next_away = simple(
                functools.partial(halve_kernel, bit + 1), order, (own, got), [shaped(shape, F32), shaped(shape, BF)],
                scratch=[pltpu.VMEM((left, 2) + own.shape[1:], F32)], name=name + "_halve",
            )
            return outer_step(next_own, next_away, bit + 1, name)

        return later

    def run_out(state):
        while callable(state):
            state = state()
        return state

    down_later = outer_step(down_own, down_away, 0, "down")
    (onward,) = simple(pass_on_kernel, order, (along, first_back), [shaped(along.shape, BF)], name="pass_on")
    second_back = partner(onward, "dp", 2)

    def second_stage(kept_x, got_x, kept_y, got_y, name):
        _, _, rows, wide = kept_x.shape
        tall = kept_y.shape[-1]
        outs = [shaped((outer, rows, wide), BF)] * 2 + [shaped((outer, rows, tall), BF)] * 2
        away_x, own_x, away_y, own_y = simple(
            second_kernel, order, (kept_x, got_x, kept_y, got_y), outs,
            scratch=[pltpu.VMEM(kept_x.shape, F32), pltpu.VMEM(kept_y.shape, F32)], name=name + "_second",
        )
        return own_x, partner(away_x, "dp", 2), own_y, partner(away_y, "dp", 1)

    def third_stage(own_x, got_x, own_y, got_y, name, direct=False):
        rows = own_x.shape[1]
        columns = own_x.shape[2] + own_y.shape[2]
        if direct and outer == 4:
            shape = (1, rows, columns)
            own, *away = simple(
                direct_kernel, order, (own_x, got_x, own_y, got_y), [shaped(shape, F32)] + [shaped(shape, BF)] * (outer - 1),
                scratch=[pltpu.VMEM((outer, rows, columns), F32)], name=name + "_direct",
            )
            return [own] + [partner(item, "dp", 4 * (m + 1)) for m, item in enumerate(away)]
        shape = (half_outer, rows, columns)
        own, away = simple(
            third_kernel, order, (own_x, got_x, own_y, got_y), [shaped(shape, F32), shaped(shape, BF)],
            scratch=[pltpu.VMEM((half_outer, 2, rows, columns), F32)], name=name + "_third",
        )
        return outer_step(own, away, 0, name)

    def advance(state):
        return state() if callable(state) else state

    down_later = advance(down_later)
    up_later = second_stage(up_kept_x, up_got_x, up_kept_y, up_got_y, "up")

    qkv_rows = 3 * D // count
    qkv_half = [shaped((outer, 2, qkv_rows + 8, HW // 2), BF), shaped((outer, 2, qkv_rows, HW // 2), BF)]

    def qkv_product(axis, at):
        return simple(
            functools.partial(qkv_product_kernel, axis, at), order, (normed, normed_prompt, local), qkv_half,
            scratch=[pltpu.VMEM((D, KEYS), BF), pltpu.VMEM((3 * D, HW // 2), BF)], name="qkv_product_" + axis,
        )

    qkv_away_x, qkv_kept_x = qkv_product("x", 0)
    qkv_got_x = partner(qkv_away_x, "dp", 1)
    qkv_away_y, qkv_kept_y = qkv_product("y", HW // 2)
    qkv_got_y = partner(qkv_away_y, "dp", 2)
    (down_rows, down_squares) = simple(
        functools.partial(finish_kernel, (2,)), order, run_out(down_later),
        [shaped((hidden_rows * D // 128, 128), F32), shaped((8, 128), F32)], name="finish_down",
    )
    up_later = third_stage(*up_later, "up")

    normed_part = call(
        grad_normed_kernel, order, (local, first_back, second_back, qkv_weight),
        [block((1, KEYS, HW), lambda c, m: (c, 0, 0)), whole(first_back.shape), whole(second_back.shape), block((1, D, HW), lambda c, m: (c, 0, 0))],
        halves, half_specs,
        grid=(3,), scratch=[pltpu.VMEM((PMAX, HW), BF), pltpu.VMEM((TOK, D), F32)], name="grad_normed",
    )
    normed_both = both(normed_part)
    (block_out,) = simple(block_out_kernel, order, (hidden, *ffn_both), [shaped((TOK, D), BF)], name="block_out")
    input_grad, tables_first = simple(
        input_grad_kernel, order, (*normed_both, tokens, rows, grad_hidden),
        [shaped((TOK, D), BF), shaped((2, D), F32)], name="input_grad",
    )


    out_rows = HW // count
    selector = (jnp.arange(SECTIONS) == codebook_section[0]).astype(F32)
    tables = jnp.stack([tables_first, tables_second])
    tables = lax.dynamic_slice_in_dim(tables, mp_index * HW, HW, 2)
    spread = selector[None, None, :, None] * jnp.transpose(tables, (1, 0, 2))[:, :, None, :]
    entries = 2 * SECTIONS * HW // count
    spread = jnp.transpose(spread.reshape(2, count, entries), (1, 0, 2)).reshape(count, 2 * entries // 128, 128).astype(BF)
    spread = jnp.pad(spread, ((0, 0), (0, out_rows - 2 * entries // 128), (0, 0)))
    wide, tall = HW + 128, HW
    away_x, kept_x, away_y, kept_y = simple(
        out_product_kernel, order, (attended_t, hidden_low, spread),
        [shaped((outer, 2, out_rows, wide), BF)] * 2 + [shaped((outer, 2, out_rows, tall), BF)] * 2,
        scratch=[pltpu.VMEM((outer, 2, 2, out_rows, wide), BF), pltpu.VMEM((outer, 2, 2, out_rows, tall), BF)],
        name="out_product",
    )
    got_x, got_y = partner(away_x, "dp", 1), partner(away_y, "dp", 2)
    up_later = advance(up_later)
    qkv_later = second_stage(qkv_kept_x, qkv_got_x, qkv_kept_y, qkv_got_y, "qkv")
    out_later = second_stage(kept_x, got_x, kept_y, got_y, "out")
    (up_lines, up_squares) = simple(
        functools.partial(finish_kernel, (2,)), order, run_out(up_later),
        [shaped((up_rows * HF // 128, 128), F32), shaped((8, 128), F32)], name="finish_up",
    )
    qkv_later = third_stage(*qkv_later, "qkv")
    out_later = third_stage(*out_later, "out", direct=True)
    qkv_later = advance(qkv_later)

    flat = master.shape[1]
    out_terms = run_out(out_later)
    (qkv_lines, out_lines, table_lines, squares) = simple(
        functools.partial(finish_last_kernel, 2), order, (*run_out(qkv_later), *out_terms, up_squares, down_squares),
        [shaped((qkv_rows * HW // 128, 128), F32), shaped((out_rows * D // 128, 128), F32), shaped((max(2 * entries // 128, 1), 128), F32), shaped((8, 128), F32)],
        name="finish",
    )
    squares = squares + partner(squares, "mp", 1)
    step = 1
    while step < count:
        squares = squares + partner(squares, "dp", step)
        step *= 2
    grad_norm = jnp.sqrt(squares[0, :1])
    step_count = adam_step[0].astype(F32)
    fixes = jnp.stack([1.0 / (1.0 - jnp.power(BETA_ONE, step_count)), 1.0 / (1.0 - jnp.power(BETA_TWO, step_count))]).reshape(1, 2)
    lines = flat // 128
    rates = [D ** (-0.5), OUT_FAN ** (-0.5), D ** (-0.5), FF ** (-0.5), 0.2]
    flats = [item.reshape(lines, 128) for item in (master, first_moment, second_moment, ema_weight)]
    new_first, new_second, new_master, copy, new_ema = simple(
        functools.partial(adam_kernel, rates), order, (squares, fixes, qkv_lines, out_lines, up_lines, down_rows, table_lines, *flats),
        [shaped((lines, 128), F32)] * 3 + [shaped((1, flat), BF), shaped((lines, 128), F32)], name="adam", vmem=40,
    )
    return (
        block_out,
        input_grad,
        grad_norm,
        new_first.reshape(1, flat),
        new_second.reshape(1, flat),
        new_master.reshape(1, flat),
        copy,
        new_ema.reshape(1, flat),
    )


def solution(mesh):
    placed = (
        P("dp", None), P("dp", None), P(None, None, "mp"), P("mp", None), P(None, "mp"), P("mp", None), P(), P(),
        P("dp"), P("dp"), P("dp"), P("dp"), P(),
        P("mp", "dp"), P("mp", "dp"), P("mp", "dp"), P("mp", "dp"),
    )
    flat = P("mp", "dp")
    return jax.shard_map(
        body, mesh=mesh, in_specs=placed,
        out_specs=(P("dp", None), P("dp", None), P(), flat, flat, flat, flat, flat),
        check_vma=False,
    )
```

```python
import functools

import jax
import jax.numpy as jnp
from jax import lax
from jax.experimental import pallas as pl
from jax.experimental.pallas import tpu as pltpu
from jax.sharding import PartitionSpec as P

D = 1024
HDIM = 64
FF = 4096
SECTIONS = 8
TOK = 384
PMAX = 96
KEYS = TOK + PMAX
OUT_FAN = 2
HW = D // 2
HF = FF // 2
HEADS = HW // HDIM
CLIP_NORM = 1.0
BETA_ONE = 0.5
BETA_TWO = 0.5
WEIGHT_DECAY = 0.1
EMA_DECAY = 0.75

BF = jnp.bfloat16
F32 = jnp.float32
MP, PX, PY, PLANE, OUTER, LENGTH, SECTION = range(7)


def shaped(shape, dtype):
    return jax.ShapeDtypeStruct(shape, dtype)


def dot_nn(a, b):
    return lax.dot_general(a, b, (((1,), (0,)), ((), ())), preferred_element_type=F32)


def dot_nt(a, b):
    return lax.dot_general(a, b, (((1,), (1,)), ((), ())), preferred_element_type=F32)


def dot_tn(a, b):
    return lax.dot_general(a, b, (((0,), (0,)), ((), ())), preferred_element_type=F32)


def block(shape, index):
    return pl.BlockSpec(shape, index)


def whole(shape):
    rank = len(shape)
    return pl.BlockSpec(shape, lambda *_: (0,) * rank)


class Order:
    def __init__(self, meta):
        self.meta = meta
        self.after = []


HBM = pl.BlockSpec(memory_space=pltpu.HBM)


def fetch(source, target, sem):
    copy = pltpu.make_async_copy(source, target, sem)
    copy.start()
    return copy


def call(kernel, order, inputs, in_specs, outs, out_specs, grid=(1,), scratch=(), name=None, vmem=20):
    after, count = list(order.after), len(inputs)

    def run(meta, *refs):
        kernel(meta, *refs[:count], *refs[count + len(after) :])

    found = pl.pallas_call(
        run,
        grid_spec=pltpu.PrefetchScalarGridSpec(
            num_scalar_prefetch=1, grid=grid, in_specs=list(in_specs) + [HBM] * len(after),
            out_specs=out_specs, scratch_shapes=scratch,
        ),
        out_shape=outs,
        compiler_params=pltpu.CompilerParams(vmem_limit_bytes=vmem << 20),
        cost_estimate=pl.CostEstimate(flops=1, bytes_accessed=1, transcendentals=0),
        name=name,
    )(order.meta, *inputs, *after)
    order.after = [min(found, key=lambda item: item.size)]
    return found


def simple(kernel, order, inputs, outs, far=(), far_out=(), **kw):
    return call(
        kernel, order, inputs,
        [HBM if k in far else pl.BlockSpec(memory_space=pltpu.SMEM) if a.shape == (1,) else whole(a.shape) for k, a in enumerate(inputs)],
        outs, [HBM if k in far_out else whole(o.shape) for k, o in enumerate(outs)], **kw
    )


def unit_rows(values):
    centred = values - jnp.mean(values, axis=-1, keepdims=True)
    scale = lax.rsqrt(jnp.mean(centred * centred, axis=-1, keepdims=True) + 1e-05)
    return centred * scale, scale


def norm_back(grad, gain_row, unit, scale):
    e = gain_row * grad
    return scale * (e - jnp.mean(e, axis=-1, keepdims=True) - unit * jnp.mean(e * unit, axis=-1, keepdims=True))


def row_of(rows, which):
    return rows[which : which + 1, :]


def valid_rows(meta):
    return lax.broadcasted_iota(jnp.int32, (TOK, 1), 0) < meta[LENGTH]


def keys_ok(meta, prompt):
    at = lax.broadcasted_iota(jnp.int32, (KEYS, 1), 0)
    return at < jnp.where(at < TOK, meta[LENGTH], TOK + prompt[0])


def summed(refs):
    here, there = refs
    return here[...].astype(F32) + there[...].astype(F32)


def start_kernel(
    tokens, cotangent, gain, shift, lengths, section,
    out, low, half, meta, rows, some, whole_low, tables, read, sems,
):
    scalars = [fetch(item, read.at[k], sems.at[6 + k]) for k, item in enumerate((lengths, section))]
    copies = [fetch(tokens.at[pl.ds(0, PMAX), :], some, sems.at[0])]
    for k, (table, norm) in enumerate(((gain, 0), (shift, 0), (gain, 1), (shift, 1))):
        copies.append(fetch(table.at[norm], tables.at[k], sems.at[1 + k]))
    late = fetch(cotangent, whole_low, sems.at[5])
    dp_index, mp_index = lax.axis_index("dp"), lax.axis_index("mp")
    plane = jnp.bitwise_and(dp_index, 3)
    meta[MP] = mp_index
    meta[PX] = jnp.bitwise_and(plane, 1)
    meta[PY] = lax.shift_right_logical(plane, 1)
    meta[PLANE] = plane
    meta[OUTER] = lax.shift_right_logical(dp_index, 2)
    for copy in scalars:
        copy.wait()
    valid_count = read[0, 0]
    meta[LENGTH] = valid_count
    meta[SECTION] = read[1, 0]
    chosen = read[1, 0]
    for copy in copies:
        copy.wait()
    for k in range(4):
        rows[k : k + 1, :] = tables[k, pl.ds(chosen, 1), :]
    rows[4:, :] = jnp.zeros((4, D), F32)
    unit, _ = unit_rows(some[...].astype(F32))
    out[...] = (row_of(rows, 0) * unit + row_of(rows, 1)).astype(BF)
    late.wait()
    valid = lax.broadcasted_iota(jnp.int32, (TOK, 1), 0) < valid_count
    kept = jnp.where(valid, whole_low[...], jnp.zeros((), BF))
    low[...] = kept

    @pl.when(mp_index == 0)
    def _():
        half[...] = kept[:, :HW]

    @pl.when(mp_index == 1)
    def _():
        half[...] = kept[:, HW:]


def qkv_kernel(meta, tokens, rows, qkv, normed, projected, frames, weights, sems):
    first = fetch(tokens, frames, sems.at[3])
    copies = [fetch(qkv.at[c], weights.at[c], sems.at[c]) for c in range(3)]
    first.wait()
    unit, _ = unit_rows(frames[...].astype(F32))
    normed[...] = (row_of(rows, 0) * unit + row_of(rows, 1)).astype(BF)
    for c in range(3):
        copies[c].wait()
        projected[c] = dot_nn(normed[...], weights[c]).astype(BF)


def grad_act_kernel(meta, low, down, out, weights, sems):
    size = HF // 4
    copies = [fetch(down.at[pl.ds(t * size, size), :], weights.at[pl.ds(t * size, size), :], sems.at[t]) for t in range(4)]
    for t in range(4):
        copies[t].wait()
        out[:, t * size : (t + 1) * size] = dot_nt(low[...], weights[t * size : (t + 1) * size, :]).astype(BF)


def attend_kernel(
    meta, projected, rows_x, rows_y, rows_far, qkv, out_weight, low_half, low_x, source, prompt,
    normed_prompt, prompt_pair, attended_t, log_total, part, joined, keys, values, values_t, weights, out_w, sems,
):
    copies = [fetch(qkv.at[c], weights.at[c - 1], sems.at[c - 1]) for c in (1, 2)]
    last = fetch(out_weight, out_w, sems.at[2])
    joined[0] = low_half[...]
    joined[1] = low_x[...]
    keys[:TOK] = projected[1]
    values[:TOK] = projected[2]
    relative = jnp.bitwise_xor(jnp.bitwise_and(source[0], 3), meta[PLANE])
    for k, rows in ((1, rows_x), (2, rows_y), (3, rows_far)):

        @pl.when(relative == k)
        def _(rows=rows):
            normed_prompt[...] = rows[...]

    rows = normed_prompt[...]
    copies[0].wait()
    pair_k = dot_nn(rows, weights[0]).astype(BF)
    copies[1].wait()
    pair_v = dot_nn(rows, weights[1]).astype(BF)
    prompt_pair[0] = pair_k
    prompt_pair[1] = pair_v
    keys[TOK:] = pair_k
    values[TOK:] = pair_v
    values_t[...] = values[...].T
    counted = keys_ok(meta, prompt)
    lane = lax.broadcasted_iota(jnp.int32, (1, 2 * HDIM), 1)
    for head in range(HEADS):
        at = (head // 2) * 2 * HDIM
        mine = jnp.where((lane // HDIM) == head % 2, HDIM ** (-0.5), 0.0).astype(BF)
        query = projected[0, :, at : at + 2 * HDIM] * mine
        scores = jnp.where(counted, dot_nt(keys[:, at : at + 2 * HDIM], query), -1e30)
        top = jnp.max(scores, axis=0, keepdims=True)
        grown = jnp.exp(scores - top)
        total = jnp.sum(grown, axis=0, keepdims=True)
        probability = (grown * (1.0 / total)).astype(BF)
        rows_at = slice(head * HDIM, (head + 1) * HDIM)
        attended_t[rows_at, :] = dot_nn(values_t[rows_at, :], probability).astype(BF)
        log_total[head : head + 1, :] = top + jnp.log(total)
    last.wait()
    part[...] = dot_tn(attended_t[...], out_w[...]).astype(BF)


TILE = 256


ERFC = (0.235325614, 0.0913858287, 0.649566092, -0.635408842, 0.886669787, -0.227538481)


def gelu_parts(values):
    decay = jnp.exp(-0.5 * values * values)
    t = 1.0 / (1.0 + (0.39 * 0.5**0.5) * jnp.abs(values))
    tail = 0.5 * ERFC[-1]
    for factor in ERFC[-2::-1]:
        tail = tail * t + 0.5 * factor
    tail = tail * t * decay
    cdf = jnp.where(values < 0.0, tail, 1.0 - tail)
    return cdf, cdf + values * (decay * (0.5 / jnp.pi) ** 0.5)


def ffn_kernel(split, meta, tokens, here, there, rows, up, grad_act, hidden, normed, *refs):
    *act, pre_low, part, pre, held, frames, weights, sems = refs
    steps = HF // TILE
    first = fetch(tokens, frames, sems.at[steps])
    copies = [fetch(up.at[:, pl.ds(t * TILE, TILE)], weights.at[:, pl.ds(t * TILE, TILE)], sems.at[t]) for t in range(steps)]
    first.wait()
    state = frames[...].astype(F32) + summed((here, there))
    hidden[...] = state
    unit, _ = unit_rows(state)
    normed[...] = (row_of(rows, 2) * unit + row_of(rows, 3)).astype(BF)
    for t in range(steps):
        copies[t].wait()
        at = slice(t * TILE, (t + 1) * TILE)
        pre[:, at] = dot_nn(normed[...], weights[:, at])
    across = split or 128

    def block_of_rows(r, _):
        some = pl.ds(pl.multiple_of(r * 64, 64), 64)
        for t in range(HF // across):
            at = slice(t * across, (t + 1) * across)
            values = pre[some, at]
            cdf, slope = gelu_parts(values)
            activated = (values * cdf).astype(BF)
            if split:
                held[t % 4, some, (t // 4) * split : (t // 4 + 1) * split] = activated
            else:
                act[0][some, at] = activated
            pre_low[some, at] = (grad_act[some, at].astype(F32) * slope).astype(BF)
        return 0

    lax.fori_loop(0, TOK // 64, block_of_rows, 0)
    part[...] = dot_nt(pre_low[...], weights[...]).astype(BF)
    if split:
        for k, out in enumerate((act[0], act[1].at[0], act[2], act[1].at[1])):
            out[...] = held[jnp.bitwise_xor(meta[PLANE], k)]


def join_kernel(meta, act_x, mine, out):
    out[0] = mine[...]
    out[1] = act_x[1]


def down_kernel(split, meta, *refs):
    *act, down, part, total = refs
    step = pl.program_id(0)

    @pl.when(step == 0)
    def _():
        total[...] = jnp.zeros_like(total)

    if split:
        rows = down[...].reshape(HF // 4, D)
        piece = jnp.bitwise_xor(step, meta[PLANE])
        for k, value in enumerate((act[0], act[1].at[0], act[2], act[1].at[1])):

            @pl.when(piece == k)
            def _(value=value):
                total[...] += dot_nn(value[...], rows)

    else:
        total[...] += dot_nn(act[0][:, pl.ds(pl.multiple_of(step * (HF // 4), HF // 4), HF // 4)], down[...])

    @pl.when(step == pl.num_programs(0) - 1)
    def _():
        part[...] = total[...].astype(BF)


def block_out_kernel(meta, hidden, here, there, out):
    out[...] = (hidden[...] + summed((here, there))).astype(BF)


def attend_back_kernel(
    meta, here, there, hidden, rows, low, out_weight, projected, prompt_pair, log_total, source, prompt,
    local, sent, along, grad_hidden, hidden_low, tables, keys, values, keys_t, grads, query_t, out_w, sems,
):
    last = fetch(out_weight, out_w, sems.at[0])
    back = summed((here, there))
    unit, scale = unit_rows(hidden[...])
    full = low[...].astype(F32) + norm_back(back, row_of(rows, 2), unit, scale)
    grad_hidden[...] = full
    tables[0:1, :] = jnp.sum(back * unit, axis=0, keepdims=True)
    tables[1:2, :] = jnp.sum(back, axis=0, keepdims=True)
    rounded = full.astype(BF)
    hidden_low[...] = rounded
    last.wait()
    grads[...] = dot_nt(rounded, out_w[...]).astype(BF)
    keys[:TOK] = projected[1]
    keys[TOK:] = prompt_pair[0]
    values[:TOK] = projected[2]
    values[TOK:] = prompt_pair[1]
    keys_t[...] = keys[...].T
    counted = keys_ok(meta, prompt)
    lane = lax.broadcasted_iota(jnp.int32, (1, 2 * HDIM), 1)
    left = lane < HDIM
    for pair in range(HEADS // 2):
        at = pair * 2 * HDIM
        span = slice(at, at + 2 * HDIM)
        key_pair, value_pair = keys[:, span], values[:, span]
        query_pair = projected[0, :, span] * jnp.asarray(HDIM ** (-0.5), BF)
        grad_pair = grads[:, span]
        found = []
        for head in (2 * pair, 2 * pair + 1):
            mine = ((lane // HDIM) == head % 2).astype(BF)
            scores = jnp.where(counted, dot_nt(key_pair, query_pair * mine), -1e30)
            probability = jnp.exp(scores - log_total[head : head + 1, :])
            grad_prob = dot_nt(value_pair, grad_pair * mine)
            centre = jnp.sum(probability * grad_prob, axis=0, keepdims=True)
            grad_scores = (probability * (grad_prob - centre)).astype(BF)
            rows_at = slice(head * HDIM, (head + 1) * HDIM)
            query_t[rows_at, :] = dot_nn(keys_t[rows_at, :], grad_scores) * HDIM ** (-0.5)
            found.append((dot_nn(grad_scores, query_pair), dot_nn(probability.astype(BF), grad_pair)))
        local[1, :, span] = jnp.where(left, found[0][0], found[1][0]).astype(BF)
        local[2, :, span] = jnp.where(left, found[0][1], found[1][1]).astype(BF)
    local[0, :TOK, :] = query_t[...].T.astype(BF)
    local[0, TOK:, :] = jnp.zeros((PMAX, HW), BF)
    relative = jnp.bitwise_xor(jnp.bitwise_and(source[0], 3), meta[PLANE])
    for c in range(2):
        prompt = local[1 + c, TOK:, :]
        for j in range(2):
            sent[j, c] = jnp.where(relative == 1 + 2 * j, prompt, jnp.zeros((), BF))
        along[c] = jnp.where(relative == 2, prompt, jnp.zeros((), BF))


def pass_on_kernel(meta, along, got, out):
    out[...] = (along[...].astype(F32) + got[1].astype(F32)).astype(BF)


def grad_normed_kernel(meta, local, first, second, qkv, part, returned_low, total):
    c = pl.program_id(0)

    @pl.when(c == 0)
    def _():
        total[...] = jnp.zeros_like(total)

    total[...] += dot_nt(local[0, :TOK, :], qkv[0])

    @pl.when(c > 0)
    def _():
        at = c - 1
        returned = first[0, at].astype(F32) + second[at].astype(F32)
        returned_low[...] = returned.astype(BF)
        total[:PMAX, :] += dot_nt(returned_low[...], qkv[0])

    @pl.when(c == 2)
    def _():
        part[...] = total[...].astype(BF)


def input_grad_kernel(meta, here, there, tokens, rows, grad_hidden, out, tables):
    back = summed((here, there))
    unit, scale = unit_rows(tokens[...].astype(F32))
    out[...] = (grad_hidden[...] + norm_back(back, row_of(rows, 0), unit, scale)).astype(BF)
    tables[0:1, :] = jnp.sum(back * unit, axis=0, keepdims=True)
    tables[1:2, :] = jnp.sum(back, axis=0, keepdims=True)


def part_out(out, at, whole_ref, axis, side):
    if axis == "x":
        out[..., at] = whole_ref[:, :, side]
    else:
        out[..., at] = whole_ref[:, side]


def pick(held, axis, side):
    return held[:, :, side] if axis == "x" else held[:, side]


def up_product_kernel(axis, at, meta, normed, pre_low, away, kept, held):
    held[...] = dot_tn(normed[...], pre_low[:, at : at + D]).astype(BF).reshape(held.shape)
    side = meta[PX] if axis == "x" else meta[PY]
    away[...] = pick(held, axis, 1 - side)
    kept[...] = pick(held, axis, side)


def down_product_kernel(meta, mine, act_x, act_y, low, low_x, low_y, swap_x, swap_y, own, away, held):
    here = pl.ds(pl.multiple_of(meta[MP] * HW, HW), HW)
    there = pl.ds(pl.multiple_of((1 - meta[MP]) * HW, HW), HW)
    for at, x, y in ((here, low_x, low_y), (there, swap_x, swap_y)):
        found = dot_tn(mine[...], low[:, at])
        found += dot_tn(act_x[0], x[...])
        found += dot_tn(act_y[0], y[0])
        found += dot_tn(act_y[1], y[1])
        held[:, :, :, at] = found.reshape(held.shape[:3] + (HW,))
    side = lax.rem(meta[OUTER], 2)
    own[...] = held[:, side]
    away[...] = held[:, 1 - side].astype(BF)


def qkv_product_kernel(axis, at, meta, normed, normed_prompt, local, away, kept, normed_t, held):
    normed_t[:, :TOK] = normed[...].T
    normed_t[:, TOK:] = normed_prompt[...].T
    outer, _, rows, columns = kept.shape
    for c in range(3):
        held[c * D : (c + 1) * D, :] = dot_nn(normed_t[...], local[c, :, at : at + columns]).astype(BF)
    parts = held.reshape(outer, 2, 2, rows, columns)
    side = meta[PX] if axis == "x" else meta[PY]
    away[:, :, :rows] = pick(parts, axis, 1 - side)
    kept[...] = pick(parts, axis, side)


def tables_of(meta, block_index, first, second):
    ref = (first, second)[block_index // SECTIONS]
    mine = ref[:, pl.ds(pl.multiple_of(meta[MP] * HW, HW), HW)]
    mine = jnp.where(meta[SECTION] == block_index % SECTIONS, mine, 0.0)
    return jnp.concatenate([mine[k : k + 1, 128 * c : 128 * (c + 1)] for k in range(2) for c in range(HW // 128)], axis=0)


def out_product_kernel(meta, attended_t, hidden_low, first, second, *refs):
    *spread, away_x, kept_x, away_y, kept_y, held_x, held_y = refs
    out_product(meta, attended_t, hidden_low, first, second, spread, away_x, kept_x, away_y, kept_y, held_x, held_y)


def out_product(meta, attended_t, hidden_low, first, second, spread, away_x, kept_x, away_y, kept_y, held_x, held_y):
    found = dot_nn(attended_t[...], hidden_low[...]).astype(BF)
    rows = held_x.shape[3]
    held_x[..., :HW] = found[:, :HW].reshape(held_x.shape[:3] + (rows, HW))
    if spread:
        held_x[..., HW:] = spread[0][...].reshape(held_x.shape[:3] + (rows, 128))
    else:
        for k in range(4 * held_x.shape[0]):
            entries = tables_of(meta, k, first, second)
            entries = jnp.concatenate([entries, jnp.zeros((rows - entries.shape[0], 128), F32)], axis=0)
            held_x[k // 4, (k // 2) % 2, k % 2, :, HW:] = entries.astype(BF)
    held_y[...] = found[:, HW:].reshape(held_y.shape)
    away_x[...] = held_x[:, :, 1 - meta[PX]]
    kept_x[...] = held_x[:, :, meta[PX]]
    away_y[...] = held_y[:, 1 - meta[PY]]
    kept_y[...] = held_y[:, meta[PY]]


def second_kernel(meta, kept_x, got_x, kept_y, got_y, away_x, own_x, away_y, own_y, held_x, held_y):
    rows = kept_x.shape[2]
    held_x[...] = kept_x[...].astype(F32) + got_x[:, :, :rows].astype(F32)
    held_y[...] = kept_y[...].astype(F32) + got_y[:, :, :rows].astype(F32)
    away_x[...] = held_x[:, 1 - meta[PY]].astype(BF)
    own_x[...] = held_x[:, meta[PY]].astype(BF)
    away_y[...] = held_y[:, 1 - meta[PX]].astype(BF)
    own_y[...] = held_y[:, meta[PX]].astype(BF)


def third_kernel(meta, kept_x, got_x, kept_y, got_y, own, away, held):
    left = kept_x.shape[-1]
    shape = held.shape[:2] + kept_x.shape[1:]
    held[..., :left] = (kept_x[...].astype(F32) + got_x[...].astype(F32)).reshape(shape)
    shape = held.shape[:2] + kept_y.shape[1:]
    held[..., left:] = (kept_y[...].astype(F32) + got_y[...].astype(F32)).reshape(shape)
    side = lax.rem(meta[OUTER], 2)
    own[...] = held[:, side]
    away[...] = held[:, 1 - side].astype(BF)


def direct_kernel(meta, kept_x, got_x, kept_y, got_y, own, *refs):
    *away, held = refs
    left = kept_x.shape[-1]
    held[..., :left] = kept_x[...].astype(F32) + got_x[...].astype(F32)
    held[..., left:] = kept_y[...].astype(F32) + got_y[...].astype(F32)
    own[0] = held[meta[OUTER]]
    for m, out in enumerate(away):
        out[0] = held[jnp.bitwise_xor(meta[OUTER], m + 1)].astype(BF)


def halve_kernel(bit, meta, kept, got, own, away, held):
    held[...] = (kept[...] + got[...].astype(F32)).reshape(held.shape)
    side = lax.rem(lax.shift_right_logical(meta[OUTER], bit), 2)
    own[...] = held[:, side]
    away[...] = held[:, 1 - side].astype(BF)


def to_rows(out, at, value):
    rows, columns = value.shape
    across = columns // 128
    for j in range(across):
        piece = value[:, 128 * j : 128 * (j + 1)]
        if across == 1:
            out[at : at + rows, :] = piece
        else:
            out[pl.ds(at + j, rows, stride=across), :] = piece


def total_of(terms):
    value = terms[0][0]
    for got in terms[1:]:
        value = value + got[0].astype(F32)
    return value


def square_sum(values):
    total = jnp.zeros((1, 128), F32)
    for value in values:
        line = jnp.sum(value * value, axis=0, keepdims=True)
        for j in range(value.shape[1] // 128):
            total = total + line[:, 128 * j : 128 * (j + 1)]
    return jnp.sum(total, axis=1, keepdims=True)


def finish_kernel(meta, *refs):
    *ins, out, squares = refs
    value = total_of(ins)
    to_rows(out, 0, value)
    squares[...] = jnp.broadcast_to(square_sum([value]), squares.shape)


def finish_last_kernel(first, meta, *refs):
    *ins, up_squares, down_squares, qkv_out, out_out, table_out, squares = refs
    value = total_of(ins[:first])
    to_rows(qkv_out, 0, value)
    both = total_of(ins[first:])
    tables = both[:, HW : HW + 128]
    third = jnp.concatenate([both[:, :HW], both[:, HW + 128 :]], axis=1)
    to_rows(out_out, 0, third)
    table_out[...] = tables[: table_out.shape[0], :]
    squares[...] = square_sum([value, third, tables]) + up_squares[...] + down_squares[...]


def adam_kernel(rates, meta, squares, fixes, *refs):
    pieces, (master, first, second, ema, new_first, new_second, new_master, copy, new_ema, norm) = refs[: len(rates)], refs[len(rates) :]
    norm[...] = jnp.sqrt(squares[0:1, 0:1])
    clip = jnp.minimum(1.0, CLIP_NORM / (norm[...] + 1e-06))
    one, two = fixes[0:1, 0:1], fixes[0:1, 1:2]
    start = 0
    for piece, rate in zip(pieces, rates):
        rows = piece.shape[0]
        step = next(n for n in (256, 128, 64, 32, 16, 8, 4, 2, 1) if rows % n == 0)

        def one_chunk(k, _, piece=piece, rate=rate, start=start, step=step):
            at = pl.ds(start + k * step, step)
            clipped = clip * piece[pl.ds(k * step, step), :]
            moment = BETA_ONE * first[at, :] + (1.0 - BETA_ONE) * clipped
            square = BETA_TWO * second[at, :] + (1.0 - BETA_TWO) * clipped * clipped
            new_first[at, :] = moment
            new_second[at, :] = square
            update = (moment * one) / (jnp.sqrt(square * two) + 1e-08)
            old = master[at, :]
            weights = old - rate * (update + WEIGHT_DECAY * old)
            new_master[at, :] = weights
            new_ema[at, :] = EMA_DECAY * ema[at, :] + (1.0 - EMA_DECAY) * weights
            return 0

        lax.fori_loop(0, rows // step, one_chunk, 0)
        start += rows
    copy[...] = new_master[...].astype(BF).reshape(copy.shape)


def partner(value, axis, flip):
    count = lax.axis_size(axis)
    return lax.ppermute(value, axis, [(i, i ^ flip) for i in range(count)])


def body(
    tokens, cotangent, qkv_weight, out_weight, up_weight, down_weight, norm_gain, norm_shift,
    lengths, prompt_src, prompt_len, codebook_section, adam_step, master, first_moment, second_moment, ema_weight,
):
    count = lax.axis_size("dp")
    outer = count // 4

    prompt_rows, low, low_half, meta, rows = pl.pallas_call(
        start_kernel,
        in_specs=[HBM] * 6,
        out_specs=[pl.BlockSpec(memory_space=pltpu.VMEM)] * 3 + [pl.BlockSpec(memory_space=pltpu.SMEM), pl.BlockSpec(memory_space=pltpu.VMEM)],
        scratch_shapes=[
            pltpu.VMEM((PMAX, D), BF), pltpu.VMEM((TOK, D), BF), pltpu.VMEM((4, SECTIONS, D), F32),
            pltpu.SMEM((2, 1), jnp.int32), pltpu.SemaphoreType.DMA((8,)),
        ],
        out_shape=[shaped((PMAX, D), BF), shaped((TOK, D), BF), shaped((TOK, HW), BF), shaped((7,), jnp.int32), shaped((8, D), F32)],
        compiler_params=pltpu.CompilerParams(vmem_limit_bytes=60 << 20),
        cost_estimate=pl.CostEstimate(flops=1, bytes_accessed=1, transcendentals=0),
        name="start",
    )(tokens, cotangent, norm_gain, norm_shift, lengths, codebook_section)
    order = Order(meta)
    plane, mp_index = meta[PLANE], meta[MP]
    rows_from = [partner(prompt_rows, "dp", k) for k in (1, 2, 3)]
    low_x = partner(low_half, "dp", 1)
    normed, projected = simple(
        qkv_kernel, order, (tokens, rows, qkv_weight), [shaped((TOK, D), BF), shaped((3, TOK, HW), BF)], far=(0, 2),
        scratch=[pltpu.VMEM((TOK, D), BF), pltpu.VMEM((3, D, HW), BF), pltpu.SemaphoreType.DMA((4,))], name="qkv",
    )
    hidden_rows = HF // count
    split = hidden_rows if hidden_rows % 128 == 0 else 0
    (grad_act,) = simple(
        grad_act_kernel, order, (low, down_weight), [shaped((TOK, HF), BF)], far=(1,),
        scratch=[pltpu.VMEM((HF, D), BF), pltpu.SemaphoreType.DMA((4,))], name="grad_act",
    )
    halves = [shaped((TOK, D), BF)]
    half_specs = [whole((TOK, D))]

    def both(parts):
        return (*parts, *[partner(item, "mp", 1) for item in parts])

    normed_prompt, prompt_pair, attended_t, log_total, mixed, joined = simple(
        attend_kernel, order, (projected, *rows_from, qkv_weight, out_weight, low_half, low_x, prompt_src, prompt_len),
        [shaped((PMAX, D), BF), shaped((2, PMAX, HW), BF), shaped((HW, TOK), BF), shaped((HEADS, TOK), F32), *halves, shaped((2, TOK, HW), BF)],
        scratch=[pltpu.VMEM((KEYS, HW), BF), pltpu.VMEM((KEYS, HW), BF), pltpu.VMEM((HW, KEYS), BF),
            pltpu.VMEM((2, D, HW), BF), pltpu.VMEM((HW, D), BF), pltpu.SemaphoreType.DMA((3,))],
        far=(4, 5), name="attend",
    )
    mixed = both((mixed,))
    low_y = partner(joined, "dp", 2)
    low_x_swap = partner(lax.optimization_barrier((low_x, mixed[0]))[0], "mp", 1)
    pieces = 4 if split else 1
    act_shape = (TOK, HF // pieces)
    act_shapes = [shaped(act_shape, BF), shaped((2, *act_shape), BF), shaped(act_shape, BF)] if split else [shaped(act_shape, BF)]
    hidden, normed_second, *act, pre_low, second_part = simple(
        functools.partial(ffn_kernel, split), order, (tokens, *mixed, rows, up_weight, grad_act),
        [shaped((TOK, D), F32), shaped((TOK, D), BF)] + act_shapes + [shaped((TOK, HF), BF), *halves],
        scratch=[pltpu.VMEM((TOK, HF), F32), pltpu.VMEM((pieces, TOK, HF // pieces), BF), pltpu.VMEM((TOK, D), BF), pltpu.VMEM((D, HF), BF), pltpu.SemaphoreType.DMA((HF // TILE + 1,))],
        far=(0, 4), name="ffn",
    )
    second = both((second_part,))

    if split:
        act_own, act_pair, act_side = act
    else:
        cut = act[0].reshape(TOK, outer, 4, hidden_rows)
        act_own, side_x, act_side, far = [
            lax.dynamic_index_in_dim(cut, plane ^ k, 2, keepdims=False).reshape(TOK, HF // 4) for k in range(4)
        ]
        act_pair = jnp.stack([side_x, far])
    act_x = partner(act_pair, "dp", 1)

    up_rows = D // count
    up_half = [shaped((outer, 2, up_rows, D), BF)] * 2

    def up_product(axis, at):
        return simple(
            functools.partial(up_product_kernel, axis, at), order, (normed_second, pre_low), up_half,
            scratch=[pltpu.VMEM((outer, 2, 2, up_rows, D), BF)], name="up_product_" + axis,
        )

    up_away_x, up_kept_x = up_product("x", 0)
    up_got_x = partner(up_away_x, "dp", 1)
    low_y_swap = partner(lax.optimization_barrier((low_y, up_away_x))[0], "mp", 1)
    up_away_y, up_kept_y = up_product("y", D)
    up_got_y = partner(up_away_y, "dp", 2)

    local, sent, along, grad_hidden, hidden_low, tables_second = simple(
        attend_back_kernel, order,
        (*second, hidden, rows, low, out_weight, projected, prompt_pair, log_total, prompt_src, prompt_len),
        [shaped((3, KEYS, HW), BF), shaped((2, 2, PMAX, HW), BF), shaped((2, PMAX, HW), BF), shaped((TOK, D), F32), shaped((TOK, D), BF), shaped((2, D), F32)],
        scratch=[pltpu.VMEM((KEYS, HW), BF), pltpu.VMEM((KEYS, HW), BF), pltpu.VMEM((HW, KEYS), BF), pltpu.VMEM((TOK, HW), BF), pltpu.VMEM((HW, TOK), F32),
            pltpu.VMEM((HW, D), BF), pltpu.SemaphoreType.DMA((1,))],
        far=(5,), name="attend_back",
    )
    first_back = partner(sent, "dp", 1)
    (act_onward,) = simple(join_kernel, order, (act_x, act_side), [shaped(act_x.shape, BF)], name="join")
    act_y = partner(act_onward, "dp", 2)

    if split:
        down_in, down_spec = down_weight.reshape(outer, 4, hidden_rows, D), block((outer, None, hidden_rows, D), lambda t, m: (0, t, 0, 0))
    else:
        down_in, down_spec = down_weight, block((HF // 4, D), lambda t, m: (t, 0))
    ffn_part = call(
        functools.partial(down_kernel, split), order, (*act, down_in), [whole(item.shape) for item in act] + [down_spec],
        halves, half_specs, grid=(4,), scratch=[pltpu.VMEM((TOK, D), F32)], name="down",
    )
    ffn_both = both(ffn_part)


    def outer_step(own, away, bit):
        return own, partner(away, "dp", 4 << bit)

    def through(state, name):
        own, got = state
        bit = 0
        while own.shape[0] > 1:
            bit += 1
            left = own.shape[0] // 2
            shape = (left,) + own.shape[1:]
            own, away = simple(
                functools.partial(halve_kernel, bit), order, (own, got), [shaped(shape, F32), shaped(shape, BF)],
                scratch=[pltpu.VMEM((left, 2) + own.shape[1:], F32)], name=name + "_halve",
            )
            own, got = outer_step(own, away, bit)
        return own, got

    def run_out(state):
        return list(state)

    def second_stage(kept_x, got_x, kept_y, got_y, name):
        _, _, rows, wide = kept_x.shape
        tall = kept_y.shape[-1]
        outs = [shaped((outer, rows, wide), BF)] * 2 + [shaped((outer, rows, tall), BF)] * 2
        away_x, own_x, away_y, own_y = simple(
            second_kernel, order, (kept_x, got_x, kept_y, got_y), outs,
            scratch=[pltpu.VMEM(kept_x.shape, F32), pltpu.VMEM(kept_y.shape, F32)], name=name + "_second",
        )
        return own_x, partner(away_x, "dp", 2), own_y, partner(away_y, "dp", 1)

    def third_stage(own_x, got_x, own_y, got_y, name, direct=False):
        rows = own_x.shape[1]
        columns = own_x.shape[2] + own_y.shape[2]
        if direct and outer == 4:
            shape = (1, rows, columns)
            own, *away = simple(
                direct_kernel, order, (own_x, got_x, own_y, got_y), [shaped(shape, F32)] + [shaped(shape, BF)] * (outer - 1),
                scratch=[pltpu.VMEM((outer, rows, columns), F32)], name=name + "_direct",
            )
            return [own] + [partner(item, "dp", 4 * (m + 1)) for m, item in enumerate(away)]
        shape = (half_outer, rows, columns)
        own, away = simple(
            third_kernel, order, (own_x, got_x, own_y, got_y), [shaped(shape, F32), shaped(shape, BF)],
            scratch=[pltpu.VMEM((half_outer, 2, rows, columns), F32)], name=name + "_third",
        )
        return outer_step(own, away, 0)

    half_outer = max(outer // 2, 1)
    lows = (act_own, act_x, act_y, low, low_x, low_y, low_x_swap, low_y_swap)
    piece_shape = (half_outer, hidden_rows, D)
    down_own, down_away = simple(
        down_product_kernel, order, lows, [shaped(piece_shape, F32), shaped(piece_shape, BF)],
        scratch=[pltpu.VMEM((half_outer, 2, hidden_rows, D), F32)], name="down_product",
    )

    down_later = outer_step(down_own, down_away, 0)
    (onward,) = simple(pass_on_kernel, order, (along, first_back), [shaped(along.shape, BF)], name="pass_on")
    second_back = partner(onward, "dp", 2)


    up_later = second_stage(up_kept_x, up_got_x, up_kept_y, up_got_y, "up")
    qkv_rows = 3 * D // count
    qkv_half = [shaped((outer, 2, qkv_rows + 8, HW // 2), BF), shaped((outer, 2, qkv_rows, HW // 2), BF)]

    def qkv_product(axis, at):
        return simple(
            functools.partial(qkv_product_kernel, axis, at), order, (normed, normed_prompt, local), qkv_half,
            scratch=[pltpu.VMEM((D, KEYS), BF), pltpu.VMEM((3 * D, HW // 2), BF)], name="qkv_product_" + axis,
        )

    qkv_away_x, qkv_kept_x = qkv_product("x", 0)
    qkv_got_x = partner(qkv_away_x, "dp", 1)
    qkv_away_y, qkv_kept_y = qkv_product("y", HW // 2)
    qkv_got_y = partner(qkv_away_y, "dp", 2)
    down_later = through(down_later, "down")
    up_later = third_stage(*up_later, "up")
    normed_part = call(
        grad_normed_kernel, order, (local, first_back, second_back, qkv_weight),
        [block((1, KEYS, HW), lambda c, m: (c, 0, 0)), whole(first_back.shape), whole(second_back.shape), block((1, D, HW), lambda c, m: (c, 0, 0))],
        halves, half_specs,
        grid=(3,), scratch=[pltpu.VMEM((PMAX, HW), BF), pltpu.VMEM((TOK, D), F32)], name="grad_normed",
    )
    normed_both = both(normed_part)
    qkv_later = second_stage(qkv_kept_x, qkv_got_x, qkv_kept_y, qkv_got_y, "qkv")
    input_grad, tables_first = simple(
        input_grad_kernel, order, (*normed_both, tokens, rows, grad_hidden),
        [shaped((TOK, D), BF), shaped((2, D), F32)], name="input_grad",
    )


    up_later = through(up_later, "up")
    down_rows, down_squares = simple(
        finish_kernel, order, run_out(down_later), [shaped((hidden_rows * D // 128, 128), F32), shaped((8, 128), F32)], name="finish_down"
    )
    out_rows = HW // count
    entries = 2 * SECTIONS * HW // count
    spread = []
    if entries != HW:
        selector = (jnp.arange(SECTIONS) == meta[SECTION]).astype(F32)
        tables = jnp.stack([tables_first, tables_second])
        tables = lax.dynamic_slice_in_dim(tables, mp_index * HW, HW, 2)
        whole_tables = selector[None, None, :, None] * jnp.transpose(tables, (1, 0, 2))[:, :, None, :]
        whole_tables = jnp.transpose(whole_tables.reshape(2, count, entries), (1, 0, 2)).reshape(count, 2 * entries // 128, 128)
        spread = [jnp.pad(whole_tables.astype(BF), ((0, 0), (0, out_rows - 2 * entries // 128), (0, 0)))]
    wide, tall = HW + 128, HW
    away_x, kept_x, away_y, kept_y = simple(
        out_product_kernel, order, (attended_t, hidden_low, tables_first, tables_second, *spread),
        [shaped((outer, 2, out_rows, wide), BF)] * 2 + [shaped((outer, 2, out_rows, tall), BF)] * 2,
        scratch=[pltpu.VMEM((outer, 2, 2, out_rows, wide), BF), pltpu.VMEM((outer, 2, 2, out_rows, tall), BF)],
        name="out_product",
    )
    got_x, got_y = partner(away_x, "dp", 1), partner(away_y, "dp", 2)
    up_terms = run_out(up_later)
    up_lines, up_squares = simple(finish_kernel, order, up_terms, [shaped((up_rows * HF // 128, 128), F32), shaped((8, 128), F32)], name="finish_up")

    qkv_later = third_stage(*qkv_later, "qkv", direct=True)
    out_later = second_stage(kept_x, got_x, kept_y, got_y, "out")
    (block_out,) = simple(block_out_kernel, order, (hidden, *ffn_both), [shaped((TOK, D), BF)], name="block_out")
    out_later = third_stage(*out_later, "out")
    out_later = run_out(through(out_later, "out"))
    qkv_terms = run_out(through(qkv_later, "qkv")) if len(qkv_later) == 2 else qkv_later

    flat = master.shape[1]
    (qkv_lines, out_lines, table_lines, squares) = simple(
        functools.partial(finish_last_kernel, len(qkv_terms)), order, (*qkv_terms, *out_later, up_squares, down_squares),
        [shaped((qkv_rows * HW // 128, 128), F32), shaped((out_rows * D // 128, 128), F32), shaped((max(2 * entries // 128, 1), 128), F32), shaped((8, 128), F32)],
        name="finish",
    )
    squares = squares + partner(squares, "mp", 1)
    squares = squares + partner(squares, "dp", 1) + partner(squares, "dp", 2) + partner(squares, "dp", 3)
    step = 4
    while step < count:
        flips = (step, 2 * step, 3 * step) if step * 4 <= count else (step,)
        squares = sum([partner(squares, "dp", flip) for flip in flips], squares)
        step *= 4 if step * 4 <= count else 2
    step_count = adam_step[0].astype(F32)
    fixes = jnp.stack([1.0 / (1.0 - jnp.power(BETA_ONE, step_count)), 1.0 / (1.0 - jnp.power(BETA_TWO, step_count))]).reshape(1, 2)
    lines = flat // 128
    rates = [D ** (-0.5), OUT_FAN ** (-0.5), D ** (-0.5), FF ** (-0.5), 0.2]
    flats = [item.reshape(lines, 128) for item in (master, first_moment, second_moment, ema_weight)]
    new_first, new_second, new_master, copy, new_ema, grad_norm = simple(
        functools.partial(adam_kernel, rates), order, (squares, fixes, qkv_lines, out_lines, up_lines, down_rows, table_lines, *flats),
        [shaped((lines, 128), F32)] * 3 + [shaped((1, flat), BF), shaped((lines, 128), F32), shaped((1, 1), F32)], name="adam", vmem=40,
    )
    return (
        block_out,
        input_grad,
        grad_norm.reshape(1),
        new_first.reshape(1, flat),
        new_second.reshape(1, flat),
        new_master.reshape(1, flat),
        copy,
        new_ema.reshape(1, flat),
    )


def solution(mesh):
    placed = (
        P("dp", None), P("dp", None), P(None, None, "mp"), P("mp", None), P(None, "mp"), P("mp", None), P(), P(),
        P("dp"), P("dp"), P("dp"), P("dp"), P(),
        P("mp", "dp"), P("mp", "dp"), P("mp", "dp"), P("mp", "dp"),
    )
    flat = P("mp", "dp")
    return jax.shard_map(
        body, mesh=mesh, in_specs=placed,
        out_specs=(P("dp", None), P("dp", None), P(), flat, flat, flat, flat, flat),
        check_vma=False,
    )
```

```python
import functools

import jax
import jax.numpy as jnp
from jax import lax
from jax.experimental import pallas as pl
from jax.experimental.pallas import tpu as pltpu
from jax.sharding import PartitionSpec as P

D = 1024
HDIM = 64
FF = 4096
SECTIONS = 8
TOK = 384
PMAX = 96
KEYS = TOK + PMAX
OUT_FAN = 2
HW = D // 2
HF = FF // 2
HEADS = HW // HDIM
CLIP_NORM = 1.0
BETA_ONE = 0.5
BETA_TWO = 0.5
WEIGHT_DECAY = 0.1
EMA_DECAY = 0.75

BF = jnp.bfloat16
F32 = jnp.float32
MP, PX, PY, PLANE, OUTER, LENGTH, SECTION = range(7)


def shaped(shape, dtype):
    return jax.ShapeDtypeStruct(shape, dtype)


def dot_nn(a, b):
    return lax.dot_general(a, b, (((1,), (0,)), ((), ())), preferred_element_type=F32)


def dot_nt(a, b):
    return lax.dot_general(a, b, (((1,), (1,)), ((), ())), preferred_element_type=F32)


def dot_tn(a, b):
    return lax.dot_general(a, b, (((0,), (0,)), ((), ())), preferred_element_type=F32)


def block(shape, index):
    return pl.BlockSpec(shape, index)


def whole(shape):
    rank = len(shape)
    return pl.BlockSpec(shape, lambda *_: (0,) * rank)


class Order:
    def __init__(self, meta):
        self.meta = meta
        self.after = []


HBM = pl.BlockSpec(memory_space=pltpu.HBM)


def fetch(source, target, sem):
    copy = pltpu.make_async_copy(source, target, sem)
    copy.start()
    return copy


def call(kernel, order, inputs, in_specs, outs, out_specs, grid=(1,), scratch=(), name=None, vmem=20):
    after, count = list(order.after), len(inputs)

    def run(meta, *refs):
        kernel(meta, *refs[:count], *refs[count + len(after) :])

    found = pl.pallas_call(
        run,
        grid_spec=pltpu.PrefetchScalarGridSpec(
            num_scalar_prefetch=1, grid=grid, in_specs=list(in_specs) + [HBM] * len(after),
            out_specs=out_specs, scratch_shapes=scratch,
        ),
        out_shape=outs,
        compiler_params=pltpu.CompilerParams(vmem_limit_bytes=vmem << 20),
        cost_estimate=pl.CostEstimate(flops=1, bytes_accessed=1, transcendentals=0),
        name=name,
    )(order.meta, *inputs, *after)
    order.after = [min(found, key=lambda item: item.size)]
    return found


def simple(kernel, order, inputs, outs, far=(), far_out=(), **kw):
    return call(
        kernel, order, inputs,
        [HBM if k in far else pl.BlockSpec(memory_space=pltpu.SMEM) if a.shape == (1,) else whole(a.shape) for k, a in enumerate(inputs)],
        outs, [HBM if k in far_out else whole(o.shape) for k, o in enumerate(outs)], **kw
    )


def unit_rows(values):
    centred = values - jnp.mean(values, axis=-1, keepdims=True)
    scale = lax.rsqrt(jnp.mean(centred * centred, axis=-1, keepdims=True) + 1e-05)
    return centred * scale, scale


def norm_back(grad, gain_row, unit, scale):
    e = gain_row * grad
    return scale * (e - jnp.mean(e, axis=-1, keepdims=True) - unit * jnp.mean(e * unit, axis=-1, keepdims=True))


def row_of(rows, which):
    return rows[which : which + 1, :]


def valid_rows(meta):
    return lax.broadcasted_iota(jnp.int32, (TOK, 1), 0) < meta[LENGTH]


def keys_ok(meta, prompt):
    at = lax.broadcasted_iota(jnp.int32, (KEYS, 1), 0)
    return at < jnp.where(at < TOK, meta[LENGTH], TOK + prompt[0])


def summed(refs):
    here, there = refs
    return here[...].astype(F32) + there[...].astype(F32)


def start_kernel(
    tokens, cotangent, gain, shift, lengths, section,
    out, low, half, meta, rows, some, whole_low, tables, read, sems,
):
    scalars = [fetch(item, read.at[k], sems.at[6 + k]) for k, item in enumerate((lengths, section))]
    copies = [fetch(tokens.at[pl.ds(0, PMAX), :], some, sems.at[0])]
    for k, (table, norm) in enumerate(((gain, 0), (shift, 0), (gain, 1), (shift, 1))):
        copies.append(fetch(table.at[norm], tables.at[k], sems.at[1 + k]))
    late = fetch(cotangent, whole_low, sems.at[5])
    dp_index, mp_index = lax.axis_index("dp"), lax.axis_index("mp")
    plane = jnp.bitwise_and(dp_index, 3)
    meta[MP] = mp_index
    meta[PX] = jnp.bitwise_and(plane, 1)
    meta[PY] = lax.shift_right_logical(plane, 1)
    meta[PLANE] = plane
    meta[OUTER] = lax.shift_right_logical(dp_index, 2)
    for copy in scalars:
        copy.wait()
    valid_count = read[0, 0]
    meta[LENGTH] = valid_count
    meta[SECTION] = read[1, 0]
    chosen = read[1, 0]
    for copy in copies:
        copy.wait()
    for k in range(4):
        rows[k : k + 1, :] = tables[k, pl.ds(chosen, 1), :]
    rows[4:, :] = jnp.zeros((4, D), F32)
    unit, _ = unit_rows(some[...].astype(F32))
    out[...] = (row_of(rows, 0) * unit + row_of(rows, 1)).astype(BF)
    late.wait()
    valid = lax.broadcasted_iota(jnp.int32, (TOK, 1), 0) < valid_count
    kept = jnp.where(valid, whole_low[...], jnp.zeros((), BF))
    low[...] = kept

    @pl.when(mp_index == 0)
    def _():
        half[...] = kept[:, :HW]

    @pl.when(mp_index == 1)
    def _():
        half[...] = kept[:, HW:]


def qkv_kernel(meta, tokens, rows, qkv, normed, projected, frames, weights, sems):
    first = fetch(tokens, frames, sems.at[3])
    copies = [fetch(qkv.at[c], weights.at[c], sems.at[c]) for c in range(3)]
    first.wait()
    unit, _ = unit_rows(frames[...].astype(F32))
    normed[...] = (row_of(rows, 0) * unit + row_of(rows, 1)).astype(BF)
    for c in range(3):
        copies[c].wait()
        projected[c] = dot_nn(normed[...], weights[c]).astype(BF)


def grad_act_kernel(meta, low, down, out, weights, sems):
    size = HF // 4
    copies = [fetch(down.at[pl.ds(t * size, size), :], weights.at[pl.ds(t * size, size), :], sems.at[t]) for t in range(4)]
    for t in range(4):
        copies[t].wait()
        out[:, t * size : (t + 1) * size] = dot_nt(low[...], weights[t * size : (t + 1) * size, :]).astype(BF)


def attend_kernel(
    meta, projected, rows_x, rows_y, rows_far, qkv, out_weight, low_half, low_x, source, prompt,
    normed_prompt, prompt_pair, attended_t, log_total, part, joined, keys, values, values_t, weights, out_w, sems,
):
    copies = [fetch(qkv.at[c], weights.at[c - 1], sems.at[c - 1]) for c in (1, 2)]
    last = fetch(out_weight, out_w, sems.at[2])
    joined[0] = low_half[...]
    joined[1] = low_x[...]
    keys[:TOK] = projected[1]
    values[:TOK] = projected[2]
    relative = jnp.bitwise_xor(jnp.bitwise_and(source[0], 3), meta[PLANE])
    for k, rows in ((1, rows_x), (2, rows_y), (3, rows_far)):

        @pl.when(relative == k)
        def _(rows=rows):
            normed_prompt[...] = rows[...]

    rows = normed_prompt[...]
    copies[0].wait()
    pair_k = dot_nn(rows, weights[0]).astype(BF)
    copies[1].wait()
    pair_v = dot_nn(rows, weights[1]).astype(BF)
    prompt_pair[0] = pair_k
    prompt_pair[1] = pair_v
    keys[TOK:] = pair_k
    values[TOK:] = pair_v
    values_t[...] = values[...].T
    counted = keys_ok(meta, prompt)
    lane = lax.broadcasted_iota(jnp.int32, (1, 2 * HDIM), 1)
    for head in range(HEADS):
        at = (head // 2) * 2 * HDIM
        mine = jnp.where((lane // HDIM) == head % 2, HDIM ** (-0.5), 0.0).astype(BF)
        query = projected[0, :, at : at + 2 * HDIM] * mine
        scores = jnp.where(counted, dot_nt(keys[:, at : at + 2 * HDIM], query), -1e30)
        top = jnp.max(scores, axis=0, keepdims=True)
        grown = jnp.exp(scores - top)
        total = jnp.sum(grown, axis=0, keepdims=True)
        probability = (grown * (1.0 / total)).astype(BF)
        rows_at = slice(head * HDIM, (head + 1) * HDIM)
        attended_t[rows_at, :] = dot_nn(values_t[rows_at, :], probability).astype(BF)
        log_total[head : head + 1, :] = top + jnp.log(total)
    last.wait()
    part[...] = dot_tn(attended_t[...], out_w[...]).astype(BF)


TILE = 256


ERFC = (0.235325614, 0.0913858287, 0.649566092, -0.635408842, 0.886669787, -0.227538481)


def gelu_parts(values):
    decay = jnp.exp(-0.5 * values * values)
    t = 1.0 / (1.0 + (0.39 * 0.5**0.5) * jnp.abs(values))
    tail = 0.5 * ERFC[-1]
    for factor in ERFC[-2::-1]:
        tail = tail * t + 0.5 * factor
    tail = tail * t * decay
    cdf = jnp.where(values < 0.0, tail, 1.0 - tail)
    return cdf, cdf + values * (decay * (0.5 / jnp.pi) ** 0.5)


def ffn_kernel(split, meta, tokens, here, there, rows, up, grad_act, hidden, normed, *refs):
    *act, pre_low, part, pre, held, frames, weights, sems = refs
    steps = HF // TILE
    first = fetch(tokens, frames, sems.at[steps])
    copies = [fetch(up.at[:, pl.ds(t * TILE, TILE)], weights.at[:, pl.ds(t * TILE, TILE)], sems.at[t]) for t in range(steps)]
    first.wait()
    state = frames[...].astype(F32) + summed((here, there))
    hidden[...] = state
    unit, _ = unit_rows(state)
    normed[...] = (row_of(rows, 2) * unit + row_of(rows, 3)).astype(BF)
    for t in range(steps):
        copies[t].wait()
        at = slice(t * TILE, (t + 1) * TILE)
        pre[:, at] = dot_nn(normed[...], weights[:, at])
    across = split or 128

    def block_of_rows(r, _):
        some = pl.ds(pl.multiple_of(r * 64, 64), 64)
        for t in range(HF // across):
            at = slice(t * across, (t + 1) * across)
            values = pre[some, at]
            cdf, slope = gelu_parts(values)
            activated = (values * cdf).astype(BF)
            if split:
                held[t % 4, some, (t // 4) * split : (t // 4 + 1) * split] = activated
            else:
                act[0][some, at] = activated
            pre_low[some, at] = (grad_act[some, at].astype(F32) * slope).astype(BF)
        return 0

    lax.fori_loop(0, TOK // 64, block_of_rows, 0)
    part[...] = dot_nt(pre_low[...], weights[...]).astype(BF)
    if split:
        for k, out in enumerate((act[0], act[1].at[0], act[2], act[1].at[1])):
            out[...] = held[jnp.bitwise_xor(meta[PLANE], k)]


def join_kernel(meta, act_x, mine, out):
    out[0] = mine[...]
    out[1] = act_x[1]


def down_kernel(split, meta, *refs):
    *act, down, part, total = refs
    step = pl.program_id(0)

    @pl.when(step == 0)
    def _():
        total[...] = jnp.zeros_like(total)

    if split:
        rows = down[...].reshape(HF // 4, D)
        piece = jnp.bitwise_xor(step, meta[PLANE])
        for k, value in enumerate((act[0], act[1].at[0], act[2], act[1].at[1])):

            @pl.when(piece == k)
            def _(value=value):
                total[...] += dot_nn(value[...], rows)

    else:
        total[...] += dot_nn(act[0][:, pl.ds(pl.multiple_of(step * (HF // 4), HF // 4), HF // 4)], down[...])

    @pl.when(step == pl.num_programs(0) - 1)
    def _():
        part[...] = total[...].astype(BF)


def block_out_kernel(meta, hidden, here, there, out):
    out[...] = (hidden[...] + summed((here, there))).astype(BF)


def attend_back_kernel(
    meta, here, there, hidden, rows, low, out_weight, projected, prompt_pair, log_total, source, prompt,
    local, sent, along, grad_hidden, hidden_low, tables, keys, values, keys_t, grads, query_t, out_w, sems,
):
    last = fetch(out_weight, out_w, sems.at[0])
    back = summed((here, there))
    unit, scale = unit_rows(hidden[...])
    full = low[...].astype(F32) + norm_back(back, row_of(rows, 2), unit, scale)
    grad_hidden[...] = full
    tables[0:1, :] = jnp.sum(back * unit, axis=0, keepdims=True)
    tables[1:2, :] = jnp.sum(back, axis=0, keepdims=True)
    rounded = full.astype(BF)
    hidden_low[...] = rounded
    last.wait()
    grads[...] = dot_nt(rounded, out_w[...]).astype(BF)
    keys[:TOK] = projected[1]
    keys[TOK:] = prompt_pair[0]
    values[:TOK] = projected[2]
    values[TOK:] = prompt_pair[1]
    keys_t[...] = keys[...].T
    counted = keys_ok(meta, prompt)
    lane = lax.broadcasted_iota(jnp.int32, (1, 2 * HDIM), 1)
    left = lane < HDIM
    for pair in range(HEADS // 2):
        at = pair * 2 * HDIM
        span = slice(at, at + 2 * HDIM)
        key_pair, value_pair = keys[:, span], values[:, span]
        query_pair = projected[0, :, span] * jnp.asarray(HDIM ** (-0.5), BF)
        grad_pair = grads[:, span]
        found = []
        for head in (2 * pair, 2 * pair + 1):
            mine = ((lane // HDIM) == head % 2).astype(BF)
            scores = jnp.where(counted, dot_nt(key_pair, query_pair * mine), -1e30)
            probability = jnp.exp(scores - log_total[head : head + 1, :])
            grad_prob = dot_nt(value_pair, grad_pair * mine)
            centre = jnp.sum(probability * grad_prob, axis=0, keepdims=True)
            grad_scores = (probability * (grad_prob - centre)).astype(BF)
            rows_at = slice(head * HDIM, (head + 1) * HDIM)
            query_t[rows_at, :] = dot_nn(keys_t[rows_at, :], grad_scores) * HDIM ** (-0.5)
            found.append((dot_nn(grad_scores, query_pair), dot_nn(probability.astype(BF), grad_pair)))
        local[1, :, span] = jnp.where(left, found[0][0], found[1][0]).astype(BF)
        local[2, :, span] = jnp.where(left, found[0][1], found[1][1]).astype(BF)
    local[0, :TOK, :] = query_t[...].T.astype(BF)
    local[0, TOK:, :] = jnp.zeros((PMAX, HW), BF)
    relative = jnp.bitwise_xor(jnp.bitwise_and(source[0], 3), meta[PLANE])
    for c in range(2):
        prompt = local[1 + c, TOK:, :]
        for j in range(2):
            sent[j, c] = jnp.where(relative == 1 + 2 * j, prompt, jnp.zeros((), BF))
        along[c] = jnp.where(relative == 2, prompt, jnp.zeros((), BF))


def pass_on_kernel(meta, along, got, out):
    out[...] = (along[...].astype(F32) + got[1].astype(F32)).astype(BF)


def grad_normed_kernel(meta, local, first, second, qkv, part, returned_low, total):
    c = pl.program_id(0)

    @pl.when(c == 0)
    def _():
        total[...] = jnp.zeros_like(total)

    total[...] += dot_nt(local[0, :TOK, :], qkv[0])

    @pl.when(c > 0)
    def _():
        at = c - 1
        returned = first[0, at].astype(F32) + second[at].astype(F32)
        returned_low[...] = returned.astype(BF)
        total[:PMAX, :] += dot_nt(returned_low[...], qkv[0])

    @pl.when(c == 2)
    def _():
        part[...] = total[...].astype(BF)


def input_grad_kernel(meta, here, there, tokens, rows, grad_hidden, out, tables):
    back = summed((here, there))
    unit, scale = unit_rows(tokens[...].astype(F32))
    out[...] = (grad_hidden[...] + norm_back(back, row_of(rows, 0), unit, scale)).astype(BF)
    tables[0:1, :] = jnp.sum(back * unit, axis=0, keepdims=True)
    tables[1:2, :] = jnp.sum(back, axis=0, keepdims=True)


def part_out(out, at, whole_ref, axis, side):
    if axis == "x":
        out[..., at] = whole_ref[:, :, side]
    else:
        out[..., at] = whole_ref[:, side]


def pick(held, axis, side):
    return held[:, :, side] if axis == "x" else held[:, side]


def up_product_kernel(axis, at, meta, normed, pre_low, away, kept, held):
    held[...] = dot_tn(normed[...], pre_low[:, at : at + D]).astype(BF).reshape(held.shape)
    side = meta[PX] if axis == "x" else meta[PY]
    away[...] = pick(held, axis, 1 - side)
    kept[...] = pick(held, axis, side)


def down_product_kernel(meta, mine, act_x, act_y, low, low_x, low_y, swap_x, swap_y, own, away, held):
    here = pl.ds(pl.multiple_of(meta[MP] * HW, HW), HW)
    there = pl.ds(pl.multiple_of((1 - meta[MP]) * HW, HW), HW)
    for at, x, y in ((here, low_x, low_y), (there, swap_x, swap_y)):
        found = dot_tn(mine[...], low[:, at])
        found += dot_tn(act_x[0], x[...])
        found += dot_tn(act_y[0], y[0])
        found += dot_tn(act_y[1], y[1])
        held[:, :, :, at] = found.reshape(held.shape[:3] + (HW,))
    side = lax.rem(meta[OUTER], 2)
    own[...] = held[:, side]
    away[...] = held[:, 1 - side].astype(BF)


def qkv_product_kernel(axis, at, meta, normed, normed_prompt, local, away, kept, normed_t, held):
    normed_t[:, :TOK] = normed[...].T
    normed_t[:, TOK:] = normed_prompt[...].T
    outer, _, rows, columns = kept.shape
    for c in range(3):
        held[c * D : (c + 1) * D, :] = dot_nn(normed_t[...], local[c, :, at : at + columns]).astype(BF)
    parts = held.reshape(outer, 2, 2, rows, columns)
    side = meta[PX] if axis == "x" else meta[PY]
    away[:, :, :rows] = pick(parts, axis, 1 - side)
    kept[...] = pick(parts, axis, side)


def tables_of(meta, block_index, first, second):
    ref = (first, second)[block_index // SECTIONS]
    mine = ref[:, pl.ds(pl.multiple_of(meta[MP] * HW, HW), HW)]
    mine = jnp.where(meta[SECTION] == block_index % SECTIONS, mine, 0.0)
    return jnp.concatenate([mine[k : k + 1, 128 * c : 128 * (c + 1)] for k in range(2) for c in range(HW // 128)], axis=0)


def out_product_kernel(meta, attended_t, hidden_low, first, second, *refs):
    *spread, away_x, kept_x, away_y, kept_y, held_x, held_y = refs
    out_product(meta, attended_t, hidden_low, first, second, spread, away_x, kept_x, away_y, kept_y, held_x, held_y)


def out_product(meta, attended_t, hidden_low, first, second, spread, away_x, kept_x, away_y, kept_y, held_x, held_y):
    found = dot_nn(attended_t[...], hidden_low[...]).astype(BF)
    rows = held_x.shape[3]
    held_x[..., :HW] = found[:, :HW].reshape(held_x.shape[:3] + (rows, HW))
    if spread:
        held_x[..., HW:] = spread[0][...].reshape(held_x.shape[:3] + (rows, 128))
    else:
        for k in range(4 * held_x.shape[0]):
            entries = tables_of(meta, k, first, second)
            entries = jnp.concatenate([entries, jnp.zeros((rows - entries.shape[0], 128), F32)], axis=0)
            held_x[k // 4, (k // 2) % 2, k % 2, :, HW:] = entries.astype(BF)
    held_y[...] = found[:, HW:].reshape(held_y.shape)
    away_x[...] = held_x[:, :, 1 - meta[PX]]
    kept_x[...] = held_x[:, :, meta[PX]]
    away_y[...] = held_y[:, 1 - meta[PY]]
    kept_y[...] = held_y[:, meta[PY]]


def second_kernel(meta, kept_x, got_x, kept_y, got_y, away_x, own_x, away_y, own_y, held_x, held_y):
    rows = kept_x.shape[2]
    held_x[...] = kept_x[...].astype(F32) + got_x[:, :, :rows].astype(F32)
    held_y[...] = kept_y[...].astype(F32) + got_y[:, :, :rows].astype(F32)
    away_x[...] = held_x[:, 1 - meta[PY]].astype(BF)
    own_x[...] = held_x[:, meta[PY]].astype(BF)
    away_y[...] = held_y[:, 1 - meta[PX]].astype(BF)
    own_y[...] = held_y[:, meta[PX]].astype(BF)


def third_kernel(meta, kept_x, got_x, kept_y, got_y, own, away, held):
    left = kept_x.shape[-1]
    shape = held.shape[:2] + kept_x.shape[1:]
    held[..., :left] = (kept_x[...].astype(F32) + got_x[...].astype(F32)).reshape(shape)
    shape = held.shape[:2] + kept_y.shape[1:]
    held[..., left:] = (kept_y[...].astype(F32) + got_y[...].astype(F32)).reshape(shape)
    side = lax.rem(meta[OUTER], 2)
    own[...] = held[:, side]
    away[...] = held[:, 1 - side].astype(BF)


def direct_kernel(meta, kept_x, got_x, kept_y, got_y, own, *refs):
    *away, held = refs
    left = kept_x.shape[-1]
    held[..., :left] = kept_x[...].astype(F32) + got_x[...].astype(F32)
    held[..., left:] = kept_y[...].astype(F32) + got_y[...].astype(F32)
    own[0] = held[meta[OUTER]]
    for m, out in enumerate(away):
        out[0] = held[jnp.bitwise_xor(meta[OUTER], m + 1)].astype(BF)


def halve_kernel(bit, meta, kept, got, own, away, held):
    held[...] = (kept[...] + got[...].astype(F32)).reshape(held.shape)
    side = lax.rem(lax.shift_right_logical(meta[OUTER], bit), 2)
    own[...] = held[:, side]
    away[...] = held[:, 1 - side].astype(BF)


def to_rows(out, at, value):
    rows, columns = value.shape
    across = columns // 128
    for j in range(across):
        piece = value[:, 128 * j : 128 * (j + 1)]
        if across == 1:
            out[at : at + rows, :] = piece
        else:
            out[pl.ds(at + j, rows, stride=across), :] = piece


def total_of(terms):
    value = terms[0][0]
    for got in terms[1:]:
        value = value + got[0].astype(F32)
    return value


def square_sum(values):
    total = jnp.zeros((1, 128), F32)
    for value in values:
        line = jnp.sum(value * value, axis=0, keepdims=True)
        for j in range(value.shape[1] // 128):
            total = total + line[:, 128 * j : 128 * (j + 1)]
    return jnp.sum(total, axis=1, keepdims=True)


def finish_kernel(meta, *refs):
    *ins, out, squares = refs
    value = total_of(ins)
    to_rows(out, 0, value)
    squares[...] = jnp.broadcast_to(square_sum([value]), squares.shape)


def finish_last_kernel(first, meta, *refs):
    *ins, up_squares, down_squares, qkv_out, out_out, table_out, squares = refs
    value = total_of(ins[:first])
    to_rows(qkv_out, 0, value)
    both = total_of(ins[first:])
    tables = both[:, HW : HW + 128]
    third = jnp.concatenate([both[:, :HW], both[:, HW + 128 :]], axis=1)
    to_rows(out_out, 0, third)
    table_out[...] = tables[: table_out.shape[0], :]
    squares[...] = square_sum([value, third, tables]) + up_squares[...] + down_squares[...]


def adam_kernel(rates, meta, squares, fixes, *refs):
    pieces, (master, first, second, ema, new_first, new_second, new_master, copy, new_ema, norm) = refs[: len(rates)], refs[len(rates) :]
    norm[...] = jnp.sqrt(squares[0:1, 0:1])
    clip = jnp.minimum(1.0, CLIP_NORM / (norm[...] + 1e-06))
    one, two = fixes[0:1, 0:1], fixes[0:1, 1:2]
    start = 0
    for piece, rate in zip(pieces, rates):
        rows = piece.shape[0]
        step = next(n for n in (256, 128, 64, 32, 16, 8, 4, 2, 1) if rows % n == 0)

        def one_chunk(k, _, piece=piece, rate=rate, start=start, step=step):
            at = pl.ds(start + k * step, step)
            clipped = clip * piece[pl.ds(k * step, step), :]
            moment = BETA_ONE * first[at, :] + (1.0 - BETA_ONE) * clipped
            square = BETA_TWO * second[at, :] + (1.0 - BETA_TWO) * clipped * clipped
            new_first[at, :] = moment
            new_second[at, :] = square
            update = (moment * one) / (jnp.sqrt(square * two) + 1e-08)
            old = master[at, :]
            weights = old - rate * (update + WEIGHT_DECAY * old)
            new_master[at, :] = weights
            new_ema[at, :] = EMA_DECAY * ema[at, :] + (1.0 - EMA_DECAY) * weights
            return 0

        lax.fori_loop(0, rows // step, one_chunk, 0)
        start += rows
    copy[...] = new_master[...].astype(BF).reshape(copy.shape)


def partner(value, axis, flip):
    count = lax.axis_size(axis)
    return lax.ppermute(value, axis, [(i, i ^ flip) for i in range(count)])


def body(
    tokens, cotangent, qkv_weight, out_weight, up_weight, down_weight, norm_gain, norm_shift,
    lengths, prompt_src, prompt_len, codebook_section, adam_step, master, first_moment, second_moment, ema_weight,
):
    count = lax.axis_size("dp")
    outer = count // 4

    prompt_rows, low, low_half, meta, rows = pl.pallas_call(
        start_kernel,
        in_specs=[HBM] * 6,
        out_specs=[pl.BlockSpec(memory_space=pltpu.VMEM)] * 3 + [pl.BlockSpec(memory_space=pltpu.SMEM), pl.BlockSpec(memory_space=pltpu.VMEM)],
        scratch_shapes=[
            pltpu.VMEM((PMAX, D), BF), pltpu.VMEM((TOK, D), BF), pltpu.VMEM((4, SECTIONS, D), F32),
            pltpu.SMEM((2, 1), jnp.int32), pltpu.SemaphoreType.DMA((8,)),
        ],
        out_shape=[shaped((PMAX, D), BF), shaped((TOK, D), BF), shaped((TOK, HW), BF), shaped((7,), jnp.int32), shaped((8, D), F32)],
        compiler_params=pltpu.CompilerParams(vmem_limit_bytes=60 << 20),
        cost_estimate=pl.CostEstimate(flops=1, bytes_accessed=1, transcendentals=0),
        name="start",
    )(tokens, cotangent, norm_gain, norm_shift, lengths, codebook_section)
    order = Order(meta)
    plane, mp_index = meta[PLANE], meta[MP]
    rows_from = [partner(prompt_rows, "dp", k) for k in (1, 2, 3)]
    low_x = partner(low_half, "dp", 1)
    normed, projected = simple(
        qkv_kernel, order, (tokens, rows, qkv_weight), [shaped((TOK, D), BF), shaped((3, TOK, HW), BF)], far=(0, 2),
        scratch=[pltpu.VMEM((TOK, D), BF), pltpu.VMEM((3, D, HW), BF), pltpu.SemaphoreType.DMA((4,))], name="qkv",
    )
    hidden_rows = HF // count
    split = hidden_rows if hidden_rows % 128 == 0 else 0
    (grad_act,) = simple(
        grad_act_kernel, order, (low, down_weight), [shaped((TOK, HF), BF)], far=(1,),
        scratch=[pltpu.VMEM((HF, D), BF), pltpu.SemaphoreType.DMA((4,))], name="grad_act",
    )
    halves = [shaped((TOK, D), BF)]
    half_specs = [whole((TOK, D))]

    def both(parts):
        return (*parts, *[partner(item, "mp", 1) for item in parts])

    normed_prompt, prompt_pair, attended_t, log_total, mixed, joined = simple(
        attend_kernel, order, (projected, *rows_from, qkv_weight, out_weight, low_half, low_x, prompt_src, prompt_len),
        [shaped((PMAX, D), BF), shaped((2, PMAX, HW), BF), shaped((HW, TOK), BF), shaped((HEADS, TOK), F32), *halves, shaped((2, TOK, HW), BF)],
        scratch=[pltpu.VMEM((KEYS, HW), BF), pltpu.VMEM((KEYS, HW), BF), pltpu.VMEM((HW, KEYS), BF),
            pltpu.VMEM((2, D, HW), BF), pltpu.VMEM((HW, D), BF), pltpu.SemaphoreType.DMA((3,))],
        far=(4, 5), name="attend",
    )
    mixed = both((mixed,))
    low_y = partner(joined, "dp", 2)
    low_x_swap = partner(lax.optimization_barrier((low_x, mixed[0]))[0], "mp", 1)
    pieces = 4 if split else 1
    act_shape = (TOK, HF // pieces)
    act_shapes = [shaped(act_shape, BF), shaped((2, *act_shape), BF), shaped(act_shape, BF)] if split else [shaped(act_shape, BF)]
    hidden, normed_second, *act, pre_low, second_part = simple(
        functools.partial(ffn_kernel, split), order, (tokens, *mixed, rows, up_weight, grad_act),
        [shaped((TOK, D), F32), shaped((TOK, D), BF)] + act_shapes + [shaped((TOK, HF), BF), *halves],
        scratch=[pltpu.VMEM((TOK, HF), F32), pltpu.VMEM((pieces, TOK, HF // pieces), BF), pltpu.VMEM((TOK, D), BF), pltpu.VMEM((D, HF), BF), pltpu.SemaphoreType.DMA((HF // TILE + 1,))],
        far=(0, 4), name="ffn",
    )
    second = both((second_part,))

    if split:
        act_own, act_pair, act_side = act
    else:
        cut = act[0].reshape(TOK, outer, 4, hidden_rows)
        act_own, side_x, act_side, far = [
            lax.dynamic_index_in_dim(cut, plane ^ k, 2, keepdims=False).reshape(TOK, HF // 4) for k in range(4)
        ]
        act_pair = jnp.stack([side_x, far])
    act_x = partner(act_pair, "dp", 1)

    up_rows = D // count
    up_half = [shaped((outer, 2, up_rows, D), BF)] * 2

    def up_product(axis, at):
        return simple(
            functools.partial(up_product_kernel, axis, at), order, (normed_second, pre_low), up_half,
            scratch=[pltpu.VMEM((outer, 2, 2, up_rows, D), BF)], name="up_product_" + axis,
        )

    up_away_x, up_kept_x = up_product("x", 0)
    up_got_x = partner(up_away_x, "dp", 1)
    low_y_swap = partner(lax.optimization_barrier((low_y, up_away_x))[0], "mp", 1)
    up_away_y, up_kept_y = up_product("y", D)
    up_got_y = partner(up_away_y, "dp", 2)

    local, sent, along, grad_hidden, hidden_low, tables_second = simple(
        attend_back_kernel, order,
        (*second, hidden, rows, low, out_weight, projected, prompt_pair, log_total, prompt_src, prompt_len),
        [shaped((3, KEYS, HW), BF), shaped((2, 2, PMAX, HW), BF), shaped((2, PMAX, HW), BF), shaped((TOK, D), F32), shaped((TOK, D), BF), shaped((2, D), F32)],
        scratch=[pltpu.VMEM((KEYS, HW), BF), pltpu.VMEM((KEYS, HW), BF), pltpu.VMEM((HW, KEYS), BF), pltpu.VMEM((TOK, HW), BF), pltpu.VMEM((HW, TOK), F32),
            pltpu.VMEM((HW, D), BF), pltpu.SemaphoreType.DMA((1,))],
        far=(5,), name="attend_back",
    )
    first_back = partner(sent, "dp", 1)
    (act_onward,) = simple(join_kernel, order, (act_x, act_side), [shaped(act_x.shape, BF)], name="join")
    act_y = partner(act_onward, "dp", 2)

    if split:
        down_in, down_spec = down_weight.reshape(outer, 4, hidden_rows, D), block((outer, None, hidden_rows, D), lambda t, m: (0, t, 0, 0))
    else:
        down_in, down_spec = down_weight, block((HF // 4, D), lambda t, m: (t, 0))
    ffn_part = call(
        functools.partial(down_kernel, split), order, (*act, down_in), [whole(item.shape) for item in act] + [down_spec],
        halves, half_specs, grid=(4,), scratch=[pltpu.VMEM((TOK, D), F32)], name="down",
    )
    ffn_both = both(ffn_part)


    def outer_step(own, away, bit):
        return own, partner(away, "dp", 4 << bit)

    def through(state, name):
        own, got = state
        bit = 0
        while own.shape[0] > 1:
            bit += 1
            left = own.shape[0] // 2
            shape = (left,) + own.shape[1:]
            own, away = simple(
                functools.partial(halve_kernel, bit), order, (own, got), [shaped(shape, F32), shaped(shape, BF)],
                scratch=[pltpu.VMEM((left, 2) + own.shape[1:], F32)], name=name + "_halve",
            )
            own, got = outer_step(own, away, bit)
        return own, got

    def run_out(state):
        return list(state)

    def second_stage(kept_x, got_x, kept_y, got_y, name):
        _, _, rows, wide = kept_x.shape
        tall = kept_y.shape[-1]
        outs = [shaped((outer, rows, wide), BF)] * 2 + [shaped((outer, rows, tall), BF)] * 2
        away_x, own_x, away_y, own_y = simple(
            second_kernel, order, (kept_x, got_x, kept_y, got_y), outs,
            scratch=[pltpu.VMEM(kept_x.shape, F32), pltpu.VMEM(kept_y.shape, F32)], name=name + "_second",
        )
        return own_x, partner(away_x, "dp", 2), own_y, partner(away_y, "dp", 1)

    def third_stage(own_x, got_x, own_y, got_y, name, direct=False):
        rows = own_x.shape[1]
        columns = own_x.shape[2] + own_y.shape[2]
        if direct and outer == 4:
            shape = (1, rows, columns)
            own, *away = simple(
                direct_kernel, order, (own_x, got_x, own_y, got_y), [shaped(shape, F32)] + [shaped(shape, BF)] * (outer - 1),
                scratch=[pltpu.VMEM((outer, rows, columns), F32)], name=name + "_direct",
            )
            return [own] + [partner(item, "dp", 4 * (m + 1)) for m, item in enumerate(away)]
        shape = (half_outer, rows, columns)
        own, away = simple(
            third_kernel, order, (own_x, got_x, own_y, got_y), [shaped(shape, F32), shaped(shape, BF)],
            scratch=[pltpu.VMEM((half_outer, 2, rows, columns), F32)], name=name + "_third",
        )
        return outer_step(own, away, 0)

    up_later = second_stage(up_kept_x, up_got_x, up_kept_y, up_got_y, "up")
    half_outer = max(outer // 2, 1)
    lows = (act_own, act_x, act_y, low, low_x, low_y, low_x_swap, low_y_swap)
    piece_shape = (half_outer, hidden_rows, D)
    down_own, down_away = simple(
        down_product_kernel, order, lows, [shaped(piece_shape, F32), shaped(piece_shape, BF)],
        scratch=[pltpu.VMEM((half_outer, 2, hidden_rows, D), F32)], name="down_product",
    )

    down_later = outer_step(down_own, down_away, 0)
    (onward,) = simple(pass_on_kernel, order, (along, first_back), [shaped(along.shape, BF)], name="pass_on")
    second_back = partner(onward, "dp", 2)


    qkv_rows = 3 * D // count
    qkv_half = [shaped((outer, 2, qkv_rows + 8, HW // 2), BF), shaped((outer, 2, qkv_rows, HW // 2), BF)]

    def qkv_product(axis, at):
        return simple(
            functools.partial(qkv_product_kernel, axis, at), order, (normed, normed_prompt, local), qkv_half,
            scratch=[pltpu.VMEM((D, KEYS), BF), pltpu.VMEM((3 * D, HW // 2), BF)], name="qkv_product_" + axis,
        )

    qkv_away_x, qkv_kept_x = qkv_product("x", 0)
    qkv_got_x = partner(qkv_away_x, "dp", 1)
    qkv_away_y, qkv_kept_y = qkv_product("y", HW // 2)
    qkv_got_y = partner(qkv_away_y, "dp", 2)
    down_later = through(down_later, "down")
    up_later = third_stage(*up_later, "up")
    normed_part = call(
        grad_normed_kernel, order, (local, first_back, second_back, qkv_weight),
        [block((1, KEYS, HW), lambda c, m: (c, 0, 0)), whole(first_back.shape), whole(second_back.shape), block((1, D, HW), lambda c, m: (c, 0, 0))],
        halves, half_specs,
        grid=(3,), scratch=[pltpu.VMEM((PMAX, HW), BF), pltpu.VMEM((TOK, D), F32)], name="grad_normed",
    )
    normed_both = both(normed_part)
    qkv_later = second_stage(qkv_kept_x, qkv_got_x, qkv_kept_y, qkv_got_y, "qkv")
    input_grad, tables_first = simple(
        input_grad_kernel, order, (*normed_both, tokens, rows, grad_hidden),
        [shaped((TOK, D), BF), shaped((2, D), F32)], name="input_grad",
    )


    up_later = through(up_later, "up")
    down_rows, down_squares = simple(
        finish_kernel, order, run_out(down_later), [shaped((hidden_rows * D // 128, 128), F32), shaped((8, 128), F32)], name="finish_down"
    )
    out_rows = HW // count
    entries = 2 * SECTIONS * HW // count
    spread = []
    if entries != HW:
        selector = (jnp.arange(SECTIONS) == meta[SECTION]).astype(F32)
        tables = jnp.stack([tables_first, tables_second])
        tables = lax.dynamic_slice_in_dim(tables, mp_index * HW, HW, 2)
        whole_tables = selector[None, None, :, None] * jnp.transpose(tables, (1, 0, 2))[:, :, None, :]
        whole_tables = jnp.transpose(whole_tables.reshape(2, count, entries), (1, 0, 2)).reshape(count, 2 * entries // 128, 128)
        spread = [jnp.pad(whole_tables.astype(BF), ((0, 0), (0, out_rows - 2 * entries // 128), (0, 0)))]
    wide, tall = HW + 128, HW
    away_x, kept_x, away_y, kept_y = simple(
        out_product_kernel, order, (attended_t, hidden_low, tables_first, tables_second, *spread),
        [shaped((outer, 2, out_rows, wide), BF)] * 2 + [shaped((outer, 2, out_rows, tall), BF)] * 2,
        scratch=[pltpu.VMEM((outer, 2, 2, out_rows, wide), BF), pltpu.VMEM((outer, 2, 2, out_rows, tall), BF)],
        name="out_product",
    )
    got_x, got_y = partner(away_x, "dp", 1), partner(away_y, "dp", 2)
    up_terms = run_out(up_later)
    up_lines, up_squares = simple(finish_kernel, order, up_terms, [shaped((up_rows * HF // 128, 128), F32), shaped((8, 128), F32)], name="finish_up")

    qkv_later = third_stage(*qkv_later, "qkv", direct=True)
    out_later = second_stage(kept_x, got_x, kept_y, got_y, "out")
    (block_out,) = simple(block_out_kernel, order, (hidden, *ffn_both), [shaped((TOK, D), BF)], name="block_out")
    out_later = third_stage(*out_later, "out", direct=True)
    if len(out_later) == 2:
        out_later = run_out(through(out_later, "out"))
    qkv_terms = run_out(through(qkv_later, "qkv")) if len(qkv_later) == 2 else qkv_later

    flat = master.shape[1]
    (qkv_lines, out_lines, table_lines, squares) = simple(
        functools.partial(finish_last_kernel, len(qkv_terms)), order, (*qkv_terms, *out_later, up_squares, down_squares),
        [shaped((qkv_rows * HW // 128, 128), F32), shaped((out_rows * D // 128, 128), F32), shaped((max(2 * entries // 128, 1), 128), F32), shaped((8, 128), F32)],
        name="finish",
    )
    squares = squares + partner(squares, "mp", 1)
    squares = squares + partner(squares, "dp", 1) + partner(squares, "dp", 2) + partner(squares, "dp", 3)
    step = 4
    while step < count:
        flips = (step, 2 * step, 3 * step) if step * 4 <= count else (step,)
        squares = sum([partner(squares, "dp", flip) for flip in flips], squares)
        step *= 4 if step * 4 <= count else 2
    step_count = adam_step[0].astype(F32)
    fixes = jnp.stack([1.0 / (1.0 - jnp.power(BETA_ONE, step_count)), 1.0 / (1.0 - jnp.power(BETA_TWO, step_count))]).reshape(1, 2)
    lines = flat // 128
    rates = [D ** (-0.5), OUT_FAN ** (-0.5), D ** (-0.5), FF ** (-0.5), 0.2]
    flats = [item.reshape(lines, 128) for item in (master, first_moment, second_moment, ema_weight)]
    new_first, new_second, new_master, copy, new_ema, grad_norm = simple(
        functools.partial(adam_kernel, rates), order, (squares, fixes, qkv_lines, out_lines, up_lines, down_rows, table_lines, *flats),
        [shaped((lines, 128), F32)] * 3 + [shaped((1, flat), BF), shaped((lines, 128), F32), shaped((1, 1), F32)], name="adam", vmem=40,
    )
    return (
        block_out,
        input_grad,
        grad_norm.reshape(1),
        new_first.reshape(1, flat),
        new_second.reshape(1, flat),
        new_master.reshape(1, flat),
        copy,
        new_ema.reshape(1, flat),
    )


def solution(mesh):
    placed = (
        P("dp", None), P("dp", None), P(None, None, "mp"), P("mp", None), P(None, "mp"), P("mp", None), P(), P(),
        P("dp"), P("dp"), P("dp"), P("dp"), P(),
        P("mp", "dp"), P("mp", "dp"), P("mp", "dp"), P("mp", "dp"),
    )
    flat = P("mp", "dp")
    return jax.shard_map(
        body, mesh=mesh, in_specs=placed,
        out_specs=(P("dp", None), P("dp", None), P(), flat, flat, flat, flat, flat),
        check_vma=False,
    )
```

```python
import functools

import jax
import jax.numpy as jnp
from jax import lax
from jax.experimental import pallas as pl
from jax.experimental.pallas import tpu as pltpu
from jax.sharding import PartitionSpec as P

D = 1024
HDIM = 64
FF = 4096
SECTIONS = 8
TOK = 384
PMAX = 96
KEYS = TOK + PMAX
OUT_FAN = 2
HW = D // 2
HF = FF // 2
HEADS = HW // HDIM
CLIP_NORM = 1.0
BETA_ONE = 0.5
BETA_TWO = 0.5
WEIGHT_DECAY = 0.1
EMA_DECAY = 0.75

BF = jnp.bfloat16
F32 = jnp.float32
MP, PX, PY, PLANE, OUTER, LENGTH, SECTION = range(7)


def shaped(shape, dtype):
    return jax.ShapeDtypeStruct(shape, dtype)


def dot_nn(a, b):
    return lax.dot_general(a, b, (((1,), (0,)), ((), ())), preferred_element_type=F32)


def dot_nt(a, b):
    return lax.dot_general(a, b, (((1,), (1,)), ((), ())), preferred_element_type=F32)


def dot_tn(a, b):
    return lax.dot_general(a, b, (((0,), (0,)), ((), ())), preferred_element_type=F32)


def block(shape, index):
    return pl.BlockSpec(shape, index)


def whole(shape):
    rank = len(shape)
    return pl.BlockSpec(shape, lambda *_: (0,) * rank)


class Order:
    def __init__(self, meta):
        self.meta = meta
        self.after = []


HBM = pl.BlockSpec(memory_space=pltpu.HBM)


def fetch(source, target, sem):
    copy = pltpu.make_async_copy(source, target, sem)
    copy.start()
    return copy


def call(kernel, order, inputs, in_specs, outs, out_specs, grid=(1,), scratch=(), name=None, vmem=20):
    after, count = list(order.after), len(inputs)

    def run(meta, *refs):
        kernel(meta, *refs[:count], *refs[count + len(after) :])

    found = pl.pallas_call(
        run,
        grid_spec=pltpu.PrefetchScalarGridSpec(
            num_scalar_prefetch=1, grid=grid, in_specs=list(in_specs) + [HBM] * len(after),
            out_specs=out_specs, scratch_shapes=scratch,
        ),
        out_shape=outs,
        compiler_params=pltpu.CompilerParams(vmem_limit_bytes=vmem << 20),
        cost_estimate=pl.CostEstimate(flops=1, bytes_accessed=1, transcendentals=0),
        name=name,
    )(order.meta, *inputs, *after)
    order.after = [min(found, key=lambda item: item.size)]
    return found


def simple(kernel, order, inputs, outs, far=(), far_out=(), **kw):
    return call(
        kernel, order, inputs,
        [HBM if k in far else pl.BlockSpec(memory_space=pltpu.SMEM) if a.shape == (1,) else whole(a.shape) for k, a in enumerate(inputs)],
        outs, [HBM if k in far_out else whole(o.shape) for k, o in enumerate(outs)], **kw
    )


def unit_rows(values):
    centred = values - jnp.mean(values, axis=-1, keepdims=True)
    scale = lax.rsqrt(jnp.mean(centred * centred, axis=-1, keepdims=True) + 1e-05)
    return centred * scale, scale


def norm_back(grad, gain_row, unit, scale):
    e = gain_row * grad
    return scale * (e - jnp.mean(e, axis=-1, keepdims=True) - unit * jnp.mean(e * unit, axis=-1, keepdims=True))


def row_of(rows, which):
    return rows[which : which + 1, :]


def valid_rows(meta):
    return lax.broadcasted_iota(jnp.int32, (TOK, 1), 0) < meta[LENGTH]


def keys_ok(meta, prompt):
    at = lax.broadcasted_iota(jnp.int32, (KEYS, 1), 0)
    return at < jnp.where(at < TOK, meta[LENGTH], TOK + prompt[0])


def summed(refs):
    here, there = refs
    return here[...].astype(F32) + there[...].astype(F32)


def start_kernel(
    tokens, cotangent, gain, shift, lengths, section,
    out, low, half, meta, rows, some, whole_low, tables, read, sems,
):
    scalars = [fetch(item, read.at[k], sems.at[6 + k]) for k, item in enumerate((lengths, section))]
    copies = [fetch(tokens.at[pl.ds(0, PMAX), :], some, sems.at[0])]
    for k, (table, norm) in enumerate(((gain, 0), (shift, 0), (gain, 1), (shift, 1))):
        copies.append(fetch(table.at[norm], tables.at[k], sems.at[1 + k]))
    late = fetch(cotangent, whole_low, sems.at[5])
    dp_index, mp_index = lax.axis_index("dp"), lax.axis_index("mp")
    plane = jnp.bitwise_and(dp_index, 3)
    meta[MP] = mp_index
    meta[PX] = jnp.bitwise_and(plane, 1)
    meta[PY] = lax.shift_right_logical(plane, 1)
    meta[PLANE] = plane
    meta[OUTER] = lax.shift_right_logical(dp_index, 2)
    for copy in scalars:
        copy.wait()
    valid_count = read[0, 0]
    meta[LENGTH] = valid_count
    meta[SECTION] = read[1, 0]
    chosen = read[1, 0]
    for copy in copies:
        copy.wait()
    for k in range(4):
        rows[k : k + 1, :] = tables[k, pl.ds(chosen, 1), :]
    rows[4:, :] = jnp.zeros((4, D), F32)
    unit, _ = unit_rows(some[...].astype(F32))
    out[...] = (row_of(rows, 0) * unit + row_of(rows, 1)).astype(BF)
    late.wait()
    valid = lax.broadcasted_iota(jnp.int32, (TOK, 1), 0) < valid_count
    kept = jnp.where(valid, whole_low[...], jnp.zeros((), BF))
    low[...] = kept

    @pl.when(mp_index == 0)
    def _():
        half[...] = kept[:, :HW]

    @pl.when(mp_index == 1)
    def _():
        half[...] = kept[:, HW:]


def qkv_kernel(meta, tokens, rows, qkv, normed, projected, frames, weights, sems):
    first = fetch(tokens, frames, sems.at[3])
    copies = [fetch(qkv.at[c], weights.at[c], sems.at[c]) for c in range(3)]
    first.wait()
    unit, _ = unit_rows(frames[...].astype(F32))
    normed[...] = (row_of(rows, 0) * unit + row_of(rows, 1)).astype(BF)
    for c in range(3):
        copies[c].wait()
        projected[c] = dot_nn(normed[...], weights[c]).astype(BF)


def grad_act_kernel(meta, low, down, out, weights, sems):
    size = HF // 4
    copies = [fetch(down.at[pl.ds(t * size, size), :], weights.at[pl.ds(t * size, size), :], sems.at[t]) for t in range(4)]
    for t in range(4):
        copies[t].wait()
        out[:, t * size : (t + 1) * size] = dot_nt(low[...], weights[t * size : (t + 1) * size, :]).astype(BF)


def attend_kernel(
    meta, projected, rows_x, rows_y, rows_far, qkv, out_weight, low_half, low_x, source, prompt,
    normed_prompt, prompt_pair, attended_t, log_total, part, joined, keys, values, values_t, weights, out_w, sems,
):
    copies = [fetch(qkv.at[c], weights.at[c - 1], sems.at[c - 1]) for c in (1, 2)]
    last = fetch(out_weight, out_w, sems.at[2])
    joined[0] = low_half[...]
    joined[1] = low_x[...]
    keys[:TOK] = projected[1]
    values[:TOK] = projected[2]
    relative = jnp.bitwise_xor(jnp.bitwise_and(source[0], 3), meta[PLANE])
    for k, rows in ((1, rows_x), (2, rows_y), (3, rows_far)):

        @pl.when(relative == k)
        def _(rows=rows):
            normed_prompt[...] = rows[...]

    rows = normed_prompt[...]
    copies[0].wait()
    pair_k = dot_nn(rows, weights[0]).astype(BF)
    copies[1].wait()
    pair_v = dot_nn(rows, weights[1]).astype(BF)
    prompt_pair[0] = pair_k
    prompt_pair[1] = pair_v
    keys[TOK:] = pair_k
    values[TOK:] = pair_v
    values_t[...] = values[...].T
    counted = keys_ok(meta, prompt)
    lane = lax.broadcasted_iota(jnp.int32, (1, 2 * HDIM), 1)
    for head in range(HEADS):
        at = (head // 2) * 2 * HDIM
        mine = jnp.where((lane // HDIM) == head % 2, HDIM ** (-0.5), 0.0).astype(BF)
        query = projected[0, :, at : at + 2 * HDIM] * mine
        scores = jnp.where(counted, dot_nt(keys[:, at : at + 2 * HDIM], query), -1e30)
        top = jnp.max(scores, axis=0, keepdims=True)
        grown = jnp.exp(scores - top)
        total = jnp.sum(grown, axis=0, keepdims=True)
        probability = (grown * (1.0 / total)).astype(BF)
        rows_at = slice(head * HDIM, (head + 1) * HDIM)
        attended_t[rows_at, :] = dot_nn(values_t[rows_at, :], probability).astype(BF)
        log_total[head : head + 1, :] = top + jnp.log(total)
    last.wait()
    part[...] = dot_tn(attended_t[...], out_w[...]).astype(BF)


TILE = 256


ERFC = (0.235325614, 0.0913858287, 0.649566092, -0.635408842, 0.886669787, -0.227538481)


def gelu_parts(values):
    decay = jnp.exp(-0.5 * values * values)
    t = 1.0 / (1.0 + (0.39 * 0.5**0.5) * jnp.abs(values))
    tail = 0.5 * ERFC[-1]
    for factor in ERFC[-2::-1]:
        tail = tail * t + 0.5 * factor
    tail = tail * t * decay
    cdf = jnp.where(values < 0.0, tail, 1.0 - tail)
    return cdf, cdf + values * (decay * (0.5 / jnp.pi) ** 0.5)


def ffn_kernel(split, meta, tokens, here, there, rows, up, grad_act, hidden, normed, *refs):
    *act, pre_low, part, pre, held, frames, weights, sems = refs
    steps = HF // TILE
    first = fetch(tokens, frames, sems.at[steps])
    copies = []

    def more(count):
        while len(copies) < min(count, steps):
            at = pl.ds(len(copies) * TILE, TILE)
            copies.append(fetch(up.at[:, at], weights.at[:, at], sems.at[len(copies)]))

    more(3)
    first.wait()
    state = frames[...].astype(F32) + summed((here, there))
    hidden[...] = state
    unit, _ = unit_rows(state)
    normed[...] = (row_of(rows, 2) * unit + row_of(rows, 3)).astype(BF)
    for t in range(steps):
        copies[t].wait()
        more(t + 4)
        at = slice(t * TILE, (t + 1) * TILE)
        pre[:, at] = dot_nn(normed[...], weights[:, at])
    across = split or 128

    def block_of_rows(r, _):
        some = pl.ds(pl.multiple_of(r * 64, 64), 64)
        for t in range(HF // across):
            at = slice(t * across, (t + 1) * across)
            values = pre[some, at]
            cdf, slope = gelu_parts(values)
            activated = (values * cdf).astype(BF)
            if split:
                held[t % 4, some, (t // 4) * split : (t // 4 + 1) * split] = activated
            else:
                act[0][some, at] = activated
            pre_low[some, at] = (grad_act[some, at].astype(F32) * slope).astype(BF)
        return 0

    lax.fori_loop(0, TOK // 64, block_of_rows, 0)
    part[...] = dot_nt(pre_low[...], weights[...]).astype(BF)
    if split:
        for k, out in enumerate((act[0], act[1].at[0], act[2], act[1].at[1])):
            out[...] = held[jnp.bitwise_xor(meta[PLANE], k)]


def join_kernel(meta, act_x, mine, out):
    out[0] = mine[...]
    out[1] = act_x[1]


def down_kernel(split, meta, *refs):
    *act, down, part, total = refs
    step = pl.program_id(0)

    @pl.when(step == 0)
    def _():
        total[...] = jnp.zeros_like(total)

    if split:
        rows = down[...].reshape(HF // 4, D)
        piece = jnp.bitwise_xor(step, meta[PLANE])
        for k, value in enumerate((act[0], act[1].at[0], act[2], act[1].at[1])):

            @pl.when(piece == k)
            def _(value=value):
                total[...] += dot_nn(value[...], rows)

    else:
        total[...] += dot_nn(act[0][:, pl.ds(pl.multiple_of(step * (HF // 4), HF // 4), HF // 4)], down[...])

    @pl.when(step == pl.num_programs(0) - 1)
    def _():
        part[...] = total[...].astype(BF)


def block_out_kernel(meta, hidden, here, there, out):
    out[...] = (hidden[...] + summed((here, there))).astype(BF)


def attend_back_kernel(
    meta, here, there, hidden, rows, low, out_weight, projected, prompt_pair, log_total, source, prompt,
    local, sent, along, grad_hidden, hidden_low, tables, keys, values, keys_t, grads, query_t, out_w, sems,
):
    last = fetch(out_weight, out_w, sems.at[0])
    back = summed((here, there))
    unit, scale = unit_rows(hidden[...])
    full = low[...].astype(F32) + norm_back(back, row_of(rows, 2), unit, scale)
    grad_hidden[...] = full
    tables[0:1, :] = jnp.sum(back * unit, axis=0, keepdims=True)
    tables[1:2, :] = jnp.sum(back, axis=0, keepdims=True)
    rounded = full.astype(BF)
    hidden_low[...] = rounded
    last.wait()
    grads[...] = dot_nt(rounded, out_w[...]).astype(BF)
    keys[:TOK] = projected[1]
    keys[TOK:] = prompt_pair[0]
    values[:TOK] = projected[2]
    values[TOK:] = prompt_pair[1]
    keys_t[...] = keys[...].T
    counted = keys_ok(meta, prompt)
    lane = lax.broadcasted_iota(jnp.int32, (1, 2 * HDIM), 1)
    left = lane < HDIM
    for pair in range(HEADS // 2):
        at = pair * 2 * HDIM
        span = slice(at, at + 2 * HDIM)
        key_pair, value_pair = keys[:, span], values[:, span]
        query_pair = projected[0, :, span] * jnp.asarray(HDIM ** (-0.5), BF)
        grad_pair = grads[:, span]
        found = []
        for head in (2 * pair, 2 * pair + 1):
            mine = ((lane // HDIM) == head % 2).astype(BF)
            scores = jnp.where(counted, dot_nt(key_pair, query_pair * mine), -1e30)
            probability = jnp.exp(scores - log_total[head : head + 1, :])
            grad_prob = dot_nt(value_pair, grad_pair * mine)
            centre = jnp.sum(probability * grad_prob, axis=0, keepdims=True)
            grad_scores = (probability * (grad_prob - centre)).astype(BF)
            rows_at = slice(head * HDIM, (head + 1) * HDIM)
            query_t[rows_at, :] = dot_nn(keys_t[rows_at, :], grad_scores) * HDIM ** (-0.5)
            found.append((dot_nn(grad_scores, query_pair), dot_nn(probability.astype(BF), grad_pair)))
        local[1, :, span] = jnp.where(left, found[0][0], found[1][0]).astype(BF)
        local[2, :, span] = jnp.where(left, found[0][1], found[1][1]).astype(BF)
    local[0, :TOK, :] = query_t[...].T.astype(BF)
    local[0, TOK:, :] = jnp.zeros((PMAX, HW), BF)
    relative = jnp.bitwise_xor(jnp.bitwise_and(source[0], 3), meta[PLANE])
    for c in range(2):
        prompt = local[1 + c, TOK:, :]
        for j in range(2):
            sent[j, c] = jnp.where(relative == 1 + 2 * j, prompt, jnp.zeros((), BF))
        along[c] = jnp.where(relative == 2, prompt, jnp.zeros((), BF))


def pass_on_kernel(meta, along, got, out):
    out[...] = (along[...].astype(F32) + got[1].astype(F32)).astype(BF)


def grad_normed_kernel(meta, local, first, second, qkv, part, returned_low, total):
    c = pl.program_id(0)

    @pl.when(c == 0)
    def _():
        total[...] = jnp.zeros_like(total)

    total[...] += dot_nt(local[0, :TOK, :], qkv[0])

    @pl.when(c > 0)
    def _():
        at = c - 1
        returned = first[0, at].astype(F32) + second[at].astype(F32)
        returned_low[...] = returned.astype(BF)
        total[:PMAX, :] += dot_nt(returned_low[...], qkv[0])

    @pl.when(c == 2)
    def _():
        part[...] = total[...].astype(BF)


def input_grad_kernel(meta, here, there, tokens, rows, grad_hidden, out, tables):
    back = summed((here, there))
    unit, scale = unit_rows(tokens[...].astype(F32))
    out[...] = (grad_hidden[...] + norm_back(back, row_of(rows, 0), unit, scale)).astype(BF)
    tables[0:1, :] = jnp.sum(back * unit, axis=0, keepdims=True)
    tables[1:2, :] = jnp.sum(back, axis=0, keepdims=True)


def part_out(out, at, whole_ref, axis, side):
    if axis == "x":
        out[..., at] = whole_ref[:, :, side]
    else:
        out[..., at] = whole_ref[:, side]


def pick(held, axis, side):
    return held[:, :, side] if axis == "x" else held[:, side]


def up_product_kernel(axis, at, meta, normed, pre_low, away, kept, held):
    held[...] = dot_tn(normed[...], pre_low[:, at : at + D]).astype(BF).reshape(held.shape)
    side = meta[PX] if axis == "x" else meta[PY]
    away[...] = pick(held, axis, 1 - side)
    kept[...] = pick(held, axis, side)


def down_product_kernel(meta, mine, act_x, act_y, low, low_x, low_y, swap_x, swap_y, own, away, held):
    here = pl.ds(pl.multiple_of(meta[MP] * HW, HW), HW)
    there = pl.ds(pl.multiple_of((1 - meta[MP]) * HW, HW), HW)
    for at, x, y in ((here, low_x, low_y), (there, swap_x, swap_y)):
        found = dot_tn(mine[...], low[:, at])
        found += dot_tn(act_x[0], x[...])
        found += dot_tn(act_y[0], y[0])
        found += dot_tn(act_y[1], y[1])
        held[:, :, :, at] = found.reshape(held.shape[:3] + (HW,))
    side = lax.rem(meta[OUTER], 2)
    own[...] = held[:, side]
    away[...] = held[:, 1 - side].astype(BF)


def qkv_product_kernel(axis, at, meta, normed, normed_prompt, local, away, kept, normed_t, held):
    normed_t[:, :TOK] = normed[...].T
    normed_t[:, TOK:] = normed_prompt[...].T
    outer, _, rows, columns = kept.shape
    for c in range(3):
        held[c * D : (c + 1) * D, :] = dot_nn(normed_t[...], local[c, :, at : at + columns]).astype(BF)
    parts = held.reshape(outer, 2, 2, rows, columns)
    side = meta[PX] if axis == "x" else meta[PY]
    away[:, :, :rows] = pick(parts, axis, 1 - side)
    kept[...] = pick(parts, axis, side)


def tables_of(meta, block_index, first, second):
    ref = (first, second)[block_index // SECTIONS]
    mine = ref[:, pl.ds(pl.multiple_of(meta[MP] * HW, HW), HW)]
    mine = jnp.where(meta[SECTION] == block_index % SECTIONS, mine, 0.0)
    return jnp.concatenate([mine[k : k + 1, 128 * c : 128 * (c + 1)] for k in range(2) for c in range(HW // 128)], axis=0)


def out_product_kernel(meta, attended_t, hidden_low, first, second, *refs):
    *spread, away_x, kept_x, away_y, kept_y, held_x, held_y = refs
    out_product(meta, attended_t, hidden_low, first, second, spread, away_x, kept_x, away_y, kept_y, held_x, held_y)


def out_product(meta, attended_t, hidden_low, first, second, spread, away_x, kept_x, away_y, kept_y, held_x, held_y):
    found = dot_nn(attended_t[...], hidden_low[...]).astype(BF)
    rows = held_x.shape[3]
    held_x[..., :HW] = found[:, :HW].reshape(held_x.shape[:3] + (rows, HW))
    if spread:
        held_x[..., HW:] = spread[0][...].reshape(held_x.shape[:3] + (rows, 128))
    else:
        for k in range(4 * held_x.shape[0]):
            entries = tables_of(meta, k, first, second)
            entries = jnp.concatenate([entries, jnp.zeros((rows - entries.shape[0], 128), F32)], axis=0)
            held_x[k // 4, (k // 2) % 2, k % 2, :, HW:] = entries.astype(BF)
    held_y[...] = found[:, HW:].reshape(held_y.shape)
    away_x[...] = held_x[:, :, 1 - meta[PX]]
    kept_x[...] = held_x[:, :, meta[PX]]
    away_y[...] = held_y[:, 1 - meta[PY]]
    kept_y[...] = held_y[:, meta[PY]]


def second_kernel(meta, kept_x, got_x, kept_y, got_y, away_x, own_x, away_y, own_y, held_x, held_y):
    rows = kept_x.shape[2]
    held_x[...] = kept_x[...].astype(F32) + got_x[:, :, :rows].astype(F32)
    held_y[...] = kept_y[...].astype(F32) + got_y[:, :, :rows].astype(F32)
    away_x[...] = held_x[:, 1 - meta[PY]].astype(BF)
    own_x[...] = held_x[:, meta[PY]].astype(BF)
    away_y[...] = held_y[:, 1 - meta[PX]].astype(BF)
    own_y[...] = held_y[:, meta[PX]].astype(BF)


def third_kernel(meta, kept_x, got_x, kept_y, got_y, own, away, held):
    left = kept_x.shape[-1]
    shape = held.shape[:2] + kept_x.shape[1:]
    held[..., :left] = (kept_x[...].astype(F32) + got_x[...].astype(F32)).reshape(shape)
    shape = held.shape[:2] + kept_y.shape[1:]
    held[..., left:] = (kept_y[...].astype(F32) + got_y[...].astype(F32)).reshape(shape)
    side = lax.rem(meta[OUTER], 2)
    own[...] = held[:, side]
    away[...] = held[:, 1 - side].astype(BF)


def direct_kernel(meta, kept_x, got_x, kept_y, got_y, own, *refs):
    *away, held = refs
    left = kept_x.shape[-1]
    held[..., :left] = kept_x[...].astype(F32) + got_x[...].astype(F32)
    held[..., left:] = kept_y[...].astype(F32) + got_y[...].astype(F32)
    own[0] = held[meta[OUTER]]
    for m, out in enumerate(away):
        out[0] = held[jnp.bitwise_xor(meta[OUTER], m + 1)].astype(BF)


def halve_kernel(bit, meta, kept, got, own, away, held):
    held[...] = (kept[...] + got[...].astype(F32)).reshape(held.shape)
    side = lax.rem(lax.shift_right_logical(meta[OUTER], bit), 2)
    own[...] = held[:, side]
    away[...] = held[:, 1 - side].astype(BF)


def to_rows(out, at, value):
    rows, columns = value.shape
    across = columns // 128
    for j in range(across):
        piece = value[:, 128 * j : 128 * (j + 1)]
        if across == 1:
            out[at : at + rows, :] = piece
        else:
            out[pl.ds(at + j, rows, stride=across), :] = piece


def total_of(terms):
    value = terms[0][0]
    for got in terms[1:]:
        value = value + got[0].astype(F32)
    return value


def square_sum(values):
    total = jnp.zeros((1, 128), F32)
    for value in values:
        line = jnp.sum(value * value, axis=0, keepdims=True)
        for j in range(value.shape[1] // 128):
            total = total + line[:, 128 * j : 128 * (j + 1)]
    return jnp.sum(total, axis=1, keepdims=True)


def finish_kernel(meta, *refs):
    *ins, out, squares = refs
    value = total_of(ins)
    to_rows(out, 0, value)
    squares[...] = jnp.broadcast_to(square_sum([value]), squares.shape)


def finish_last_kernel(first, meta, *refs):
    *ins, up_squares, down_squares, qkv_out, out_out, table_out, squares = refs
    value = total_of(ins[:first])
    to_rows(qkv_out, 0, value)
    both = total_of(ins[first:])
    tables = both[:, HW : HW + 128]
    third = jnp.concatenate([both[:, :HW], both[:, HW + 128 :]], axis=1)
    to_rows(out_out, 0, third)
    table_out[...] = tables[: table_out.shape[0], :]
    squares[...] = square_sum([value, third, tables]) + up_squares[...] + down_squares[...]


def adam_kernel(rates, meta, squares, fixes, *refs):
    pieces, (master, first, second, ema, new_first, new_second, new_master, copy, new_ema, norm) = refs[: len(rates)], refs[len(rates) :]
    norm[...] = jnp.sqrt(squares[0:1, 0:1])
    clip = jnp.minimum(1.0, CLIP_NORM / (norm[...] + 1e-06))
    one, two = fixes[0:1, 0:1], fixes[0:1, 1:2]
    start = 0
    for piece, rate in zip(pieces, rates):
        rows = piece.shape[0]
        step = next(n for n in (256, 128, 64, 32, 16, 8, 4, 2, 1) if rows % n == 0)

        def one_chunk(k, _, piece=piece, rate=rate, start=start, step=step):
            at = pl.ds(start + k * step, step)
            clipped = clip * piece[pl.ds(k * step, step), :]
            moment = BETA_ONE * first[at, :] + (1.0 - BETA_ONE) * clipped
            square = BETA_TWO * second[at, :] + (1.0 - BETA_TWO) * clipped * clipped
            new_first[at, :] = moment
            new_second[at, :] = square
            update = (moment * one) / (jnp.sqrt(square * two) + 1e-08)
            old = master[at, :]
            weights = old - rate * (update + WEIGHT_DECAY * old)
            new_master[at, :] = weights
            new_ema[at, :] = EMA_DECAY * ema[at, :] + (1.0 - EMA_DECAY) * weights
            return 0

        lax.fori_loop(0, rows // step, one_chunk, 0)
        start += rows
    copy[...] = new_master[...].astype(BF).reshape(copy.shape)


def partner(value, axis, flip):
    count = lax.axis_size(axis)
    return lax.ppermute(value, axis, [(i, i ^ flip) for i in range(count)])


def body(
    tokens, cotangent, qkv_weight, out_weight, up_weight, down_weight, norm_gain, norm_shift,
    lengths, prompt_src, prompt_len, codebook_section, adam_step, master, first_moment, second_moment, ema_weight,
):
    count = lax.axis_size("dp")
    outer = count // 4

    prompt_rows, low, low_half, meta, rows = pl.pallas_call(
        start_kernel,
        in_specs=[HBM] * 6,
        out_specs=[pl.BlockSpec(memory_space=pltpu.VMEM)] * 3 + [pl.BlockSpec(memory_space=pltpu.SMEM), pl.BlockSpec(memory_space=pltpu.VMEM)],
        scratch_shapes=[
            pltpu.VMEM((PMAX, D), BF), pltpu.VMEM((TOK, D), BF), pltpu.VMEM((4, SECTIONS, D), F32),
            pltpu.SMEM((2, 1), jnp.int32), pltpu.SemaphoreType.DMA((8,)),
        ],
        out_shape=[shaped((PMAX, D), BF), shaped((TOK, D), BF), shaped((TOK, HW), BF), shaped((7,), jnp.int32), shaped((8, D), F32)],
        compiler_params=pltpu.CompilerParams(vmem_limit_bytes=60 << 20),
        cost_estimate=pl.CostEstimate(flops=1, bytes_accessed=1, transcendentals=0),
        name="start",
    )(tokens, cotangent, norm_gain, norm_shift, lengths, codebook_section)
    order = Order(meta)
    plane, mp_index = meta[PLANE], meta[MP]
    rows_from = [partner(prompt_rows, "dp", k) for k in (1, 2, 3)]
    low_x = partner(low_half, "dp", 1)
    normed, projected = simple(
        qkv_kernel, order, (tokens, rows, qkv_weight), [shaped((TOK, D), BF), shaped((3, TOK, HW), BF)], far=(0, 2),
        scratch=[pltpu.VMEM((TOK, D), BF), pltpu.VMEM((3, D, HW), BF), pltpu.SemaphoreType.DMA((4,))], name="qkv",
    )
    hidden_rows = HF // count
    split = hidden_rows if hidden_rows % 128 == 0 else 0
    (grad_act,) = simple(
        grad_act_kernel, order, (low, down_weight), [shaped((TOK, HF), BF)], far=(1,),
        scratch=[pltpu.VMEM((HF, D), BF), pltpu.SemaphoreType.DMA((4,))], name="grad_act",
    )
    halves = [shaped((TOK, D), BF)]
    half_specs = [whole((TOK, D))]

    def both(parts):
        return (*parts, *[partner(item, "mp", 1) for item in parts])

    normed_prompt, prompt_pair, attended_t, log_total, mixed, joined = simple(
        attend_kernel, order, (projected, *rows_from, qkv_weight, out_weight, low_half, low_x, prompt_src, prompt_len),
        [shaped((PMAX, D), BF), shaped((2, PMAX, HW), BF), shaped((HW, TOK), BF), shaped((HEADS, TOK), F32), *halves, shaped((2, TOK, HW), BF)],
        scratch=[pltpu.VMEM((KEYS, HW), BF), pltpu.VMEM((KEYS, HW), BF), pltpu.VMEM((HW, KEYS), BF),
            pltpu.VMEM((2, D, HW), BF), pltpu.VMEM((HW, D), BF), pltpu.SemaphoreType.DMA((3,))],
        far=(4, 5), name="attend",
    )
    mixed = both((mixed,))
    low_y = partner(joined, "dp", 2)
    low_x_swap = partner(lax.optimization_barrier((low_x, mixed[0]))[0], "mp", 1)
    pieces = 4 if split else 1
    act_shape = (TOK, HF // pieces)
    act_shapes = [shaped(act_shape, BF), shaped((2, *act_shape), BF), shaped(act_shape, BF)] if split else [shaped(act_shape, BF)]
    hidden, normed_second, *act, pre_low, second_part = simple(
        functools.partial(ffn_kernel, split), order, (tokens, *mixed, rows, up_weight, grad_act),
        [shaped((TOK, D), F32), shaped((TOK, D), BF)] + act_shapes + [shaped((TOK, HF), BF), *halves],
        scratch=[pltpu.VMEM((TOK, HF), F32), pltpu.VMEM((pieces, TOK, HF // pieces), BF), pltpu.VMEM((TOK, D), BF), pltpu.VMEM((D, HF), BF), pltpu.SemaphoreType.DMA((HF // TILE + 1,))],
        far=(0, 4), name="ffn",
    )
    second = both((second_part,))

    if split:
        act_own, act_pair, act_side = act
    else:
        cut = act[0].reshape(TOK, outer, 4, hidden_rows)
        act_own, side_x, act_side, far = [
            lax.dynamic_index_in_dim(cut, plane ^ k, 2, keepdims=False).reshape(TOK, HF // 4) for k in range(4)
        ]
        act_pair = jnp.stack([side_x, far])
    act_x = partner(act_pair, "dp", 1)

    up_rows = D // count
    up_half = [shaped((outer, 2, up_rows, D), BF)] * 2

    def up_product(axis, at):
        return simple(
            functools.partial(up_product_kernel, axis, at), order, (normed_second, pre_low), up_half,
            scratch=[pltpu.VMEM((outer, 2, 2, up_rows, D), BF)], name="up_product_" + axis,
        )

    up_away_x, up_kept_x = up_product("x", 0)
    up_got_x = partner(up_away_x, "dp", 1)
    low_y_swap = partner(lax.optimization_barrier((low_y, up_away_x))[0], "mp", 1)
    up_away_y, up_kept_y = up_product("y", D)
    up_got_y = partner(up_away_y, "dp", 2)

    local, sent, along, grad_hidden, hidden_low, tables_second = simple(
        attend_back_kernel, order,
        (*second, hidden, rows, low, out_weight, projected, prompt_pair, log_total, prompt_src, prompt_len),
        [shaped((3, KEYS, HW), BF), shaped((2, 2, PMAX, HW), BF), shaped((2, PMAX, HW), BF), shaped((TOK, D), F32), shaped((TOK, D), BF), shaped((2, D), F32)],
        scratch=[pltpu.VMEM((KEYS, HW), BF), pltpu.VMEM((KEYS, HW), BF), pltpu.VMEM((HW, KEYS), BF), pltpu.VMEM((TOK, HW), BF), pltpu.VMEM((HW, TOK), F32),
            pltpu.VMEM((HW, D), BF), pltpu.SemaphoreType.DMA((1,))],
        far=(5,), name="attend_back",
    )
    first_back = partner(sent, "dp", 1)
    (act_onward,) = simple(join_kernel, order, (act_x, act_side), [shaped(act_x.shape, BF)], name="join")
    act_y = partner(act_onward, "dp", 2)

    if split:
        down_in, down_spec = down_weight.reshape(outer, 4, hidden_rows, D), block((outer, None, hidden_rows, D), lambda t, m: (0, t, 0, 0))
    else:
        down_in, down_spec = down_weight, block((HF // 4, D), lambda t, m: (t, 0))
    ffn_part = call(
        functools.partial(down_kernel, split), order, (*act, down_in), [whole(item.shape) for item in act] + [down_spec],
        halves, half_specs, grid=(4,), scratch=[pltpu.VMEM((TOK, D), F32)], name="down",
    )
    ffn_both = both(ffn_part)


    def outer_step(own, away, bit):
        return own, partner(away, "dp", 4 << bit)

    def through(state, name):
        own, got = state
        bit = 0
        while own.shape[0] > 1:
            bit += 1
            left = own.shape[0] // 2
            shape = (left,) + own.shape[1:]
            own, away = simple(
                functools.partial(halve_kernel, bit), order, (own, got), [shaped(shape, F32), shaped(shape, BF)],
                scratch=[pltpu.VMEM((left, 2) + own.shape[1:], F32)], name=name + "_halve",
            )
            own, got = outer_step(own, away, bit)
        return own, got

    def run_out(state):
        return list(state)

    def second_stage(kept_x, got_x, kept_y, got_y, name):
        _, _, rows, wide = kept_x.shape
        tall = kept_y.shape[-1]
        outs = [shaped((outer, rows, wide), BF)] * 2 + [shaped((outer, rows, tall), BF)] * 2
        away_x, own_x, away_y, own_y = simple(
            second_kernel, order, (kept_x, got_x, kept_y, got_y), outs,
            scratch=[pltpu.VMEM(kept_x.shape, F32), pltpu.VMEM(kept_y.shape, F32)], name=name + "_second",
        )
        return own_x, partner(away_x, "dp", 2), own_y, partner(away_y, "dp", 1)

    def third_stage(own_x, got_x, own_y, got_y, name, direct=False):
        rows = own_x.shape[1]
        columns = own_x.shape[2] + own_y.shape[2]
        if direct and outer == 4:
            shape = (1, rows, columns)
            own, *away = simple(
                direct_kernel, order, (own_x, got_x, own_y, got_y), [shaped(shape, F32)] + [shaped(shape, BF)] * (outer - 1),
                scratch=[pltpu.VMEM((outer, rows, columns), F32)], name=name + "_direct",
            )
            return [own] + [partner(item, "dp", 4 * (m + 1)) for m, item in enumerate(away)]
        shape = (half_outer, rows, columns)
        own, away = simple(
            third_kernel, order, (own_x, got_x, own_y, got_y), [shaped(shape, F32), shaped(shape, BF)],
            scratch=[pltpu.VMEM((half_outer, 2, rows, columns), F32)], name=name + "_third",
        )
        return outer_step(own, away, 0)

    up_later = second_stage(up_kept_x, up_got_x, up_kept_y, up_got_y, "up")
    half_outer = max(outer // 2, 1)
    lows = (act_own, act_x, act_y, low, low_x, low_y, low_x_swap, low_y_swap)
    piece_shape = (half_outer, hidden_rows, D)
    down_own, down_away = simple(
        down_product_kernel, order, lows, [shaped(piece_shape, F32), shaped(piece_shape, BF)],
        scratch=[pltpu.VMEM((half_outer, 2, hidden_rows, D), F32)], name="down_product",
    )

    down_later = outer_step(down_own, down_away, 0)
    (onward,) = simple(pass_on_kernel, order, (along, first_back), [shaped(along.shape, BF)], name="pass_on")
    second_back = partner(onward, "dp", 2)


    qkv_rows = 3 * D // count
    qkv_half = [shaped((outer, 2, qkv_rows + 8, HW // 2), BF), shaped((outer, 2, qkv_rows, HW // 2), BF)]

    def qkv_product(axis, at):
        return simple(
            functools.partial(qkv_product_kernel, axis, at), order, (normed, normed_prompt, local), qkv_half,
            scratch=[pltpu.VMEM((D, KEYS), BF), pltpu.VMEM((3 * D, HW // 2), BF)], name="qkv_product_" + axis,
        )

    qkv_away_x, qkv_kept_x = qkv_product("x", 0)
    qkv_got_x = partner(qkv_away_x, "dp", 1)
    qkv_away_y, qkv_kept_y = qkv_product("y", HW // 2)
    qkv_got_y = partner(qkv_away_y, "dp", 2)
    down_later = through(down_later, "down")
    up_later = third_stage(*up_later, "up")
    normed_part = call(
        grad_normed_kernel, order, (local, first_back, second_back, qkv_weight),
        [block((1, KEYS, HW), lambda c, m: (c, 0, 0)), whole(first_back.shape), whole(second_back.shape), block((1, D, HW), lambda c, m: (c, 0, 0))],
        halves, half_specs,
        grid=(3,), scratch=[pltpu.VMEM((PMAX, HW), BF), pltpu.VMEM((TOK, D), F32)], name="grad_normed",
    )
    normed_both = both(normed_part)
    qkv_later = second_stage(qkv_kept_x, qkv_got_x, qkv_kept_y, qkv_got_y, "qkv")
    input_grad, tables_first = simple(
        input_grad_kernel, order, (*normed_both, tokens, rows, grad_hidden),
        [shaped((TOK, D), BF), shaped((2, D), F32)], name="input_grad",
    )


    up_later = through(up_later, "up")
    (block_out,) = simple(block_out_kernel, order, (hidden, *ffn_both), [shaped((TOK, D), BF)], name="block_out")
    out_rows = HW // count
    entries = 2 * SECTIONS * HW // count
    spread = []
    if entries != HW:
        selector = (jnp.arange(SECTIONS) == meta[SECTION]).astype(F32)
        tables = jnp.stack([tables_first, tables_second])
        tables = lax.dynamic_slice_in_dim(tables, mp_index * HW, HW, 2)
        whole_tables = selector[None, None, :, None] * jnp.transpose(tables, (1, 0, 2))[:, :, None, :]
        whole_tables = jnp.transpose(whole_tables.reshape(2, count, entries), (1, 0, 2)).reshape(count, 2 * entries // 128, 128)
        spread = [jnp.pad(whole_tables.astype(BF), ((0, 0), (0, out_rows - 2 * entries // 128), (0, 0)))]
    wide, tall = HW + 128, HW
    away_x, kept_x, away_y, kept_y = simple(
        out_product_kernel, order, (attended_t, hidden_low, tables_first, tables_second, *spread),
        [shaped((outer, 2, out_rows, wide), BF)] * 2 + [shaped((outer, 2, out_rows, tall), BF)] * 2,
        scratch=[pltpu.VMEM((outer, 2, 2, out_rows, wide), BF), pltpu.VMEM((outer, 2, 2, out_rows, tall), BF)],
        name="out_product",
    )
    got_x, got_y = partner(away_x, "dp", 1), partner(away_y, "dp", 2)
    up_terms = run_out(up_later)
    up_lines, up_squares = simple(finish_kernel, order, up_terms, [shaped((up_rows * HF // 128, 128), F32), shaped((8, 128), F32)], name="finish_up")

    qkv_later = third_stage(*qkv_later, "qkv", direct=True)
    out_later = second_stage(kept_x, got_x, kept_y, got_y, "out")
    down_rows, down_squares = simple(
        finish_kernel, order, run_out(down_later), [shaped((hidden_rows * D // 128, 128), F32), shaped((8, 128), F32)], name="finish_down"
    )
    out_later = third_stage(*out_later, "out", direct=True)
    if len(out_later) == 2:
        out_later = run_out(through(out_later, "out"))
    qkv_terms = run_out(through(qkv_later, "qkv")) if len(qkv_later) == 2 else qkv_later

    flat = master.shape[1]
    (qkv_lines, out_lines, table_lines, squares) = simple(
        functools.partial(finish_last_kernel, len(qkv_terms)), order, (*qkv_terms, *out_later, up_squares, down_squares),
        [shaped((qkv_rows * HW // 128, 128), F32), shaped((out_rows * D // 128, 128), F32), shaped((max(2 * entries // 128, 1), 128), F32), shaped((8, 128), F32)],
        name="finish",
    )
    squares = squares + partner(squares, "mp", 1)
    squares = squares + partner(squares, "dp", 1) + partner(squares, "dp", 2) + partner(squares, "dp", 3)
    step = 4
    while step < count:
        flips = (step, 2 * step, 3 * step) if step * 4 <= count else (step,)
        squares = sum([partner(squares, "dp", flip) for flip in flips], squares)
        step *= 4 if step * 4 <= count else 2
    step_count = adam_step[0].astype(F32)
    fixes = jnp.stack([1.0 / (1.0 - jnp.power(BETA_ONE, step_count)), 1.0 / (1.0 - jnp.power(BETA_TWO, step_count))]).reshape(1, 2)
    lines = flat // 128
    rates = [D ** (-0.5), OUT_FAN ** (-0.5), D ** (-0.5), FF ** (-0.5), 0.2]
    flats = [item.reshape(lines, 128) for item in (master, first_moment, second_moment, ema_weight)]
    new_first, new_second, new_master, copy, new_ema, grad_norm = simple(
        functools.partial(adam_kernel, rates), order, (squares, fixes, qkv_lines, out_lines, up_lines, down_rows, table_lines, *flats),
        [shaped((lines, 128), F32)] * 3 + [shaped((1, flat), BF), shaped((lines, 128), F32), shaped((1, 1), F32)], name="adam", vmem=40,
    )
    return (
        block_out,
        input_grad,
        grad_norm.reshape(1),
        new_first.reshape(1, flat),
        new_second.reshape(1, flat),
        new_master.reshape(1, flat),
        copy,
        new_ema.reshape(1, flat),
    )


def solution(mesh):
    placed = (
        P("dp", None), P("dp", None), P(None, None, "mp"), P("mp", None), P(None, "mp"), P("mp", None), P(), P(),
        P("dp"), P("dp"), P("dp"), P("dp"), P(),
        P("mp", "dp"), P("mp", "dp"), P("mp", "dp"), P("mp", "dp"),
    )
    flat = P("mp", "dp")
    return jax.shard_map(
        body, mesh=mesh, in_specs=placed,
        out_specs=(P("dp", None), P("dp", None), P(), flat, flat, flat, flat, flat),
        check_vma=False,
    )
```

```python
import functools

import jax
import jax.numpy as jnp
from jax import lax
from jax.experimental import pallas as pl
from jax.experimental.pallas import tpu as pltpu
from jax.sharding import PartitionSpec as P

D = 1024
HDIM = 64
FF = 4096
SECTIONS = 8
TOK = 384
PMAX = 96
KEYS = TOK + PMAX
OUT_FAN = 2
HW = D // 2
HF = FF // 2
HEADS = HW // HDIM
CLIP_NORM = 1.0
BETA_ONE = 0.5
BETA_TWO = 0.5
WEIGHT_DECAY = 0.1
EMA_DECAY = 0.75

BF = jnp.bfloat16
F32 = jnp.float32
MP, PX, PY, PLANE, OUTER, LENGTH, SECTION = range(7)


def shaped(shape, dtype):
    return jax.ShapeDtypeStruct(shape, dtype)


def dot_nn(a, b):
    return lax.dot_general(a, b, (((1,), (0,)), ((), ())), preferred_element_type=F32)


def dot_nt(a, b):
    return lax.dot_general(a, b, (((1,), (1,)), ((), ())), preferred_element_type=F32)


def dot_tn(a, b):
    return lax.dot_general(a, b, (((0,), (0,)), ((), ())), preferred_element_type=F32)


def block(shape, index):
    return pl.BlockSpec(shape, index)


def whole(shape):
    rank = len(shape)
    return pl.BlockSpec(shape, lambda *_: (0,) * rank)


class Order:
    def __init__(self, meta):
        self.meta = meta
        self.after = []


HBM = pl.BlockSpec(memory_space=pltpu.HBM)


def fetch(source, target, sem):
    copy = pltpu.make_async_copy(source, target, sem)
    copy.start()
    return copy


def call(kernel, order, inputs, in_specs, outs, out_specs, grid=(1,), scratch=(), name=None, vmem=20):
    after, count = list(order.after), len(inputs)

    def run(meta, *refs):
        kernel(meta, *refs[:count], *refs[count + len(after) :])

    found = pl.pallas_call(
        run,
        grid_spec=pltpu.PrefetchScalarGridSpec(
            num_scalar_prefetch=1, grid=grid, in_specs=list(in_specs) + [HBM] * len(after),
            out_specs=out_specs, scratch_shapes=scratch,
        ),
        out_shape=outs,
        compiler_params=pltpu.CompilerParams(vmem_limit_bytes=vmem << 20),
        cost_estimate=pl.CostEstimate(flops=1, bytes_accessed=1, transcendentals=0),
        name=name,
    )(order.meta, *inputs, *after)
    order.after = [min(found, key=lambda item: item.size)]
    return found


def simple(kernel, order, inputs, outs, far=(), far_out=(), **kw):
    return call(
        kernel, order, inputs,
        [HBM if k in far else pl.BlockSpec(memory_space=pltpu.SMEM) if a.shape == (1,) else whole(a.shape) for k, a in enumerate(inputs)],
        outs, [HBM if k in far_out else whole(o.shape) for k, o in enumerate(outs)], **kw
    )


def unit_rows(values):
    centred = values - jnp.mean(values, axis=-1, keepdims=True)
    scale = lax.rsqrt(jnp.mean(centred * centred, axis=-1, keepdims=True) + 1e-05)
    return centred * scale, scale


def norm_back(grad, gain_row, unit, scale):
    e = gain_row * grad
    return scale * (e - jnp.mean(e, axis=-1, keepdims=True) - unit * jnp.mean(e * unit, axis=-1, keepdims=True))


def row_of(rows, which):
    return rows[which : which + 1, :]


def valid_rows(meta):
    return lax.broadcasted_iota(jnp.int32, (TOK, 1), 0) < meta[LENGTH]


def keys_ok(meta, prompt):
    at = lax.broadcasted_iota(jnp.int32, (KEYS, 1), 0)
    return at < jnp.where(at < TOK, meta[LENGTH], TOK + prompt[0])


def summed(refs):
    here, there = refs
    return here[...].astype(F32) + there[...].astype(F32)


def start_kernel(
    tokens, cotangent, gain, shift, lengths, section,
    out, low, half, meta, rows, some, whole_low, tables, read, sems,
):
    scalars = [fetch(item, read.at[k], sems.at[6 + k]) for k, item in enumerate((lengths, section))]
    copies = [fetch(tokens.at[pl.ds(0, PMAX), :], some, sems.at[0])]
    for k, (table, norm) in enumerate(((gain, 0), (shift, 0), (gain, 1), (shift, 1))):
        copies.append(fetch(table.at[norm], tables.at[k], sems.at[1 + k]))
    late = fetch(cotangent, whole_low, sems.at[5])
    dp_index, mp_index = lax.axis_index("dp"), lax.axis_index("mp")
    plane = jnp.bitwise_and(dp_index, 3)
    meta[MP] = mp_index
    meta[PX] = jnp.bitwise_and(plane, 1)
    meta[PY] = lax.shift_right_logical(plane, 1)
    meta[PLANE] = plane
    meta[OUTER] = lax.shift_right_logical(dp_index, 2)
    for copy in scalars:
        copy.wait()
    valid_count = read[0, 0]
    meta[LENGTH] = valid_count
    meta[SECTION] = read[1, 0]
    chosen = read[1, 0]
    for copy in copies:
        copy.wait()
    for k in range(4):
        rows[k : k + 1, :] = tables[k, pl.ds(chosen, 1), :]
    rows[4:, :] = jnp.zeros((4, D), F32)
    unit, _ = unit_rows(some[...].astype(F32))
    out[...] = (row_of(rows, 0) * unit + row_of(rows, 1)).astype(BF)
    late.wait()
    valid = lax.broadcasted_iota(jnp.int32, (TOK, 1), 0) < valid_count
    kept = jnp.where(valid, whole_low[...], jnp.zeros((), BF))
    low[...] = kept

    @pl.when(mp_index == 0)
    def _():
        half[...] = kept[:, :HW]

    @pl.when(mp_index == 1)
    def _():
        half[...] = kept[:, HW:]


def qkv_kernel(meta, tokens, rows, qkv, normed, projected, frames, weights, sems):
    first = fetch(tokens, frames, sems.at[3])
    copies = [fetch(qkv.at[c], weights.at[c], sems.at[c]) for c in range(3)]
    first.wait()
    unit, _ = unit_rows(frames[...].astype(F32))
    normed[...] = (row_of(rows, 0) * unit + row_of(rows, 1)).astype(BF)
    for c in range(3):
        copies[c].wait()
        projected[c] = dot_nn(normed[...], weights[c]).astype(BF)


def grad_act_kernel(meta, low, down, out, weights, sems):
    size = HF // 4
    copies = [fetch(down.at[pl.ds(t * size, size), :], weights.at[pl.ds(t * size, size), :], sems.at[t]) for t in range(4)]
    for t in range(4):
        copies[t].wait()
        out[:, t * size : (t + 1) * size] = dot_nt(low[...], weights[t * size : (t + 1) * size, :]).astype(BF)


def attend_kernel(
    meta, projected, rows_x, rows_y, rows_far, qkv, out_weight, low_half, low_x, source, prompt,
    normed_prompt, prompt_pair, attended_t, log_total, part, joined, keys, values, values_t, weights, out_w, sems,
):
    copies = [fetch(qkv.at[c], weights.at[c - 1], sems.at[c - 1]) for c in (1, 2)]
    last = fetch(out_weight, out_w, sems.at[2])
    joined[0] = low_half[...]
    joined[1] = low_x[...]
    keys[:TOK] = projected[1]
    values[:TOK] = projected[2]
    relative = jnp.bitwise_xor(jnp.bitwise_and(source[0], 3), meta[PLANE])
    for k, rows in ((1, rows_x), (2, rows_y), (3, rows_far)):

        @pl.when(relative == k)
        def _(rows=rows):
            normed_prompt[...] = rows[...]

    rows = normed_prompt[...]
    copies[0].wait()
    pair_k = dot_nn(rows, weights[0]).astype(BF)
    copies[1].wait()
    pair_v = dot_nn(rows, weights[1]).astype(BF)
    prompt_pair[0] = pair_k
    prompt_pair[1] = pair_v
    keys[TOK:] = pair_k
    values[TOK:] = pair_v
    values_t[...] = values[...].T
    counted = keys_ok(meta, prompt)
    lane = lax.broadcasted_iota(jnp.int32, (1, 2 * HDIM), 1)
    for head in range(HEADS):
        at = (head // 2) * 2 * HDIM
        mine = jnp.where((lane // HDIM) == head % 2, HDIM ** (-0.5), 0.0).astype(BF)
        query = projected[0, :, at : at + 2 * HDIM] * mine
        scores = jnp.where(counted, dot_nt(keys[:, at : at + 2 * HDIM], query), -1e30)
        top = jnp.max(scores, axis=0, keepdims=True)
        grown = jnp.exp(scores - top)
        total = jnp.sum(grown, axis=0, keepdims=True)
        probability = (grown * (1.0 / total)).astype(BF)
        rows_at = slice(head * HDIM, (head + 1) * HDIM)
        attended_t[rows_at, :] = dot_nn(values_t[rows_at, :], probability).astype(BF)
        log_total[head : head + 1, :] = top + jnp.log(total)
    last.wait()
    part[...] = dot_tn(attended_t[...], out_w[...]).astype(BF)


TILE = 256


ERFC = (0.235325614, 0.0913858287, 0.649566092, -0.635408842, 0.886669787, -0.227538481)


def gelu_parts(values):
    decay = jnp.exp(-0.5 * values * values)
    t = 1.0 / (1.0 + (0.39 * 0.5**0.5) * jnp.abs(values))
    tail = 0.5 * ERFC[-1]
    for factor in ERFC[-2::-1]:
        tail = tail * t + 0.5 * factor
    tail = tail * t * decay
    cdf = jnp.where(values < 0.0, tail, 1.0 - tail)
    return cdf, cdf + values * (decay * (0.5 / jnp.pi) ** 0.5)


def ffn_kernel(split, meta, tokens, here, there, rows, up, grad_act, hidden, normed, *refs):
    *act, pre_low, part, pre, held, frames, weights, sems = refs
    steps = HF // TILE
    first = fetch(tokens, frames, sems.at[steps])
    copies = []

    def more(count):
        while len(copies) < min(count, steps):
            at = pl.ds(len(copies) * TILE, TILE)
            copies.append(fetch(up.at[:, at], weights.at[:, at], sems.at[len(copies)]))

    more(3)
    first.wait()
    state = frames[...].astype(F32) + summed((here, there))
    hidden[...] = state
    unit, _ = unit_rows(state)
    normed[...] = (row_of(rows, 2) * unit + row_of(rows, 3)).astype(BF)
    for t in range(steps):
        copies[t].wait()
        more(t + 4)
        at = slice(t * TILE, (t + 1) * TILE)
        pre[:, at] = dot_nn(normed[...], weights[:, at])
    across = split or 128

    def block_of_rows(r, _):
        some = pl.ds(pl.multiple_of(r * 64, 64), 64)
        for t in range(HF // across):
            at = slice(t * across, (t + 1) * across)
            values = pre[some, at]
            cdf, slope = gelu_parts(values)
            activated = (values * cdf).astype(BF)
            if split:
                held[t % 4, some, (t // 4) * split : (t // 4 + 1) * split] = activated
            else:
                act[0][some, at] = activated
            pre_low[some, at] = (grad_act[some, at].astype(F32) * slope).astype(BF)
        return 0

    lax.fori_loop(0, TOK // 64, block_of_rows, 0)
    part[...] = dot_nt(pre_low[...], weights[...]).astype(BF)
    if split:
        for k, out in enumerate((act[0], act[1].at[0], act[2], act[1].at[1])):
            out[...] = held[jnp.bitwise_xor(meta[PLANE], k)]


def join_kernel(meta, act_x, mine, out):
    out[0] = mine[...]
    out[1] = act_x[1]


def down_kernel(split, meta, *refs):
    *act, down, part, total = refs
    step = pl.program_id(0)

    @pl.when(step == 0)
    def _():
        total[...] = jnp.zeros_like(total)

    if split:
        rows = down[...].reshape(HF // 4, D)
        piece = jnp.bitwise_xor(step, meta[PLANE])
        for k, value in enumerate((act[0], act[1].at[0], act[2], act[1].at[1])):

            @pl.when(piece == k)
            def _(value=value):
                total[...] += dot_nn(value[...], rows)

    else:
        total[...] += dot_nn(act[0][:, pl.ds(pl.multiple_of(step * (HF // 4), HF // 4), HF // 4)], down[...])

    @pl.when(step == pl.num_programs(0) - 1)
    def _():
        part[...] = total[...].astype(BF)


def block_out_kernel(meta, hidden, here, there, out):
    out[...] = (hidden[...] + summed((here, there))).astype(BF)


def attend_back_kernel(
    meta, here, there, hidden, rows, low, out_weight, projected, prompt_pair, log_total, source, prompt,
    local, sent, along, grad_hidden, hidden_low, tables, keys, values, keys_t, grads, query_t, out_w, sems,
):
    last = fetch(out_weight, out_w, sems.at[0])
    back = summed((here, there))
    unit, scale = unit_rows(hidden[...])
    full = low[...].astype(F32) + norm_back(back, row_of(rows, 2), unit, scale)
    grad_hidden[...] = full
    tables[0:1, :] = jnp.sum(back * unit, axis=0, keepdims=True)
    tables[1:2, :] = jnp.sum(back, axis=0, keepdims=True)
    rounded = full.astype(BF)
    hidden_low[...] = rounded
    last.wait()
    grads[...] = dot_nt(rounded, out_w[...]).astype(BF)
    keys[:TOK] = projected[1]
    keys[TOK:] = prompt_pair[0]
    values[:TOK] = projected[2]
    values[TOK:] = prompt_pair[1]
    keys_t[...] = keys[...].T
    counted = keys_ok(meta, prompt)
    lane = lax.broadcasted_iota(jnp.int32, (1, 2 * HDIM), 1)
    left = lane < HDIM
    for pair in range(HEADS // 2):
        at = pair * 2 * HDIM
        span = slice(at, at + 2 * HDIM)
        key_pair, value_pair = keys[:, span], values[:, span]
        query_pair = projected[0, :, span] * jnp.asarray(HDIM ** (-0.5), BF)
        grad_pair = grads[:, span]
        found = []
        for head in (2 * pair, 2 * pair + 1):
            mine = ((lane // HDIM) == head % 2).astype(BF)
            scores = jnp.where(counted, dot_nt(key_pair, query_pair * mine), -1e30)
            probability = jnp.exp(scores - log_total[head : head + 1, :])
            grad_prob = dot_nt(value_pair, grad_pair * mine)
            centre = jnp.sum(probability * grad_prob, axis=0, keepdims=True)
            grad_scores = (probability * (grad_prob - centre)).astype(BF)
            rows_at = slice(head * HDIM, (head + 1) * HDIM)
            query_t[rows_at, :] = dot_nn(keys_t[rows_at, :], grad_scores) * HDIM ** (-0.5)
            found.append((dot_nn(grad_scores, query_pair), dot_nn(probability.astype(BF), grad_pair)))
        local[1, :, span] = jnp.where(left, found[0][0], found[1][0]).astype(BF)
        local[2, :, span] = jnp.where(left, found[0][1], found[1][1]).astype(BF)
    local[0, :TOK, :] = query_t[...].T.astype(BF)
    local[0, TOK:, :] = jnp.zeros((PMAX, HW), BF)
    relative = jnp.bitwise_xor(jnp.bitwise_and(source[0], 3), meta[PLANE])
    for c in range(2):
        prompt = local[1 + c, TOK:, :]
        for j in range(2):
            sent[j, c] = jnp.where(relative == 1 + 2 * j, prompt, jnp.zeros((), BF))
        along[c] = jnp.where(relative == 2, prompt, jnp.zeros((), BF))


def pass_on_kernel(meta, along, got, out):
    out[...] = (along[...].astype(F32) + got[1].astype(F32)).astype(BF)


def grad_normed_kernel(meta, local, first, second, qkv, part, returned_low, total):
    c = pl.program_id(0)

    @pl.when(c == 0)
    def _():
        total[...] = jnp.zeros_like(total)

    total[...] += dot_nt(local[0, :TOK, :], qkv[0])

    @pl.when(c > 0)
    def _():
        at = c - 1
        returned = first[0, at].astype(F32) + second[at].astype(F32)
        returned_low[...] = returned.astype(BF)
        total[:PMAX, :] += dot_nt(returned_low[...], qkv[0])

    @pl.when(c == 2)
    def _():
        part[...] = total[...].astype(BF)


def input_grad_kernel(meta, here, there, tokens, rows, grad_hidden, out, tables):
    back = summed((here, there))
    unit, scale = unit_rows(tokens[...].astype(F32))
    out[...] = (grad_hidden[...] + norm_back(back, row_of(rows, 0), unit, scale)).astype(BF)
    tables[0:1, :] = jnp.sum(back * unit, axis=0, keepdims=True)
    tables[1:2, :] = jnp.sum(back, axis=0, keepdims=True)


def part_out(out, at, whole_ref, axis, side):
    if axis == "x":
        out[..., at] = whole_ref[:, :, side]
    else:
        out[..., at] = whole_ref[:, side]


def pick(held, axis, side):
    return held[:, :, side] if axis == "x" else held[:, side]


def up_product_kernel(axis, at, meta, normed, pre_low, away, kept, held):
    held[...] = dot_tn(normed[...], pre_low[:, at : at + D]).astype(BF).reshape(held.shape)
    side = meta[PX] if axis == "x" else meta[PY]
    away[...] = pick(held, axis, 1 - side)
    kept[...] = pick(held, axis, side)


def down_product_kernel(meta, mine, act_x, act_y, low, low_x, low_y, swap_x, swap_y, own, away, held):
    here = pl.ds(pl.multiple_of(meta[MP] * HW, HW), HW)
    there = pl.ds(pl.multiple_of((1 - meta[MP]) * HW, HW), HW)
    for at, x, y in ((here, low_x, low_y), (there, swap_x, swap_y)):
        found = dot_tn(mine[...], low[:, at])
        found += dot_tn(act_x[0], x[...])
        found += dot_tn(act_y[0], y[0])
        found += dot_tn(act_y[1], y[1])
        held[:, :, :, at] = found.reshape(held.shape[:3] + (HW,))
    side = lax.rem(meta[OUTER], 2)
    own[...] = held[:, side]
    away[...] = held[:, 1 - side].astype(BF)


def qkv_product_kernel(axis, at, meta, normed, normed_prompt, local, away, kept, normed_t, held):
    normed_t[:, :TOK] = normed[...].T
    normed_t[:, TOK:] = normed_prompt[...].T
    outer, _, rows, columns = kept.shape
    for c in range(3):
        held[c * D : (c + 1) * D, :] = dot_nn(normed_t[...], local[c, :, at : at + columns]).astype(BF)
    parts = held.reshape(outer, 2, 2, rows, columns)
    side = meta[PX] if axis == "x" else meta[PY]
    away[:, :, :rows] = pick(parts, axis, 1 - side)
    kept[...] = pick(parts, axis, side)


def tables_of(meta, block_index, first, second):
    ref = (first, second)[block_index // SECTIONS]
    mine = ref[:, pl.ds(pl.multiple_of(meta[MP] * HW, HW), HW)]
    mine = jnp.where(meta[SECTION] == block_index % SECTIONS, mine, 0.0)
    return jnp.concatenate([mine[k : k + 1, 128 * c : 128 * (c + 1)] for k in range(2) for c in range(HW // 128)], axis=0)


def out_product_kernel(meta, attended_t, hidden_low, first, second, *refs):
    *spread, away_x, kept_x, away_y, kept_y, held_x, held_y = refs
    out_product(meta, attended_t, hidden_low, first, second, spread, away_x, kept_x, away_y, kept_y, held_x, held_y)


def out_product(meta, attended_t, hidden_low, first, second, spread, away_x, kept_x, away_y, kept_y, held_x, held_y):
    found = dot_nn(attended_t[...], hidden_low[...]).astype(BF)
    rows = held_x.shape[3]
    held_x[..., :HW] = found[:, :HW].reshape(held_x.shape[:3] + (rows, HW))
    if spread:
        held_x[..., HW:] = spread[0][...].reshape(held_x.shape[:3] + (rows, 128))
    else:
        for k in range(4 * held_x.shape[0]):
            entries = tables_of(meta, k, first, second)
            entries = jnp.concatenate([entries, jnp.zeros((rows - entries.shape[0], 128), F32)], axis=0)
            held_x[k // 4, (k // 2) % 2, k % 2, :, HW:] = entries.astype(BF)
    held_y[...] = found[:, HW:].reshape(held_y.shape)
    away_x[...] = held_x[:, :, 1 - meta[PX]]
    kept_x[...] = held_x[:, :, meta[PX]]
    away_y[...] = held_y[:, 1 - meta[PY]]
    kept_y[...] = held_y[:, meta[PY]]


def second_kernel(meta, kept_x, got_x, kept_y, got_y, away_x, own_x, away_y, own_y, held_x, held_y):
    rows = kept_x.shape[2]
    held_x[...] = kept_x[...].astype(F32) + got_x[:, :, :rows].astype(F32)
    held_y[...] = kept_y[...].astype(F32) + got_y[:, :, :rows].astype(F32)
    away_x[...] = held_x[:, 1 - meta[PY]].astype(BF)
    own_x[...] = held_x[:, meta[PY]].astype(BF)
    away_y[...] = held_y[:, 1 - meta[PX]].astype(BF)
    own_y[...] = held_y[:, meta[PX]].astype(BF)


def third_kernel(meta, kept_x, got_x, kept_y, got_y, own, away, held):
    left = kept_x.shape[-1]
    shape = held.shape[:2] + kept_x.shape[1:]
    held[..., :left] = (kept_x[...].astype(F32) + got_x[...].astype(F32)).reshape(shape)
    shape = held.shape[:2] + kept_y.shape[1:]
    held[..., left:] = (kept_y[...].astype(F32) + got_y[...].astype(F32)).reshape(shape)
    side = lax.rem(meta[OUTER], 2)
    own[...] = held[:, side]
    away[...] = held[:, 1 - side].astype(BF)


def direct_kernel(meta, kept_x, got_x, kept_y, got_y, own, *refs):
    *away, held = refs
    left = kept_x.shape[-1]
    held[..., :left] = kept_x[...].astype(F32) + got_x[...].astype(F32)
    held[..., left:] = kept_y[...].astype(F32) + got_y[...].astype(F32)
    own[0] = held[meta[OUTER]]
    for m, out in enumerate(away):
        out[0] = held[jnp.bitwise_xor(meta[OUTER], m + 1)].astype(BF)


def halve_kernel(bit, meta, kept, got, own, away, held):
    held[...] = (kept[...] + got[...].astype(F32)).reshape(held.shape)
    side = lax.rem(lax.shift_right_logical(meta[OUTER], bit), 2)
    own[...] = held[:, side]
    away[...] = held[:, 1 - side].astype(BF)


def to_rows(out, at, value):
    rows, columns = value.shape
    across = columns // 128
    for j in range(across):
        piece = value[:, 128 * j : 128 * (j + 1)]
        if across == 1:
            out[at : at + rows, :] = piece
        else:
            out[pl.ds(at + j, rows, stride=across), :] = piece


def total_of(terms):
    value = terms[0][0]
    for got in terms[1:]:
        value = value + got[0].astype(F32)
    return value


def square_sum(values):
    total = jnp.zeros((1, 128), F32)
    for value in values:
        line = jnp.sum(value * value, axis=0, keepdims=True)
        for j in range(value.shape[1] // 128):
            total = total + line[:, 128 * j : 128 * (j + 1)]
    return jnp.sum(total, axis=1, keepdims=True)


def finish_kernel(meta, *refs):
    *ins, out, squares = refs
    value = total_of(ins)
    to_rows(out, 0, value)
    squares[...] = jnp.broadcast_to(square_sum([value]), squares.shape)


def finish_last_kernel(first, meta, *refs):
    *ins, up_squares, down_squares, qkv_out, out_out, table_out, squares = refs
    value = total_of(ins[:first])
    to_rows(qkv_out, 0, value)
    both = total_of(ins[first:])
    tables = both[:, HW : HW + 128]
    third = jnp.concatenate([both[:, :HW], both[:, HW + 128 :]], axis=1)
    to_rows(out_out, 0, third)
    table_out[...] = tables[: table_out.shape[0], :]
    squares[...] = square_sum([value, third, tables]) + up_squares[...] + down_squares[...]


def adam_kernel(rates, meta, squares, fixes, *refs):
    pieces, (master, first, second, ema, new_first, new_second, new_master, copy, new_ema, norm) = refs[: len(rates)], refs[len(rates) :]
    norm[...] = jnp.sqrt(squares[0:1, 0:1])
    clip = jnp.minimum(1.0, CLIP_NORM / (norm[...] + 1e-06))
    one, two = fixes[0:1, 0:1], fixes[0:1, 1:2]
    start = 0
    for piece, rate in zip(pieces, rates):
        rows = piece.shape[0]
        step = next(n for n in (256, 128, 64, 32, 16, 8, 4, 2, 1) if rows % n == 0)

        def one_chunk(k, _, piece=piece, rate=rate, start=start, step=step):
            at = pl.ds(start + k * step, step)
            clipped = clip * piece[pl.ds(k * step, step), :]
            moment = BETA_ONE * first[at, :] + (1.0 - BETA_ONE) * clipped
            square = BETA_TWO * second[at, :] + (1.0 - BETA_TWO) * clipped * clipped
            new_first[at, :] = moment
            new_second[at, :] = square
            update = (moment * one) / (jnp.sqrt(square * two) + 1e-08)
            old = master[at, :]
            weights = old - rate * (update + WEIGHT_DECAY * old)
            new_master[at, :] = weights
            new_ema[at, :] = EMA_DECAY * ema[at, :] + (1.0 - EMA_DECAY) * weights
            return 0

        lax.fori_loop(0, rows // step, one_chunk, 0)
        start += rows
    copy[...] = new_master[...].astype(BF).reshape(copy.shape)


def partner(value, axis, flip):
    count = lax.axis_size(axis)
    return lax.ppermute(value, axis, [(i, i ^ flip) for i in range(count)])


def body(
    tokens, cotangent, qkv_weight, out_weight, up_weight, down_weight, norm_gain, norm_shift,
    lengths, prompt_src, prompt_len, codebook_section, adam_step, master, first_moment, second_moment, ema_weight,
):
    count = lax.axis_size("dp")
    outer = count // 4

    prompt_rows, low, low_half, meta, rows = pl.pallas_call(
        start_kernel,
        in_specs=[HBM] * 6,
        out_specs=[pl.BlockSpec(memory_space=pltpu.VMEM)] * 3 + [pl.BlockSpec(memory_space=pltpu.SMEM), pl.BlockSpec(memory_space=pltpu.VMEM)],
        scratch_shapes=[
            pltpu.VMEM((PMAX, D), BF), pltpu.VMEM((TOK, D), BF), pltpu.VMEM((4, SECTIONS, D), F32),
            pltpu.SMEM((2, 1), jnp.int32), pltpu.SemaphoreType.DMA((8,)),
        ],
        out_shape=[shaped((PMAX, D), BF), shaped((TOK, D), BF), shaped((TOK, HW), BF), shaped((7,), jnp.int32), shaped((8, D), F32)],
        compiler_params=pltpu.CompilerParams(vmem_limit_bytes=60 << 20),
        cost_estimate=pl.CostEstimate(flops=1, bytes_accessed=1, transcendentals=0),
        name="start",
    )(tokens, cotangent, norm_gain, norm_shift, lengths, codebook_section)
    order = Order(meta)
    plane, mp_index = meta[PLANE], meta[MP]
    rows_from = [partner(prompt_rows, "dp", k) for k in (1, 2, 3)]
    low_x = partner(low_half, "dp", 1)
    normed, projected = simple(
        qkv_kernel, order, (tokens, rows, qkv_weight), [shaped((TOK, D), BF), shaped((3, TOK, HW), BF)], far=(0, 2),
        scratch=[pltpu.VMEM((TOK, D), BF), pltpu.VMEM((3, D, HW), BF), pltpu.SemaphoreType.DMA((4,))], name="qkv",
    )
    hidden_rows = HF // count
    split = hidden_rows if hidden_rows % 128 == 0 else 0
    (grad_act,) = simple(
        grad_act_kernel, order, (low, down_weight), [shaped((TOK, HF), BF)], far=(1,),
        scratch=[pltpu.VMEM((HF, D), BF), pltpu.SemaphoreType.DMA((4,))], name="grad_act",
    )
    halves = [shaped((TOK, D), BF)]
    half_specs = [whole((TOK, D))]

    def both(parts):
        return (*parts, *[partner(item, "mp", 1) for item in parts])

    normed_prompt, prompt_pair, attended_t, log_total, mixed, joined = simple(
        attend_kernel, order, (projected, *rows_from, qkv_weight, out_weight, low_half, low_x, prompt_src, prompt_len),
        [shaped((PMAX, D), BF), shaped((2, PMAX, HW), BF), shaped((HW, TOK), BF), shaped((HEADS, TOK), F32), *halves, shaped((2, TOK, HW), BF)],
        scratch=[pltpu.VMEM((KEYS, HW), BF), pltpu.VMEM((KEYS, HW), BF), pltpu.VMEM((HW, KEYS), BF),
            pltpu.VMEM((2, D, HW), BF), pltpu.VMEM((HW, D), BF), pltpu.SemaphoreType.DMA((3,))],
        far=(4, 5), name="attend",
    )
    mixed = both((mixed,))
    low_y = partner(joined, "dp", 2)
    low_x_swap = partner(lax.optimization_barrier((low_x, mixed[0]))[0], "mp", 1)
    pieces = 4 if split else 1
    act_shape = (TOK, HF // pieces)
    act_shapes = [shaped(act_shape, BF), shaped((2, *act_shape), BF), shaped(act_shape, BF)] if split else [shaped(act_shape, BF)]
    hidden, normed_second, *act, pre_low, second_part = simple(
        functools.partial(ffn_kernel, split), order, (tokens, *mixed, rows, up_weight, grad_act),
        [shaped((TOK, D), F32), shaped((TOK, D), BF)] + act_shapes + [shaped((TOK, HF), BF), *halves],
        scratch=[pltpu.VMEM((TOK, HF), F32), pltpu.VMEM((pieces, TOK, HF // pieces), BF), pltpu.VMEM((TOK, D), BF), pltpu.VMEM((D, HF), BF), pltpu.SemaphoreType.DMA((HF // TILE + 1,))],
        far=(0, 4), name="ffn",
    )
    second = both((second_part,))

    if split:
        act_own, act_pair, act_side = act
    else:
        cut = act[0].reshape(TOK, outer, 4, hidden_rows)
        act_own, side_x, act_side, far = [
            lax.dynamic_index_in_dim(cut, plane ^ k, 2, keepdims=False).reshape(TOK, HF // 4) for k in range(4)
        ]
        act_pair = jnp.stack([side_x, far])
    act_x = partner(act_pair, "dp", 1)

    up_rows = D // count
    up_half = [shaped((outer, 2, up_rows, D), BF)] * 2

    def up_product(axis, at):
        return simple(
            functools.partial(up_product_kernel, axis, at), order, (normed_second, pre_low), up_half,
            scratch=[pltpu.VMEM((outer, 2, 2, up_rows, D), BF)], name="up_product_" + axis,
        )

    up_away_x, up_kept_x = up_product("x", 0)
    up_got_x = partner(up_away_x, "dp", 1)
    low_y_swap = partner(lax.optimization_barrier((low_y, up_away_x))[0], "mp", 1)
    up_away_y, up_kept_y = up_product("y", D)
    up_got_y = partner(up_away_y, "dp", 2)

    local, sent, along, grad_hidden, hidden_low, tables_second = simple(
        attend_back_kernel, order,
        (*second, hidden, rows, low, out_weight, projected, prompt_pair, log_total, prompt_src, prompt_len),
        [shaped((3, KEYS, HW), BF), shaped((2, 2, PMAX, HW), BF), shaped((2, PMAX, HW), BF), shaped((TOK, D), F32), shaped((TOK, D), BF), shaped((2, D), F32)],
        scratch=[pltpu.VMEM((KEYS, HW), BF), pltpu.VMEM((KEYS, HW), BF), pltpu.VMEM((HW, KEYS), BF), pltpu.VMEM((TOK, HW), BF), pltpu.VMEM((HW, TOK), F32),
            pltpu.VMEM((HW, D), BF), pltpu.SemaphoreType.DMA((1,))],
        far=(5,), name="attend_back",
    )
    first_back = partner(sent, "dp", 1)
    (act_onward,) = simple(join_kernel, order, (act_x, act_side), [shaped(act_x.shape, BF)], name="join")
    act_y = partner(act_onward, "dp", 2)

    if split:
        down_in, down_spec = down_weight.reshape(outer, 4, hidden_rows, D), block((outer, None, hidden_rows, D), lambda t, m: (0, t, 0, 0))
    else:
        down_in, down_spec = down_weight, block((HF // 4, D), lambda t, m: (t, 0))
    ffn_part = call(
        functools.partial(down_kernel, split), order, (*act, down_in), [whole(item.shape) for item in act] + [down_spec],
        halves, half_specs, grid=(4,), scratch=[pltpu.VMEM((TOK, D), F32)], name="down",
    )
    ffn_both = both(ffn_part)


    def outer_step(own, away, bit):
        return own, partner(away, "dp", 4 << bit)

    def through(state, name):
        own, got = state
        bit = 0
        while own.shape[0] > 1:
            bit += 1
            left = own.shape[0] // 2
            shape = (left,) + own.shape[1:]
            own, away = simple(
                functools.partial(halve_kernel, bit), order, (own, got), [shaped(shape, F32), shaped(shape, BF)],
                scratch=[pltpu.VMEM((left, 2) + own.shape[1:], F32)], name=name + "_halve",
            )
            own, got = outer_step(own, away, bit)
        return own, got

    def run_out(state):
        return list(state)

    def second_stage(kept_x, got_x, kept_y, got_y, name):
        _, _, rows, wide = kept_x.shape
        tall = kept_y.shape[-1]
        outs = [shaped((outer, rows, wide), BF)] * 2 + [shaped((outer, rows, tall), BF)] * 2
        away_x, own_x, away_y, own_y = simple(
            second_kernel, order, (kept_x, got_x, kept_y, got_y), outs,
            scratch=[pltpu.VMEM(kept_x.shape, F32), pltpu.VMEM(kept_y.shape, F32)], name=name + "_second",
        )
        return own_x, partner(away_x, "dp", 2), own_y, partner(away_y, "dp", 1)

    def third_stage(own_x, got_x, own_y, got_y, name, direct=False):
        rows = own_x.shape[1]
        columns = own_x.shape[2] + own_y.shape[2]
        if direct and outer == 4:
            shape = (1, rows, columns)
            own, *away = simple(
                direct_kernel, order, (own_x, got_x, own_y, got_y), [shaped(shape, F32)] + [shaped(shape, BF)] * (outer - 1),
                scratch=[pltpu.VMEM((outer, rows, columns), F32)], name=name + "_direct",
            )
            return [own] + [partner(item, "dp", 4 * (m + 1)) for m, item in enumerate(away)]
        shape = (half_outer, rows, columns)
        own, away = simple(
            third_kernel, order, (own_x, got_x, own_y, got_y), [shaped(shape, F32), shaped(shape, BF)],
            scratch=[pltpu.VMEM((half_outer, 2, rows, columns), F32)], name=name + "_third",
        )
        return outer_step(own, away, 0)

    up_later = second_stage(up_kept_x, up_got_x, up_kept_y, up_got_y, "up")
    half_outer = max(outer // 2, 1)
    lows = (act_own, act_x, act_y, low, low_x, low_y, low_x_swap, low_y_swap)
    piece_shape = (half_outer, hidden_rows, D)
    down_own, down_away = simple(
        down_product_kernel, order, lows, [shaped(piece_shape, F32), shaped(piece_shape, BF)],
        scratch=[pltpu.VMEM((half_outer, 2, hidden_rows, D), F32)], name="down_product",
    )

    down_later = outer_step(down_own, down_away, 0)
    (onward,) = simple(pass_on_kernel, order, (along, first_back), [shaped(along.shape, BF)], name="pass_on")
    second_back = partner(onward, "dp", 2)


    qkv_rows = 3 * D // count
    qkv_half = [shaped((outer, 2, qkv_rows + 8, HW // 2), BF), shaped((outer, 2, qkv_rows, HW // 2), BF)]

    def qkv_product(axis, at):
        return simple(
            functools.partial(qkv_product_kernel, axis, at), order, (normed, normed_prompt, local), qkv_half,
            scratch=[pltpu.VMEM((D, KEYS), BF), pltpu.VMEM((3 * D, HW // 2), BF)], name="qkv_product_" + axis,
        )

    qkv_away_x, qkv_kept_x = qkv_product("x", 0)
    qkv_got_x = partner(qkv_away_x, "dp", 1)
    qkv_away_y, qkv_kept_y = qkv_product("y", HW // 2)
    qkv_got_y = partner(qkv_away_y, "dp", 2)
    down_later = through(down_later, "down")
    up_later = third_stage(*up_later, "up")
    normed_part = call(
        grad_normed_kernel, order, (local, first_back, second_back, qkv_weight),
        [block((1, KEYS, HW), lambda c, m: (c, 0, 0)), whole(first_back.shape), whole(second_back.shape), block((1, D, HW), lambda c, m: (c, 0, 0))],
        halves, half_specs,
        grid=(3,), scratch=[pltpu.VMEM((PMAX, HW), BF), pltpu.VMEM((TOK, D), F32)], name="grad_normed",
    )
    normed_both = both(normed_part)
    qkv_later = second_stage(qkv_kept_x, qkv_got_x, qkv_kept_y, qkv_got_y, "qkv")
    input_grad, tables_first = simple(
        input_grad_kernel, order, (*normed_both, tokens, rows, grad_hidden),
        [shaped((TOK, D), BF), shaped((2, D), F32)], name="input_grad",
    )


    up_later = through(up_later, "up")
    (block_out,) = simple(block_out_kernel, order, (hidden, *ffn_both), [shaped((TOK, D), BF)], name="block_out")
    out_rows = HW // count
    entries = 2 * SECTIONS * HW // count
    spread = []
    if entries != HW:
        selector = (jnp.arange(SECTIONS) == meta[SECTION]).astype(F32)
        tables = jnp.stack([tables_first, tables_second])
        tables = lax.dynamic_slice_in_dim(tables, mp_index * HW, HW, 2)
        whole_tables = selector[None, None, :, None] * jnp.transpose(tables, (1, 0, 2))[:, :, None, :]
        whole_tables = jnp.transpose(whole_tables.reshape(2, count, entries), (1, 0, 2)).reshape(count, 2 * entries // 128, 128)
        spread = [jnp.pad(whole_tables.astype(BF), ((0, 0), (0, out_rows - 2 * entries // 128), (0, 0)))]
    wide, tall = HW + 128, HW
    away_x, kept_x, away_y, kept_y = simple(
        out_product_kernel, order, (attended_t, hidden_low, tables_first, tables_second, *spread),
        [shaped((outer, 2, out_rows, wide), BF)] * 2 + [shaped((outer, 2, out_rows, tall), BF)] * 2,
        scratch=[pltpu.VMEM((outer, 2, 2, out_rows, wide), BF), pltpu.VMEM((outer, 2, 2, out_rows, tall), BF)],
        name="out_product",
    )
    got_x, got_y = partner(away_x, "dp", 1), partner(away_y, "dp", 2)

    qkv_later = third_stage(*qkv_later, "qkv", direct=True)
    out_later = second_stage(kept_x, got_x, kept_y, got_y, "out")
    down_rows, down_squares = simple(
        finish_kernel, order, run_out(down_later), [shaped((hidden_rows * D // 128, 128), F32), shaped((8, 128), F32)], name="finish_down"
    )
    up_terms = run_out(up_later)
    up_lines, up_squares = simple(finish_kernel, order, up_terms, [shaped((up_rows * HF // 128, 128), F32), shaped((8, 128), F32)], name="finish_up")
    out_later = third_stage(*out_later, "out", direct=True)
    if len(out_later) == 2:
        out_later = run_out(through(out_later, "out"))
    qkv_terms = run_out(through(qkv_later, "qkv")) if len(qkv_later) == 2 else qkv_later

    flat = master.shape[1]
    (qkv_lines, out_lines, table_lines, squares) = simple(
        functools.partial(finish_last_kernel, len(qkv_terms)), order, (*qkv_terms, *out_later, up_squares, down_squares),
        [shaped((qkv_rows * HW // 128, 128), F32), shaped((out_rows * D // 128, 128), F32), shaped((max(2 * entries // 128, 1), 128), F32), shaped((8, 128), F32)],
        name="finish",
    )
    squares = squares + partner(squares, "mp", 1)
    squares = squares + partner(squares, "dp", 1) + partner(squares, "dp", 2) + partner(squares, "dp", 3)
    step = 4
    while step < count:
        flips = (step, 2 * step, 3 * step) if step * 4 <= count else (step,)
        squares = sum([partner(squares, "dp", flip) for flip in flips], squares)
        step *= 4 if step * 4 <= count else 2
    step_count = adam_step[0].astype(F32)
    fixes = jnp.stack([1.0 / (1.0 - jnp.power(BETA_ONE, step_count)), 1.0 / (1.0 - jnp.power(BETA_TWO, step_count))]).reshape(1, 2)
    lines = flat // 128
    rates = [D ** (-0.5), OUT_FAN ** (-0.5), D ** (-0.5), FF ** (-0.5), 0.2]
    flats = [item.reshape(lines, 128) for item in (master, first_moment, second_moment, ema_weight)]
    new_first, new_second, new_master, copy, new_ema, grad_norm = simple(
        functools.partial(adam_kernel, rates), order, (squares, fixes, qkv_lines, out_lines, up_lines, down_rows, table_lines, *flats),
        [shaped((lines, 128), F32)] * 3 + [shaped((1, flat), BF), shaped((lines, 128), F32), shaped((1, 1), F32)], name="adam", vmem=40,
    )
    return (
        block_out,
        input_grad,
        grad_norm.reshape(1),
        new_first.reshape(1, flat),
        new_second.reshape(1, flat),
        new_master.reshape(1, flat),
        copy,
        new_ema.reshape(1, flat),
    )


def solution(mesh):
    placed = (
        P("dp", None), P("dp", None), P(None, None, "mp"), P("mp", None), P(None, "mp"), P("mp", None), P(), P(),
        P("dp"), P("dp"), P("dp"), P("dp"), P(),
        P("mp", "dp"), P("mp", "dp"), P("mp", "dp"), P("mp", "dp"),
    )
    flat = P("mp", "dp")
    return jax.shard_map(
        body, mesh=mesh, in_specs=placed,
        out_specs=(P("dp", None), P("dp", None), P(), flat, flat, flat, flat, flat),
        check_vma=False,
    )
```
